512 devices in a mesh: member: 8 (over z_lo, core), space: 64 (over x, z_hi, y).
Axes of the slice: x: 4, y: 4, z: 16 (z_hi: 4, z_lo: 4; z = z_hi * 4 + z_lo), core: 2. Of those that a mesh axis runs over, the one named last changes fastest.
Arguments:
- hidden: bfloat16 [8, 49152, 1024], P('member', 'space'), may hold values from -16 to 16
- truth: float32 [100, 49152], P(None, 'space'), may hold values from -6 to 6
- lat_row: int32 [49152], P('space'), may hold values from 0 to 720
- gain: float32 [1024], replicated, may hold values from 0.25 to 1.75
- w_in: bfloat16 [1024, 1024], P('space'), may hold values from -0.1875 to 0.1875
- w_out: bfloat16 [100, 1024], replicated, may hold values from -0.1875 to 0.1875
Outputs:
- grad_hidden: bfloat16 [8, 49152, 1024], P('member', 'space')
- grad_w1: float32 [1024, 1024], P('space')
The draws below stay inside these ranges and needn't reach their ends.
Inputs may be any that keep to these rules, and one draw needn't show every extreme that they name: `lat_row`: global latitude row of each grid point.
All inputs are finite; a program needn't handle non-finite values.
Results may differ from the reference program's by a relative error of at most 0.012.
Values may be sent and summed in bfloat16 or wider, within the bound.
A program may use at most 64 MiB of HBM per device.

```python
import math
import jax
import jax.numpy as jnp
from jax import lax

W = 1024
V = 100
LATS = 721
MEMBERS = 8
POINTS = 49152


def plant(values, own_key, low, high):
    longest = values.shape.index(max(values.shape))
    spots = []
    for shift in (0, 1):
        where = [jax.random.randint(jax.random.fold_in(own_key, axis), (), 0, length) for axis, length in enumerate(values.shape)]
        where[longest] = (where[longest] + shift) % values.shape[longest]
        spots.append(tuple(where))
    return values.at[spots[0]].set(low).at[spots[1]].set(high)


def spiked(array, own_key, source, target, blocks, factor):
    def block_of(position):
        return (jnp.arange(array.shape[position]) // (array.shape[position] // blocks)).reshape((-1,) + (1,) * (array.ndim - 1 - position))

    one_side = jax.random.permutation(own_key, blocks)[block_of(target)]
    second = (block_of(target) + blocks // 2) % blocks
    return jnp.where((block_of(source) == one_side) | (block_of(source) == second), factor * array, array)


def shard_levels(key, dims, split, smallest, high):
    level = 1.0
    for position, shards_of in split:
        draws = jax.random.uniform(jax.random.fold_in(jax.random.fold_in(key, 6), position), (shards_of,), jnp.float32, smallest / len(split), high / len(split))
        level = level * jnp.repeat(jnp.exp(draws), dims[position] // shards_of).reshape((-1,) + (1,) * (len(dims) - 1 - position))
    return level


def gaussian(stream_key, dims, deviation, reach, shards=(), held_as=jnp.bfloat16):
    level = shard_levels(stream_key, dims, shards, -0.22, 0.18) if shards else 1.0
    values = jax.random.normal(stream_key, dims, jnp.float32) * deviation * level
    return jnp.minimum(jnp.maximum(values, -reach), reach).astype(held_as)


def heavy_noise(stream_key, extent, deviation, reach, pieces, heavy, held_as=jnp.bfloat16):
    result = deviation * jax.random.normal(stream_key, extent, jnp.float32)
    if pieces:
        result = result * shard_levels(stream_key, extent, pieces, -0.22, 0.18)
    return jnp.clip(spiked(result, jax.random.fold_in(stream_key, 3), *heavy), -reach, reach).astype(held_as)


def setup_inputs(seed: int = 0) -> dict:
    arg_keys = jax.random.split(jax.random.key(seed), 7)
    hidden = heavy_noise(arg_keys[0], (MEMBERS, POINTS, W), 1.0, 16.0, ((0, 8), (1, 64)), (1, 2, 64, 4.0))
    truth = gaussian(arg_keys[1], (V, POINTS), 1.0, 6.0, ((1, 64),), jnp.float32)
    lat_row = plant(jax.random.randint(arg_keys[2], (POINTS,), 0, LATS), jax.random.fold_in(arg_keys[2], 1), 0, LATS - 1).astype(jnp.int32)
    gain = jnp.clip(1.0 + 0.15 * jax.random.normal(arg_keys[3], (W,), jnp.float32), 0.25, 1.75)
    w_in = gaussian(arg_keys[4], (W, W), W ** -0.5, 0.1875, ((0, 64),))
    w_out = gaussian(arg_keys[5], (V, W), W ** -0.5, 0.1875)
    return dict(hidden=hidden, truth=truth, lat_row=lat_row, gain=gain, w_in=w_in, w_out=w_out)


ALPHA = 0.95
SMOOTH = 0.1
LOSS_SCALE = 64.0
EPSILON = 1e-05

def slope(diff):
    return diff / jnp.sqrt(diff * diff + SMOOTH * SMOOTH)

def forward(member_rows, gain, w_in, w_out):
    rows = member_rows.astype(jnp.float32)
    root_mean = jnp.sqrt(lax.optimization_barrier(jnp.mean(rows * rows, axis=-1, keepdims=True)) + EPSILON)
    unit_rows = rows / root_mean
    normed = (unit_rows * gain).astype(jnp.bfloat16)
    preact = jnp.dot(normed, w_in, preferred_element_type=jnp.float32)
    hidden_act = jax.nn.silu(preact).astype(jnp.bfloat16)
    fields = jnp.dot(w_out, hidden_act.T, preferred_element_type=jnp.float32)
    return (root_mean, unit_rows, normed, preact, hidden_act, fields)

def reference(hidden, truth, lat_row, gain, w_in, w_out):
    count = hidden.shape[0]
    total_points = hidden.shape[1]
    fields = [forward(hidden[member], gain, w_in, w_out)[5] for member in range(count)]
    coarse = [lax.optimization_barrier(field.astype(jnp.bfloat16)).astype(jnp.float32) for field in fields]
    latitude = math.pi * ((lat_row.astype(jnp.float32) + 0.5) / LATS - 0.5)
    area = jnp.cos(latitude)[None, :]
    fair = (1.0 - (1.0 - ALPHA) / count) / (count * (count - 1))
    grad_rows = []
    grad_first = jnp.zeros((w_in.shape[0], w_in.shape[1]), jnp.float32)
    for member in range(count):
        pairs = jnp.zeros(truth.shape, jnp.float32)
        for other in range(count):
            if other != member:
                pairs = pairs + slope(coarse[member] - coarse[other])
        grad_fields = (LOSS_SCALE * area * (slope(fields[member] - truth) / count - fair * pairs)).astype(jnp.bfloat16)
        root_mean, unit_rows, normed, preact, hidden_act, unused = forward(hidden[member], gain, w_in, w_out)
        grad_act = jnp.dot(grad_fields.T, w_out, preferred_element_type=jnp.float32)
        sigma = jax.nn.sigmoid(preact)
        grad_pre = (grad_act * sigma * (1.0 + preact * (1.0 - sigma))).astype(jnp.bfloat16)
        grad_normed = jnp.dot(grad_pre, w_in.T, preferred_element_type=jnp.float32)
        scaled = grad_normed * gain
        inner = lax.optimization_barrier(jnp.mean(scaled * unit_rows, axis=-1, keepdims=True))
        grad_rows.append(((scaled - unit_rows * inner) / root_mean).astype(jnp.bfloat16))
        grad_first = grad_first + jnp.dot(normed.T, grad_pre, preferred_element_type=jnp.float32)
    factor = 1.0 / math.sqrt(count * total_points)
    return (jnp.stack(grad_rows), grad_first * factor)
```

```python
import functools
import math

import jax
import jax.numpy as jnp
from jax import lax
from jax.experimental import pallas as pl
from jax.experimental.pallas import tpu as pltpu
from jax.sharding import PartitionSpec as P

LATS = 721
ALPHA = 0.95
SMOOTH = 0.1
LOSS_SCALE = 64.0
EPSILON = 1e-05

GRID = (4, 4, 4)
LANES = 128
TILE = 256
MESH = pl.DeviceIdType.MESH


def slope(diff):
    return diff * lax.rsqrt(diff * diff + SMOOTH * SMOOTH)


def rows_at(start, size):
    return pl.ds(pl.multiple_of(start, size), size)


def kernel(
    tile,
    hid_hbm, truth_hbm, lat_hbm, gain_hbm, w_hbm, wo_hbm,
    gh, gw_ref,
    hid, truth, lat, gain, wo_raw, w_full, normed, planes, inv_root, wo_pad, wo_t, hidden_act,
    truth_pad, truth_t, area_t, act, fields, coarse, theirs, answers, pairs, gp,
    csend, crecv, sums, send1, recv1, send2, recv2, send3, recv3, finals,
    local_sem, a1_s, a1_r, a2_s, a2_r, a3_s, a3_r, a4_s, a4_r,
    b1_s, b1_r, b2_s, b2_r, c0_s, c0_r, c1_s, c1_r, c2_s, c2_r, c3_s, c3_r, c4_s, c4_r,
):
    nx, nh, ny = GRID
    n = nx
    points, width = hid.shape
    half = width // 2
    quarter = half // 2
    levels = truth.shape[0]
    count = finals.shape[0]
    chips = count // 2
    block = w_full.shape[3]
    tiles, share = theirs.shape[0], theirs.shape[2]
    f32, bf16 = jnp.float32, jnp.bfloat16

    member, space = lax.axis_index("member"), lax.axis_index("space")
    core, low = member % 2, member // 2
    x, h, y = space // (nh * ny), (space // ny) % nh, space % ny
    q, p = x * (1 - core) + y * core, y * (1 - core) + x * core
    mine = pl.ds(pl.multiple_of(core * half, half), half)
    other = pl.ds(pl.multiple_of((1 - core) * half, half), half)
    quarters = [
        pl.ds(pl.multiple_of(core * half + i * quarter, quarter), quarter) for i in range(2)
    ]

    def place(p_, q_):
        return q_ * (1 - core) + p_ * core, p_ * (1 - core) + q_ * core

    def at(p_, q_, h_):
        x_, y_ = place(p_, q_)
        return (member, (x_ * nh + h_) * ny + y_)

    def h_peer(k):
        return at(p, q, (h + k) % nh)

    def q_peer(k):
        return at(p, (q + k) % n, h)

    def m_peer(k):
        return ((member + k) % count, space)

    def z_peer(i):
        dh, dl = i // chips, i % chips
        return (2 * ((low + dl) % chips) + core, (x * nh + (h + dh) % nh) * ny + y)

    sides = [p + 1 - 2 * (p % 2), n - 1 - p]
    far = (p + 2) % n
    p_peers = [at(v, q, h) for v in sides]
    partner = (member + 1 - 2 * core, space)

    def send(src, dst, send_sem, recv_sem, target):
        pltpu.make_async_remote_copy(
            src_ref=src, dst_ref=dst, send_sem=send_sem, recv_sem=recv_sem,
            device_id=target, device_id_type=MESH,
        ).start()

    def drain(ref, sem):
        pltpu.make_async_copy(ref, ref, sem).wait()

    def loop(first, last, body):
        def step(i, carry):
            body(i)
            return carry

        lax.fori_loop(first, last, step, 0)

    barrier = pltpu.get_barrier_semaphore()

    def greet(peer):
        pl.semaphore_signal(barrier, inc=1, device_id=peer, device_id_type=MESH)

    loop(chips, nh * chips, lambda i: greet(z_peer(i)))
    loop(1, n, lambda k: greet(q_peer(k)))
    for peer in p_peers:
        greet(peer)
    loop(1, count, lambda k: greet(m_peer(k)))

    own_w = pltpu.make_async_copy(w_hbm.at[:, mine], w_full.at[x, h, y, :, mine], local_sem.at[0])
    loads = [
        pltpu.make_async_copy(source, target, local_sem.at[1 + i])
        for i, (source, target) in enumerate(
            [(hid_hbm, hid), (gain_hbm, gain), (truth_hbm, truth), (lat_hbm, lat), (wo_hbm, wo_raw)]
        )
    ]
    own_w.start()
    for load in loads:
        load.start()
    pl.semaphore_wait(barrier, nh * chips - chips + n - 1 + 2 + count - 1)

    own_block = w_full.at[x, h, y, :, mine]
    loop(1, nh, lambda k: send(w_hbm.at[:, mine], own_block, a1_s.at[0], a1_r.at[0], h_peer(k)))
    loads[0].wait()
    loads[1].wait()

    def normalise(i):
        rows = rows_at(i * 32, 32)
        values = hid[rows, :].astype(f32)
        root = jnp.sqrt(jnp.mean(values * values, axis=-1, keepdims=True) + EPSILON)
        inverse = 1.0 / root
        inv_root[rows, :] = jnp.broadcast_to(inverse, (32, LANES))
        normed[rows, :] = (values * inverse * gain[...]).astype(bf16)

    steps = points // 32
    loop(0, steps, normalise)
    own_w.wait()
    z_blocks = w_full.at[0, 0, pl.ds(0, nh - 1), :, mine]
    drain(z_blocks, a1_r.at[0])

    def group(p_, b, cols=mine):
        x_, y_ = place(p_, (q - b + n) % n)
        return w_full.at[x_, :, y_, :, cols]

    def to_partner(p_, b):
        part = group(p_, b)
        send(part, part, a4_s.at[0], a4_r.at[0], partner)

    def to_second(b):
        part = group(p, b)
        for i in range(2):
            send(part, part, a3_s.at[0], a3_r.at[b, i], p_peers[i])
        to_partner(p, b)

    def ordered(j):
        return j + (j // 2) * (n + 1 - 2 * j)

    own_group = group(p, 0)
    loop(1, n, lambda j: send(
        own_group, own_group, a2_s.at[0], a2_r.at[ordered(j) - 1], q_peer(ordered(j))
    ))
    to_second(0)
    for load in loads[2:]:
        load.wait()
    truth_pad[...] = jnp.zeros_like(truth_pad)
    truth_pad[0:levels, :] = truth[...]
    wo_pad[...] = jnp.zeros_like(wo_pad)
    wo_pad[0:levels, :] = wo_raw[...]

    def pass_first(j):
        b = ordered(j)
        drain(own_group, a2_r.at[b - 1])
        to_second(b)

    loop(1, n, pass_first)

    def pass_second(j):
        b = ordered(j)
        for i in range(2):
            drain(own_group, a3_r.at[b, i])
            part = group(sides[i], b, quarters[i])
            send(part, part, a3_s.at[0], a3_r.at[b, 2 + i], p_peers[1 - i])
        for i in range(2):
            to_partner(sides[i], b)

    loop(0, n, pass_second)

    def pass_far(j):
        b = ordered(j)
        for i in range(2):
            drain(group(far, b, quarters[i]), a3_r.at[b, 2 + i])
        to_partner(far, b)

    loop(0, n, pass_far)

    def project(rows, cols):
        act[rows, cols] = jnp.dot(
            normed[rows, :], w_full[:, :, :, :, cols].reshape(width, half),
            preferred_element_type=f32,
        )

    def activate(i, cols):
        rows = rows_at(i * 32, 32)
        a = act[rows, cols]
        hidden_act[rows, cols] = (a * (0.5 * jnp.tanh(0.5 * a) + 0.5)).astype(bf16)

    loop(0, tiles, lambda t: project(rows_at(t * tile, tile), mine))
    loop(0, steps, lambda i: activate(i, mine))

    truth_t[...] = truth_pad[...].T
    latitude = math.pi * ((lat[...].astype(f32) + 0.5) / LATS - 0.5)
    area = LOSS_SCALE * jnp.cos(latitude)
    strip = lat.shape[1]
    for i in range(lat.shape[0]):
        area_t[i * strip:(i + 1) * strip, :] = jnp.broadcast_to(area[i:i + 1, :], (LANES, strip)).T
    wo_t[...] = wo_pad[...].T
    drain(w_full.at[:, :, :, :, other], a4_r.at[0])

    def share_of(t, m):
        return rows_at(t * tile + m * share, share)

    tile_steps = tile // 32

    def forward(t):
        rows = rows_at(t * tile, tile)
        project(rows, other)
        loop(t * tile_steps, (t + 1) * tile_steps, lambda i: activate(i, other))
        field = jnp.dot(hidden_act[rows, :], wo_t[...], preferred_element_type=f32)
        fields[rows, :] = field
        coarse[rows, :] = field.astype(bf16)

        def spread(k):
            peer = m_peer(k)
            send(
                coarse.at[share_of(t, peer[0]), :], theirs.at[t, member],
                b1_s.at[0], b1_r.at[t], peer,
            )

        loop(1, count, spread)
        theirs[t, member] = coarse[share_of(t, member), :]

    loop(0, tiles, forward)

    def differentiate(i):
        rows = rows_at(i * 32, 32)
        a = act[rows, :]
        s = 0.5 * jnp.tanh(0.5 * a) + 0.5
        act[rows, :] = s * (1.0 + a * (1.0 - s))

    span = min(LANES, points)
    turns = points // span

    def turn(i):
        cols = rows_at(i * span, span)
        turned = normed[cols, :].T
        for x_ in range(nx):
            for h_ in range(nh):
                for y_ in range(ny):
                    first = ((x_ * nh + h_) * ny + y_) * block
                    piece = turned[first:first + block, :]
                    to_x, to_y = (x_ * nh + h_) * block, (y_ * nh + h_) * block
                    planes[0, y_, to_x:to_x + block, cols] = piece
                    planes[1, x_, to_y:to_y + block, cols] = piece

    def answer(t):
        come = theirs.at[t, pl.ds(0, count - 1)]
        drain(come, b1_r.at[t])

        def compare(i):
            rows = rows_at(i * 16, 16)
            values = [theirs[t, m, rows, :].astype(f32) for m in range(count)]
            totals = [jnp.zeros_like(values[0]) for m in range(count)]
            for m in range(count):
                for o in range(m + 1, count):
                    s = slope(values[m] - values[o])
                    totals[m] = totals[m] + s
                    totals[o] = totals[o] - s
            for m in range(count):
                answers[t, m, rows, :] = totals[m].astype(bf16)

        loop(0, share // 16, compare)

        def reply(k):
            peer = m_peer(k)
            send(
                answers.at[t, peer[0]], pairs.at[share_of(t, member), :],
                b2_s.at[0], b2_r.at[t], peer,
            )

        loop(1, count, reply)
        pairs[share_of(t, member), :] = answers[t, member]
        loop(t * tile_steps, (t + 1) * tile_steps, differentiate)
        loop(t * turns // tiles, (t + 1) * turns // tiles, turn)

    loop(0, tiles, answer)

    fair = (1.0 - (1.0 - ALPHA) / count) / (count * (count - 1))

    def backward(t):
        come = pairs.at[pl.ds(0, tile - share), :]
        drain(come, b2_r.at[t])
        rows = rows_at(t * tile, tile)
        grad_fields = area_t[rows, :] * (
            slope(fields[rows, :] - truth_t[rows, :]) * (1.0 / count)
            - fair * pairs[rows, :].astype(f32)
        )
        grad_act = jnp.dot(grad_fields.astype(bf16), wo_pad[...], preferred_element_type=f32)
        gp[rows, :] = (grad_act * act[rows, :]).astype(bf16)

    loop(0, tiles, backward)

    depth = width // n

    def nth(i, own):
        first = jnp.where(i == 0, (own + 2) % n, own + 1 - 2 * (own % 2))
        return jnp.where(i < 2, first, jnp.where(i == 2, n - 1 - own, own))

    def other_plane(i):
        part = jnp.dot(planes[1 - core, nth(i, q)], gp[:, other], preferred_element_type=f32)
        csend[i] = part.astype(bf16)
        send(csend.at[i], crecv.at[i], c0_s.at[0], c0_r.at[i], partner)

    loop(0, n, other_plane)

    halves = [slice(0, quarter), slice(quarter, half)]

    def to_side(slot, target):
        send(send1.at[slot], recv1.at[slot], c1_s.at[0], c1_r.at[slot], p_peers[target])

    def own_plane(i):
        part = jnp.dot(planes[core, nth(i, p)], gp[:, mine], preferred_element_type=f32)
        drain(crecv.at[i], c0_r.at[i])
        total = part + crecv[i].astype(f32)
        sums[i] = total

        @pl.when(i == 0)
        def _():
            for side in range(2):
                send1[side] = total[:, halves[side]].astype(bf16)
                to_side(side, side)

        for side in range(2):
            @pl.when(i == 1 + side)
            def _():
                send1[2 + side] = total[:, halves[side]].astype(bf16)
                to_side(2 + side, side)

    loop(0, n, own_plane)
    for side in range(2):
        drain(recv1.at[side], c1_r.at[side])
        term = sums[2 - side, :, halves[side]] + recv1[side].astype(f32)
        send1[4 + side] = term.astype(bf16)
        to_side(4 + side, 1 - side)

    def grad_normed(x_):
        cols = rows_at(x_ * depth, depth)
        act[:, cols] = lax.dot_general(
            gp[...], w_full[x_].reshape(depth, width), (((1,), (1,)), ((), ())),
            preferred_element_type=f32,
        )

    def hidden_grad(i):
        rows = rows_at(i * 32, 32)
        scaled = act[rows, :] * gain[...]
        inverse = inv_root[rows, 0:1]
        unit = hid[rows, :].astype(f32) * inverse
        inner = jnp.mean(scaled * unit, axis=-1, keepdims=True)
        gh[rows, :] = ((scaled - unit * inner) * inverse).astype(bf16)

    loop(0, n // 2, grad_normed)
    for slot in range(2, 6):
        drain(recv1.at[slot], c1_r.at[slot])
    line_rows = nh * block

    def add_planes(q_):
        rows = rows_at(q_ * line_rows, line_rows)
        both = [
            sums[n - 1, rows, halves[i]] + recv1[2 + i, rows, :].astype(f32)
            + recv1[4 + i, rows, :].astype(f32)
            for i in range(2)
        ]
        return jnp.concatenate(both, axis=1)

    def to_first(j):
        k = ordered(n - j)
        send2[j - 1] = add_planes((q + k) % n).astype(bf16)
        send(send2.at[j - 1], recv2.at[j - 1], c2_s.at[0], c2_r.at[0], q_peer(k))

    loop(1, n, to_first)
    total = add_planes(q)
    loop(n // 2, n, grad_normed)
    drain(recv2, c2_r.at[0])
    for i in range(n - 1):
        total = total + recv2[i].astype(f32)
    strip = half // chips
    for h_ in range(nh):
        for l_ in range(chips):
            send3[h_, l_] = total[
                h_ * block:(h_ + 1) * block, l_ * strip:(l_ + 1) * strip
            ].astype(bf16)
    loop(1, nh * chips, lambda i: send(
        send3.at[(h + i // chips) % nh, (low + i % chips) % chips], recv3.at[i - 1],
        c3_s.at[0], c3_r.at[0], z_peer(i),
    ))
    loop(0, steps // 2, hidden_grad)
    drain(recv3, c3_r.at[0])
    total = send3[h, low].astype(f32)
    for i in range(nh * chips - 1):
        total = total + recv3[i].astype(f32)
    factor = 1.0 / math.sqrt(count * points * nx * nh * ny)
    finals[core * chips + low] = total * factor
    own_final = finals.at[core * chips + low]
    loop(1, count, lambda k: send(own_final, own_final, c4_s.at[0], c4_r.at[0], m_peer(k)))
    loop(steps // 2, steps, hidden_grad)
    others = finals.at[pl.ds(0, count - 1)]
    drain(others, c4_r.at[0])
    for i in range(count):
        gw_ref[:, i * strip:(i + 1) * strip] = finals[i]

    drain(z_blocks, a1_s.at[0])
    drain(w_full.at[pl.ds(0, n - 1), :, 0, :, mine], a2_s.at[0])
    drain(w_full.at[:, :, pl.ds(0, 3), :, mine], a3_s.at[0])
    drain(w_full.at[:, :, :, :, mine], a4_s.at[0])
    drain(coarse.at[pl.ds(0, points - points // count), :], b1_s.at[0])
    drain(coarse.at[pl.ds(0, points - points // count), :], b2_s.at[0])
    drain(csend, c0_s.at[0])
    drain(send1, c1_s.at[0])
    drain(send2, c2_s.at[0])
    drain(recv3, c3_s.at[0])
    drain(others, c4_s.at[0])


def hand_over(*arrays):
    pieces = 4

    def body(*refs):
        sources, targets, sems = refs[:len(arrays)], refs[len(arrays):-1], refs[-1]
        copies = []
        for source, target in zip(sources, targets):
            rows = source.shape[0]
            parts = pieces if rows % (16 * pieces) == 0 else 1
            for i in range(parts):
                part = pl.ds(i * (rows // parts), rows // parts)
                copies.append(
                    pltpu.make_async_copy(source.at[part], target.at[part], sems.at[len(copies)])
                )
        for copy in copies:
            copy.start()
        for copy in copies:
            copy.wait()

    anywhere = pl.BlockSpec(memory_space=pl.ANY)
    return pl.pallas_call(
        body,
        out_shape=tuple(jax.ShapeDtypeStruct(a.shape, a.dtype) for a in arrays),
        in_specs=[anywhere] * len(arrays),
        out_specs=(anywhere,) * len(arrays),
        scratch_shapes=[pltpu.SemaphoreType.DMA((pieces * len(arrays),))],
        compiler_params=pltpu.CompilerParams(vmem_limit_bytes=1024 * 1024),
        name="hand_over",
    )(*arrays)


def per_device(hidden, truth, lat_row, gain, w_in, w_out):
    nx, nh, ny = GRID
    count = lax.axis_size("member")
    _, points, width = hidden.shape
    levels = truth.shape[0]
    block = w_in.shape[0]
    half = width // 2
    tile = min(TILE, points)
    tiles, share = points // tile, tile // count
    f32, bf16 = jnp.float32, jnp.bfloat16
    vmem, dma = pltpu.VMEM, pltpu.SemaphoreType.DMA
    n, chips, lat_strip = nx, count // 2, min(LANES, points)
    scratch = [
        vmem((points, width), bf16),
        vmem((levels, points), f32),
        vmem((points // lat_strip, lat_strip), jnp.int32),
        vmem((1, width), f32),
        vmem((levels, width), bf16),
        vmem((nx, nh, ny, block, width), bf16),
        vmem((points, width), bf16),
        vmem((2, n, width // n, points), bf16),
        vmem((points, LANES), f32),
        vmem((LANES, width), bf16),
        vmem((width, LANES), bf16),
        vmem((points, width), bf16),
        vmem((LANES, points), f32),
        vmem((points, LANES), f32),
        vmem((points, LANES), f32),
        vmem((points, width), f32),
        vmem((points, LANES), f32),
        vmem((points, LANES), bf16),
        vmem((tiles, count, share, LANES), bf16),
        vmem((tiles, count, share, LANES), bf16),
        vmem((points, LANES), bf16),
        vmem((points, width), bf16),
        vmem((n, width // n, half), bf16),
        vmem((n, width // n, half), bf16),
        vmem((n, width // n, half), f32),
        vmem((6, width // n, half // 2), bf16),
        vmem((6, width // n, half // 2), bf16),
        vmem((n - 1, nh * block, half), bf16),
        vmem((n - 1, nh * block, half), bf16),
        vmem((nh, chips, block, half // chips), bf16),
        vmem((nh * chips - 1, block, half // chips), bf16),
        vmem((count, block, half // chips), f32),
        dma((6,)),
    ]
    for arrivals in (
        (1,), (n - 1,), (n, 4), (1,),
        (tiles,), (tiles,),
        (n,), (6,), (1,), (1,), (1,),
    ):
        scratch += [dma((1,)), dma(arrivals)]
    grad_rows, grad_first = pl.pallas_call(
        functools.partial(kernel, tile),
        out_shape=(
            vmem((points, width), bf16),
            vmem((block, width), f32),
        ),
        in_specs=[pl.BlockSpec(memory_space=pltpu.HBM)] * 6,
        out_specs=(pl.BlockSpec(memory_space=vmem),) * 2,
        scratch_shapes=scratch,
        compiler_params=pltpu.CompilerParams(
            collective_id=0, has_side_effects=True, vmem_limit_bytes=57 * 1024 * 1024
        ),
        name="crps_step",
    )(
        hidden[0], truth, lat_row.reshape(points // lat_strip, lat_strip), gain[None], w_in, w_out
    )
    grad_rows, grad_first = hand_over(grad_rows, grad_first)
    return (grad_rows[None], grad_first)


def solution(mesh):
    in_specs = (
        P("member", "space", None),
        P(None, "space"),
        P("space"),
        P(),
        P("space", None),
        P(),
    )
    out_specs = (P("member", "space", None), P("space", None))
    return jax.shard_map(
        per_device, mesh=mesh, in_specs=in_specs, out_specs=out_specs, check_vma=False
    )
```

```python
import functools
import math

import jax
import jax.numpy as jnp
from jax import lax
from jax.experimental import pallas as pl
from jax.experimental.pallas import tpu as pltpu
from jax.sharding import PartitionSpec as P

LATS = 721
ALPHA = 0.95
SMOOTH = 0.1
LOSS_SCALE = 64.0
EPSILON = 1e-05

GRID = (4, 4, 4)
LANES = 128
TILE = 256
MESH = pl.DeviceIdType.MESH


def slope(diff):
    return diff * lax.rsqrt(diff * diff + SMOOTH * SMOOTH)


def rows_at(start, size):
    return pl.ds(pl.multiple_of(start, size), size)


def kernel(
    tile,
    hid_hbm, truth_hbm, lat_hbm, gain_hbm, w_hbm, wo_hbm,
    gh, gw_ref,
    hid, truth, lat, gain, wo_raw, w_full, normed, planes, inv_root, wo_pad, wo_t, hidden_act,
    truth_pad, truth_t, area_t, act, fields, coarse, theirs, answers, pairs, gp, parts,
    csend, crecv, sums, send1, recv1, send2, recv2, send3, recv3, finals,
    local_sem, a1_s, a1_r, a2_s, a2_r, a3_s, a3_r, a4_s, a4_r,
    b1_s, b1_r, b2_s, b2_r, c0_s, c0_r, c1_s, c1_r, c2_s, c2_r, c3_s, c3_r, c4_s, c4_r,
):
    nx, nh, ny = GRID
    n = nx
    points, width = hid.shape
    half = width // 2
    quarter = half // 2
    levels = truth.shape[0]
    count = finals.shape[0]
    chips = count // 2
    block = w_full.shape[3]
    tiles, share = theirs.shape[0], theirs.shape[2]
    f32, bf16 = jnp.float32, jnp.bfloat16

    member, space = lax.axis_index("member"), lax.axis_index("space")
    core, low = member % 2, member // 2
    x, h, y = space // (nh * ny), (space // ny) % nh, space % ny
    q, p = x * (1 - core) + y * core, y * (1 - core) + x * core
    mine = pl.ds(pl.multiple_of(core * half, half), half)
    other = pl.ds(pl.multiple_of((1 - core) * half, half), half)
    quarters = [
        pl.ds(pl.multiple_of(core * half + i * quarter, quarter), quarter) for i in range(2)
    ]

    def place(p_, q_):
        return q_ * (1 - core) + p_ * core, p_ * (1 - core) + q_ * core

    def at(p_, q_, h_):
        x_, y_ = place(p_, q_)
        return (member, (x_ * nh + h_) * ny + y_)

    def h_peer(k):
        return at(p, q, (h + k) % nh)

    def q_peer(k):
        return at(p, (q + k) % n, h)

    def m_peer(k):
        return ((member + k) % count, space)

    def z_peer(i):
        dh, dl = i // chips, i % chips
        return (2 * ((low + dl) % chips) + core, (x * nh + (h + dh) % nh) * ny + y)

    sides = [p + 1 - 2 * (p % 2), n - 1 - p]
    far = (p + 2) % n
    p_peers = [at(v, q, h) for v in sides]
    partner = (member + 1 - 2 * core, space)

    def send(src, dst, send_sem, recv_sem, target):
        pltpu.make_async_remote_copy(
            src_ref=src, dst_ref=dst, send_sem=send_sem, recv_sem=recv_sem,
            device_id=target, device_id_type=MESH,
        ).start()

    def drain(ref, sem):
        pltpu.make_async_copy(ref, ref, sem).wait()

    def loop(first, last, body):
        def step(i, carry):
            body(i)
            return carry

        lax.fori_loop(first, last, step, 0)

    def by_rows(first, last, body):
        chunks = math.gcd(4, (last - first) // 16)

        def step(i):
            for u in range(chunks):
                body(rows_at(first + (i * chunks + u) * 16, 16))

        loop(0, (last - first) // (16 * chunks), step)

    barrier = pltpu.get_barrier_semaphore()

    def greet(peer):
        pl.semaphore_signal(barrier, inc=1, device_id=peer, device_id_type=MESH)

    loop(chips, nh * chips, lambda i: greet(z_peer(i)))
    loop(1, n, lambda k: greet(q_peer(k)))
    for peer in p_peers:
        greet(peer)
    loop(1, count, lambda k: greet(m_peer(k)))

    own_w = pltpu.make_async_copy(w_hbm.at[:, mine], w_full.at[x, h, y, :, mine], local_sem.at[0])
    loads = [
        pltpu.make_async_copy(source, target, local_sem.at[1 + i])
        for i, (source, target) in enumerate(
            [(hid_hbm, hid), (gain_hbm, gain), (truth_hbm, truth), (lat_hbm, lat), (wo_hbm, wo_raw)]
        )
    ]
    own_w.start()
    for load in loads:
        load.start()
    pl.semaphore_wait(barrier, nh * chips - chips + n - 1 + 2 + count - 1)

    own_block = w_full.at[x, h, y, :, mine]
    loop(1, nh, lambda k: send(w_hbm.at[:, mine], own_block, a1_s.at[0], a1_r.at[0], h_peer(k)))
    loads[0].wait()
    loads[1].wait()

    def normalise(rows):
        values = hid[rows, :].astype(f32)
        root = jnp.sqrt(jnp.mean(values * values, axis=-1, keepdims=True) + EPSILON)
        inverse = 1.0 / root
        inv_root[rows, :] = jnp.broadcast_to(inverse, (16, LANES))
        normed[rows, :] = (values * inverse * gain[...]).astype(bf16)

    by_rows(0, points, normalise)
    own_w.wait()
    z_blocks = w_full.at[0, 0, pl.ds(0, nh - 1), :, mine]
    drain(z_blocks, a1_r.at[0])

    def group(p_, b, cols=mine):
        x_, y_ = place(p_, (q - b + n) % n)
        return w_full.at[x_, :, y_, :, cols]

    def to_partner(p_, b):
        part = group(p_, b)
        send(part, part, a4_s.at[0], a4_r.at[0], partner)

    def to_second(b):
        part = group(p, b)
        for i in range(2):
            send(part, part, a3_s.at[0], a3_r.at[b, i], p_peers[i])
        to_partner(p, b)

    def ordered(j):
        return j + (j // 2) * (n + 1 - 2 * j)

    own_group = group(p, 0)
    loop(1, n, lambda j: send(
        own_group, own_group, a2_s.at[0], a2_r.at[ordered(j) - 1], q_peer(ordered(j))
    ))
    to_second(0)
    for load in loads[2:]:
        load.wait()
    truth_pad[...] = jnp.zeros_like(truth_pad)
    truth_pad[0:levels, :] = truth[...]
    wo_pad[...] = jnp.zeros_like(wo_pad)
    wo_pad[0:levels, :] = wo_raw[...]

    def pass_first(j):
        b = ordered(j)
        drain(own_group, a2_r.at[b - 1])
        to_second(b)

    loop(1, n, pass_first)

    truth_t[...] = truth_pad[...].T
    latitude = math.pi * ((lat[...].astype(f32) + 0.5) / LATS - 0.5)
    area = LOSS_SCALE * jnp.cos(latitude)
    strip = lat.shape[1]
    for i in range(lat.shape[0]):
        area_t[i * strip:(i + 1) * strip, :] = jnp.broadcast_to(area[i:i + 1, :], (LANES, strip)).T
    wo_t[...] = wo_pad[...].T

    def pass_second(j):
        b = ordered(j)
        for i in range(2):
            drain(own_group, a3_r.at[b, i])
            part = group(sides[i], b, quarters[i])
            send(part, part, a3_s.at[0], a3_r.at[b, 2 + i], p_peers[1 - i])
        for i in range(2):
            to_partner(sides[i], b)

    loop(0, n, pass_second)

    def pass_far(j):
        b = ordered(j)
        for i in range(2):
            drain(group(far, b, quarters[i]), a3_r.at[b, 2 + i])
        to_partner(far, b)

    loop(0, n, pass_far)

    def project(rows, cols):
        act[rows, cols] = jnp.dot(
            normed[rows, :], w_full[:, :, :, :, cols].reshape(width, half),
            preferred_element_type=f32,
        )

    def activate(rows, cols):
        a = act[rows, cols]
        hidden_act[rows, cols] = (a * (0.5 * jnp.tanh(0.5 * a) + 0.5)).astype(bf16)

    loop(0, tiles, lambda t: project(rows_at(t * tile, tile), mine))
    by_rows(0, points, lambda rows: activate(rows, mine))

    drain(w_full.at[:, :, :, :, other], a4_r.at[0])

    def share_of(t, m):
        return rows_at(t * tile + m * share, share)

    def tile_rows(t, body):
        by_rows(0, tile, lambda rows: body(rows_at(t * tile + rows.start, 16)))

    def forward(t):
        rows = rows_at(t * tile, tile)
        project(rows, other)
        tile_rows(t, lambda rows: activate(rows, other))
        field = jnp.dot(hidden_act[rows, :], wo_t[...], preferred_element_type=f32)
        fields[rows, :] = field
        coarse[rows, :] = field.astype(bf16)

        def spread(k):
            peer = m_peer(k)
            send(
                coarse.at[share_of(t, peer[0]), :], theirs.at[t, member],
                b1_s.at[0], b1_r.at[t], peer,
            )

        loop(1, count, spread)
        theirs[t, member] = coarse[share_of(t, member), :]

    loop(0, tiles, forward)

    def differentiate(rows):
        a = act[rows, :]
        s = 0.5 * jnp.tanh(0.5 * a) + 0.5
        act[rows, :] = s * (1.0 + a * (1.0 - s))

    span = min(LANES, points)
    turns = points // span

    def turn(i):
        cols = rows_at(i * span, span)
        turned = normed[cols, :].T
        for x_ in range(nx):
            for h_ in range(nh):
                for y_ in range(ny):
                    first = ((x_ * nh + h_) * ny + y_) * block
                    piece = turned[first:first + block, :]
                    to_x, to_y = (x_ * nh + h_) * block, (y_ * nh + h_) * block
                    planes[0, y_, to_x:to_x + block, cols] = piece
                    planes[1, x_, to_y:to_y + block, cols] = piece

    def answer(t):
        come = theirs.at[t, pl.ds(0, count - 1)]
        drain(come, b1_r.at[t])

        def compare(i):
            rows = rows_at(i * 16, 16)
            values = [theirs[t, m, rows, :].astype(f32) for m in range(count)]
            totals = [jnp.zeros_like(values[0]) for m in range(count)]
            for m in range(count):
                for o in range(m + 1, count):
                    s = slope(values[m] - values[o])
                    totals[m] = totals[m] + s
                    totals[o] = totals[o] - s
            for m in range(count):
                answers[t, m, rows, :] = totals[m].astype(bf16)

        loop(0, share // 16, compare)

        def reply(k):
            peer = m_peer(k)
            send(
                answers.at[t, peer[0]], pairs.at[share_of(t, member), :],
                b2_s.at[0], b2_r.at[t], peer,
            )

        loop(1, count, reply)
        pairs[share_of(t, member), :] = answers[t, member]
        tile_rows(t, differentiate)

    loop(0, tiles, answer)
    loop(0, turns, turn)

    fair = (1.0 - (1.0 - ALPHA) / count) / (count * (count - 1))

    def backward(t):
        come = pairs.at[pl.ds(0, tile - share), :]
        drain(come, b2_r.at[t])
        rows = rows_at(t * tile, tile)
        grad_fields = area_t[rows, :] * (
            slope(fields[rows, :] - truth_t[rows, :]) * (1.0 / count)
            - fair * pairs[rows, :].astype(f32)
        )
        grad_act = jnp.dot(grad_fields.astype(bf16), wo_pad[...], preferred_element_type=f32)
        gp[rows, :] = (grad_act * act[rows, :]).astype(bf16)

    depth = width // n
    early = (tiles - 1) * tile

    def nth(i, own):
        first = jnp.where(i == 0, (own + 2) % n, own + 1 - 2 * (own % 2))
        return jnp.where(i < 2, first, jnp.where(i == 2, n - 1 - own, own))

    def product(which, i, begin, end):
        plane, cols = (nth(i, p), mine) if which else (nth(i, q), other)
        return jnp.dot(
            planes[core if which else 1 - core, plane, :, begin:end], gp[begin:end, cols],
            preferred_element_type=f32,
        )

    def early_planes(i):
        for which in range(2):
            parts[which, i] = product(which, i, 0, early)

    loop(0, tiles - 1, backward)
    loop(0, n, early_planes)
    backward(tiles - 1)

    def other_plane(i):
        part = parts[0, i] + product(0, i, early, points)
        csend[i] = part.astype(bf16)
        send(csend.at[i], crecv.at[i], c0_s.at[0], c0_r.at[i], partner)

    loop(0, n, other_plane)

    halves = [slice(0, quarter), slice(quarter, half)]

    def to_side(slot, target):
        send(send1.at[slot], recv1.at[slot], c1_s.at[0], c1_r.at[slot], p_peers[target])

    def own_plane(i):
        part = parts[1, i] + product(1, i, early, points)
        drain(crecv.at[i], c0_r.at[i])
        total = part + crecv[i].astype(f32)
        sums[i] = total

        @pl.when(i == 0)
        def _():
            for side in range(2):
                send1[side] = total[:, halves[side]].astype(bf16)
                to_side(side, side)

        for side in range(2):
            @pl.when(i == 1 + side)
            def _():
                send1[2 + side] = total[:, halves[side]].astype(bf16)
                to_side(2 + side, side)

    loop(0, n, own_plane)
    for side in range(2):
        drain(recv1.at[side], c1_r.at[side])
        term = sums[2 - side, :, halves[side]] + recv1[side].astype(f32)
        send1[4 + side] = term.astype(bf16)
        to_side(4 + side, 1 - side)

    def grad_normed(x_):
        cols = rows_at(x_ * depth, depth)
        act[:, cols] = lax.dot_general(
            gp[...], w_full[x_].reshape(depth, width), (((1,), (1,)), ((), ())),
            preferred_element_type=f32,
        )

    def hidden_grad(rows):
        scaled = act[rows, :] * gain[...]
        inverse = inv_root[rows, 0:1]
        unit = hid[rows, :].astype(f32) * inverse
        inner = jnp.mean(scaled * unit, axis=-1, keepdims=True)
        gh[rows, :] = ((scaled - unit * inner) * inverse).astype(bf16)

    loop(0, n // 2, grad_normed)
    for slot in range(2, 6):
        drain(recv1.at[slot], c1_r.at[slot])
    line_rows = nh * block

    def add_planes(q_):
        rows = rows_at(q_ * line_rows, line_rows)
        both = [
            sums[n - 1, rows, halves[i]] + recv1[2 + i, rows, :].astype(f32)
            + recv1[4 + i, rows, :].astype(f32)
            for i in range(2)
        ]
        return jnp.concatenate(both, axis=1)

    def to_first(j):
        k = ordered(n - j)
        send2[j - 1] = add_planes((q + k) % n).astype(bf16)
        send(send2.at[j - 1], recv2.at[j - 1], c2_s.at[0], c2_r.at[0], q_peer(k))

    loop(1, n, to_first)
    total = add_planes(q)
    loop(n // 2, n, grad_normed)
    drain(recv2, c2_r.at[0])
    for i in range(n - 1):
        total = total + recv2[i].astype(f32)
    strip = half // chips
    for h_ in range(nh):
        for l_ in range(chips):
            send3[h_, l_] = total[
                h_ * block:(h_ + 1) * block, l_ * strip:(l_ + 1) * strip
            ].astype(bf16)
    loop(1, nh * chips, lambda i: send(
        send3.at[(h + i // chips) % nh, (low + i % chips) % chips], recv3.at[i - 1],
        c3_s.at[0], c3_r.at[0], z_peer(i),
    ))
    by_rows(0, points // 2, hidden_grad)
    drain(recv3, c3_r.at[0])
    total = send3[h, low].astype(f32)
    for i in range(nh * chips - 1):
        total = total + recv3[i].astype(f32)
    factor = 1.0 / math.sqrt(count * points * nx * nh * ny)
    finals[core * chips + low] = total * factor
    own_final = finals.at[core * chips + low]
    loop(1, count, lambda k: send(own_final, own_final, c4_s.at[0], c4_r.at[0], m_peer(k)))
    by_rows(points // 2, points, hidden_grad)
    others = finals.at[pl.ds(0, count - 1)]
    drain(others, c4_r.at[0])
    for i in range(count):
        gw_ref[:, i * strip:(i + 1) * strip] = finals[i]

    drain(z_blocks, a1_s.at[0])
    drain(w_full.at[pl.ds(0, n - 1), :, 0, :, mine], a2_s.at[0])
    drain(w_full.at[:, :, pl.ds(0, 3), :, mine], a3_s.at[0])
    drain(w_full.at[:, :, :, :, mine], a4_s.at[0])
    drain(coarse.at[pl.ds(0, points - points // count), :], b1_s.at[0])
    drain(coarse.at[pl.ds(0, points - points // count), :], b2_s.at[0])
    drain(csend, c0_s.at[0])
    drain(send1, c1_s.at[0])
    drain(send2, c2_s.at[0])
    drain(recv3, c3_s.at[0])
    drain(others, c4_s.at[0])


def hand_over(*arrays):
    pieces = 4

    def body(*refs):
        sources, targets, sems = refs[:len(arrays)], refs[len(arrays):-1], refs[-1]
        copies = []
        for source, target in zip(sources, targets):
            rows = source.shape[0]
            parts = pieces if rows % (16 * pieces) == 0 else 1
            for i in range(parts):
                part = pl.ds(i * (rows // parts), rows // parts)
                copies.append(
                    pltpu.make_async_copy(source.at[part], target.at[part], sems.at[len(copies)])
                )
        for copy in copies:
            copy.start()
        for copy in copies:
            copy.wait()

    anywhere = pl.BlockSpec(memory_space=pl.ANY)
    return pl.pallas_call(
        body,
        out_shape=tuple(jax.ShapeDtypeStruct(a.shape, a.dtype) for a in arrays),
        in_specs=[anywhere] * len(arrays),
        out_specs=(anywhere,) * len(arrays),
        scratch_shapes=[pltpu.SemaphoreType.DMA((pieces * len(arrays),))],
        compiler_params=pltpu.CompilerParams(vmem_limit_bytes=1024 * 1024),
        name="hand_over",
    )(*arrays)


def per_device(hidden, truth, lat_row, gain, w_in, w_out):
    nx, nh, ny = GRID
    count = lax.axis_size("member")
    _, points, width = hidden.shape
    levels = truth.shape[0]
    block = w_in.shape[0]
    half = width // 2
    tile = min(TILE, points)
    tiles, share = points // tile, tile // count
    f32, bf16 = jnp.float32, jnp.bfloat16
    vmem, dma = pltpu.VMEM, pltpu.SemaphoreType.DMA
    n, chips, lat_strip = nx, count // 2, min(LANES, points)
    scratch = [
        vmem((points, width), bf16),
        vmem((levels, points), f32),
        vmem((points // lat_strip, lat_strip), jnp.int32),
        vmem((1, width), f32),
        vmem((levels, width), bf16),
        vmem((nx, nh, ny, block, width), bf16),
        vmem((points, width), bf16),
        vmem((2, n, width // n, points), bf16),
        vmem((points, LANES), f32),
        vmem((LANES, width), bf16),
        vmem((width, LANES), bf16),
        vmem((points, width), bf16),
        vmem((LANES, points), f32),
        vmem((points, LANES), f32),
        vmem((points, LANES), f32),
        vmem((points, width), f32),
        vmem((points, LANES), f32),
        vmem((points, LANES), bf16),
        vmem((tiles, count, share, LANES), bf16),
        vmem((tiles, count, share, LANES), bf16),
        vmem((points, LANES), bf16),
        vmem((points, width), bf16),
        vmem((2, n, width // n, half), f32),
        vmem((n, width // n, half), bf16),
        vmem((n, width // n, half), bf16),
        vmem((n, width // n, half), f32),
        vmem((6, width // n, half // 2), bf16),
        vmem((6, width // n, half // 2), bf16),
        vmem((n - 1, nh * block, half), bf16),
        vmem((n - 1, nh * block, half), bf16),
        vmem((nh, chips, block, half // chips), bf16),
        vmem((nh * chips - 1, block, half // chips), bf16),
        vmem((count, block, half // chips), f32),
        dma((6,)),
    ]
    for arrivals in (
        (1,), (n - 1,), (n, 4), (1,),
        (tiles,), (tiles,),
        (n,), (6,), (1,), (1,), (1,),
    ):
        scratch += [dma((1,)), dma(arrivals)]
    grad_rows, grad_first = pl.pallas_call(
        functools.partial(kernel, tile),
        out_shape=(
            vmem((points, width), bf16),
            vmem((block, width), f32),
        ),
        in_specs=[pl.BlockSpec(memory_space=pltpu.HBM)] * 6,
        out_specs=(pl.BlockSpec(memory_space=vmem),) * 2,
        scratch_shapes=scratch,
        compiler_params=pltpu.CompilerParams(
            collective_id=0, has_side_effects=True, vmem_limit_bytes=57 * 1024 * 1024
        ),
        name="crps_step",
    )(
        hidden[0], truth, lat_row.reshape(points // lat_strip, lat_strip), gain[None], w_in, w_out
    )
    grad_rows, grad_first = hand_over(grad_rows, grad_first)
    return (grad_rows[None], grad_first)


def solution(mesh):
    in_specs = (
        P("member", "space", None),
        P(None, "space"),
        P("space"),
        P(),
        P("space", None),
        P(),
    )
    out_specs = (P("member", "space", None), P("space", None))
    return jax.shard_map(
        per_device, mesh=mesh, in_specs=in_specs, out_specs=out_specs, check_vma=False
    )
```

```python
import functools
import math

import jax
import jax.numpy as jnp
from jax import lax
from jax.experimental import pallas as pl
from jax.experimental.pallas import tpu as pltpu
from jax.sharding import PartitionSpec as P

LATS = 721
ALPHA = 0.95
SMOOTH = 0.1
LOSS_SCALE = 64.0
EPSILON = 1e-05

GRID = (4, 4, 4)
LANES = 128
TILE = 256
MESH = pl.DeviceIdType.MESH


def slope(diff):
    return diff * lax.rsqrt(diff * diff + SMOOTH * SMOOTH)


def rows_at(start, size):
    return pl.ds(pl.multiple_of(start, size), size)


def kernel(
    tile,
    hid_hbm, truth_hbm, lat_hbm, gain_hbm, w_hbm, wo_hbm,
    gh, gw_ref,
    hid, truth, lat, gain, wo_raw, w_full, normed, planes, inv_root, wo_pad, wo_t, hidden_act,
    truth_pad, truth_t, area_t, act, fields, coarse, theirs, answers, pairs, gp, parts,
    csend, crecv, sums, send1, recv1, send2, recv2, send3, recv3, finals,
    local_sem, a1_s, a1_r, a2_s, a2_r, a3_s, a3_r, a4_s, a4_r,
    b1_s, b1_r, b2_s, b2_r, c0_s, c0_r, c1_s, c1_r, c2_s, c2_r, c3_s, c3_r, c4_s, c4_r,
):
    nx, nh, ny = GRID
    n = nx
    points, width = hid.shape
    half = width // 2
    quarter = half // 2
    levels = truth.shape[0]
    count = finals.shape[0]
    chips = count // 2
    block = w_full.shape[3]
    tiles, share = theirs.shape[0], theirs.shape[2]
    f32, bf16 = jnp.float32, jnp.bfloat16

    member, space = lax.axis_index("member"), lax.axis_index("space")
    core, low = member % 2, member // 2
    x, h, y = space // (nh * ny), (space // ny) % nh, space % ny
    q, p = x * (1 - core) + y * core, y * (1 - core) + x * core
    mine = pl.ds(pl.multiple_of(core * half, half), half)
    other = pl.ds(pl.multiple_of((1 - core) * half, half), half)
    quarters = [
        pl.ds(pl.multiple_of(core * half + i * quarter, quarter), quarter) for i in range(2)
    ]

    def place(p_, q_):
        return q_ * (1 - core) + p_ * core, p_ * (1 - core) + q_ * core

    def at(p_, q_, h_):
        x_, y_ = place(p_, q_)
        return (member, (x_ * nh + h_) * ny + y_)

    def h_peer(k):
        return at(p, q, (h + k) % nh)

    def q_peer(k):
        return at(p, (q + k) % n, h)

    def m_peer(k):
        return ((member + k) % count, space)

    def z_peer(i):
        dh, dl = i // chips, i % chips
        return (2 * ((low + dl) % chips) + core, (x * nh + (h + dh) % nh) * ny + y)

    sides = [p + 1 - 2 * (p % 2), n - 1 - p]
    far = (p + 2) % n
    p_peers = [at(v, q, h) for v in sides]
    partner = (member + 1 - 2 * core, space)

    def send(src, dst, send_sem, recv_sem, target):
        pltpu.make_async_remote_copy(
            src_ref=src, dst_ref=dst, send_sem=send_sem, recv_sem=recv_sem,
            device_id=target, device_id_type=MESH,
        ).start()

    def drain(ref, sem):
        pltpu.make_async_copy(ref, ref, sem).wait()

    def loop(first, last, body):
        def step(i, carry):
            body(i)
            return carry

        lax.fori_loop(first, last, step, 0)

    def by_rows(first, last, body):
        chunks = math.gcd(4, (last - first) // 16)

        def step(i):
            for u in range(chunks):
                body(rows_at(first + (i * chunks + u) * 16, 16))

        loop(0, (last - first) // (16 * chunks), step)

    barrier = pltpu.get_barrier_semaphore()

    def greet(peer):
        pl.semaphore_signal(barrier, inc=1, device_id=peer, device_id_type=MESH)

    loop(chips, nh * chips, lambda i: greet(z_peer(i)))
    loop(1, n, lambda k: greet(q_peer(k)))
    for peer in p_peers:
        greet(peer)
    loop(1, count, lambda k: greet(m_peer(k)))

    own_w = pltpu.make_async_copy(w_hbm.at[:, mine], w_full.at[x, h, y, :, mine], local_sem.at[0])
    loads = [
        pltpu.make_async_copy(source, target, local_sem.at[1 + i])
        for i, (source, target) in enumerate(
            [(hid_hbm, hid), (gain_hbm, gain), (truth_hbm, truth), (lat_hbm, lat), (wo_hbm, wo_raw)]
        )
    ]
    own_w.start()
    for load in loads:
        load.start()
    pl.semaphore_wait(barrier, nh * chips - chips + n - 1 + 2 + count - 1)

    own_block = w_full.at[x, h, y, :, mine]
    loop(1, nh, lambda k: send(w_hbm.at[:, mine], own_block, a1_s.at[0], a1_r.at[0], h_peer(k)))
    loads[0].wait()
    loads[1].wait()

    def normalise(rows):
        values = hid[rows, :].astype(f32)
        root = jnp.sqrt(jnp.mean(values * values, axis=-1, keepdims=True) + EPSILON)
        inverse = 1.0 / root
        inv_root[rows, :] = jnp.broadcast_to(inverse, (16, LANES))
        normed[rows, :] = (values * inverse * gain[...]).astype(bf16)

    by_rows(0, points, normalise)
    own_w.wait()
    z_blocks = w_full.at[0, 0, pl.ds(0, nh - 1), :, mine]
    drain(z_blocks, a1_r.at[0])

    span = min(LANES, points)
    turns = points // span

    def turn(i):
        cols = rows_at(i * span, span)
        turned = normed[cols, :].T
        for x_ in range(nx):
            for h_ in range(nh):
                for y_ in range(ny):
                    first = ((x_ * nh + h_) * ny + y_) * block
                    piece = turned[first:first + block, :]
                    to_x, to_y = (x_ * nh + h_) * block, (y_ * nh + h_) * block
                    planes[0, y_, to_x:to_x + block, cols] = piece
                    planes[1, x_, to_y:to_y + block, cols] = piece

    def group(p_, b, cols=mine):
        x_, y_ = place(p_, (q - b + n) % n)
        return w_full.at[x_, :, y_, :, cols]

    def to_partner(p_, b):
        part = group(p_, b)
        send(part, part, a4_s.at[0], a4_r.at[0], partner)

    def to_second(b):
        part = group(p, b)
        for i in range(2):
            send(part, part, a3_s.at[0], a3_r.at[b, i], p_peers[i])
        to_partner(p, b)

    def ordered(j):
        return j + (j // 2) * (n + 1 - 2 * j)

    own_group = group(p, 0)
    loop(1, n, lambda j: send(
        own_group, own_group, a2_s.at[0], a2_r.at[ordered(j) - 1], q_peer(ordered(j))
    ))
    to_second(0)
    loop(0, turns // 3, turn)
    for load in loads[2:]:
        load.wait()
    truth_pad[...] = jnp.zeros_like(truth_pad)
    truth_pad[0:levels, :] = truth[...]
    wo_pad[...] = jnp.zeros_like(wo_pad)
    wo_pad[0:levels, :] = wo_raw[...]

    def pass_first(j):
        b = ordered(j)
        drain(own_group, a2_r.at[b - 1])
        to_second(b)

    loop(1, n, pass_first)
    loop(turns // 3, 2 * turns // 3, turn)

    truth_t[...] = truth_pad[...].T
    latitude = math.pi * ((lat[...].astype(f32) + 0.5) / LATS - 0.5)
    area = LOSS_SCALE * jnp.cos(latitude)
    strip = lat.shape[1]
    for i in range(lat.shape[0]):
        area_t[i * strip:(i + 1) * strip, :] = jnp.broadcast_to(area[i:i + 1, :], (LANES, strip)).T
    wo_t[...] = wo_pad[...].T

    def pass_second(j):
        b = ordered(j)
        for i in range(2):
            drain(own_group, a3_r.at[b, i])
            part = group(sides[i], b, quarters[i])
            send(part, part, a3_s.at[0], a3_r.at[b, 2 + i], p_peers[1 - i])
        for i in range(2):
            to_partner(sides[i], b)

    loop(0, n, pass_second)
    loop(2 * turns // 3, turns, turn)

    def pass_far(j):
        b = ordered(j)
        for i in range(2):
            drain(group(far, b, quarters[i]), a3_r.at[b, 2 + i])
        to_partner(far, b)

    loop(0, n, pass_far)

    def project(rows, cols):
        act[rows, cols] = jnp.dot(
            normed[rows, :], w_full[:, :, :, :, cols].reshape(width, half),
            preferred_element_type=f32,
        )

    def activate(rows, cols):
        a = act[rows, cols]
        hidden_act[rows, cols] = (a * (0.5 * jnp.tanh(0.5 * a) + 0.5)).astype(bf16)

    loop(0, tiles, lambda t: project(rows_at(t * tile, tile), mine))
    by_rows(0, points, lambda rows: activate(rows, mine))

    drain(w_full.at[:, :, :, :, other], a4_r.at[0])

    def share_of(t, m):
        return rows_at(t * tile + m * share, share)

    def tile_rows(t, body):
        by_rows(0, tile, lambda rows: body(rows_at(t * tile + rows.start, 16)))

    def forward(t):
        rows = rows_at(t * tile, tile)
        project(rows, other)
        tile_rows(t, lambda rows: activate(rows, other))
        field = jnp.dot(hidden_act[rows, :], wo_t[...], preferred_element_type=f32)
        fields[rows, :] = field
        coarse[rows, :] = field.astype(bf16)

        def spread(k):
            peer = m_peer(k)
            send(
                coarse.at[share_of(t, peer[0]), :], theirs.at[t, member],
                b1_s.at[0], b1_r.at[t], peer,
            )

        loop(1, count, spread)
        theirs[t, member] = coarse[share_of(t, member), :]

    def answer(t):
        come = theirs.at[t, pl.ds(0, count - 1)]
        drain(come, b1_r.at[t])

        def compare(i):
            rows = rows_at(i * 16, 16)
            values = [theirs[t, m, rows, :].astype(f32) for m in range(count)]
            totals = [jnp.zeros_like(values[0]) for m in range(count)]
            for m in range(count):
                for o in range(m + 1, count):
                    s = slope(values[m] - values[o])
                    totals[m] = totals[m] + s
                    totals[o] = totals[o] - s
            for m in range(count):
                answers[t, m, rows, :] = totals[m].astype(bf16)

        loop(0, share // 16, compare)

        def reply(k):
            peer = m_peer(k)
            send(
                answers.at[t, peer[0]], pairs.at[share_of(t, member), :],
                b2_s.at[0], b2_r.at[t], peer,
            )

        loop(1, count, reply)
        pairs[share_of(t, member), :] = answers[t, member]


    def differentiate(rows):
        a = act[rows, :]
        s = 0.5 * jnp.tanh(0.5 * a) + 0.5
        act[rows, :] = s * (1.0 + a * (1.0 - s))

    loop(0, tiles - 1, forward)
    if tiles > 1:
        loop(0, tiles - 2, answer)
    forward(tiles - 1)
    if tiles > 1:
        answer(tiles - 2)
    tile_rows(0, differentiate)
    answer(tiles - 1)
    by_rows(tile, points, differentiate)

    fair = (1.0 - (1.0 - ALPHA) / count) / (count * (count - 1))

    def backward(t):
        come = pairs.at[pl.ds(0, tile - share), :]
        drain(come, b2_r.at[t])
        rows = rows_at(t * tile, tile)
        grad_fields = area_t[rows, :] * (
            slope(fields[rows, :] - truth_t[rows, :]) * (1.0 / count)
            - fair * pairs[rows, :].astype(f32)
        )
        grad_act = jnp.dot(grad_fields.astype(bf16), wo_pad[...], preferred_element_type=f32)
        gp[rows, :] = (grad_act * act[rows, :]).astype(bf16)

    depth = width // n
    early = (tiles - 1) * tile

    def nth(i, own):
        first = jnp.where(i == 0, (own + 2) % n, own + 1 - 2 * (own % 2))
        return jnp.where(i < 2, first, jnp.where(i == 2, n - 1 - own, own))

    def product(which, i, begin, end):
        plane, cols = (nth(i, p), mine) if which else (nth(i, q), other)
        return jnp.dot(
            planes[core if which else 1 - core, plane, :, begin:end], gp[begin:end, cols],
            preferred_element_type=f32,
        )

    def early_planes(i):
        for which in range(2):
            parts[which, i] = product(which, i, 0, early)

    loop(0, tiles - 1, backward)
    loop(0, n, early_planes)
    backward(tiles - 1)

    def other_plane(i):
        part = parts[0, i] + product(0, i, early, points)
        csend[i] = part.astype(bf16)
        send(csend.at[i], crecv.at[i], c0_s.at[0], c0_r.at[i], partner)

    loop(0, n, other_plane)

    halves = [slice(0, quarter), slice(quarter, half)]

    def to_side(slot, target):
        send(send1.at[slot], recv1.at[slot], c1_s.at[0], c1_r.at[slot], p_peers[target])

    def own_plane(i):
        part = parts[1, i] + product(1, i, early, points)
        drain(crecv.at[i], c0_r.at[i])
        total = part + crecv[i].astype(f32)
        sums[i] = total

        @pl.when(i == 0)
        def _():
            for side in range(2):
                send1[side] = total[:, halves[side]].astype(bf16)
                to_side(side, side)

        for side in range(2):
            @pl.when(i == 1 + side)
            def _():
                send1[2 + side] = total[:, halves[side]].astype(bf16)
                to_side(2 + side, side)

    loop(0, n, own_plane)
    for side in range(2):
        drain(recv1.at[side], c1_r.at[side])
        term = sums[2 - side, :, halves[side]] + recv1[side].astype(f32)
        send1[4 + side] = term.astype(bf16)
        to_side(4 + side, 1 - side)

    def grad_normed(x_):
        cols = rows_at(x_ * depth, depth)
        act[:, cols] = lax.dot_general(
            gp[...], w_full[x_].reshape(depth, width), (((1,), (1,)), ((), ())),
            preferred_element_type=f32,
        )

    def hidden_grad(rows):
        scaled = act[rows, :] * gain[...]
        inverse = inv_root[rows, 0:1]
        unit = hid[rows, :].astype(f32) * inverse
        inner = jnp.mean(scaled * unit, axis=-1, keepdims=True)
        gh[rows, :] = ((scaled - unit * inner) * inverse).astype(bf16)

    loop(0, n // 2, grad_normed)
    for slot in range(2, 6):
        drain(recv1.at[slot], c1_r.at[slot])
    line_rows = nh * block

    def add_planes(q_):
        rows = rows_at(q_ * line_rows, line_rows)
        both = [
            sums[n - 1, rows, halves[i]] + recv1[2 + i, rows, :].astype(f32)
            + recv1[4 + i, rows, :].astype(f32)
            for i in range(2)
        ]
        return jnp.concatenate(both, axis=1)

    def to_first(j):
        k = ordered(n - j)
        send2[j - 1] = add_planes((q + k) % n).astype(bf16)
        send(send2.at[j - 1], recv2.at[j - 1], c2_s.at[0], c2_r.at[0], q_peer(k))

    loop(1, n, to_first)
    total = add_planes(q)
    loop(n // 2, n, grad_normed)
    drain(recv2, c2_r.at[0])
    for i in range(n - 1):
        total = total + recv2[i].astype(f32)
    strip = half // chips
    for h_ in range(nh):
        for l_ in range(chips):
            send3[h_, l_] = total[
                h_ * block:(h_ + 1) * block, l_ * strip:(l_ + 1) * strip
            ].astype(bf16)
    loop(1, nh * chips, lambda i: send(
        send3.at[(h + i // chips) % nh, (low + i % chips) % chips], recv3.at[i - 1],
        c3_s.at[0], c3_r.at[0], z_peer(i),
    ))
    by_rows(0, points // 2, hidden_grad)
    drain(recv3, c3_r.at[0])
    total = send3[h, low].astype(f32)
    for i in range(nh * chips - 1):
        total = total + recv3[i].astype(f32)
    factor = 1.0 / math.sqrt(count * points * nx * nh * ny)
    finals[core * chips + low] = total * factor
    own_final = finals.at[core * chips + low]
    loop(1, count, lambda k: send(own_final, own_final, c4_s.at[0], c4_r.at[0], m_peer(k)))
    by_rows(points // 2, points, hidden_grad)
    others = finals.at[pl.ds(0, count - 1)]
    drain(others, c4_r.at[0])
    for i in range(count):
        gw_ref[:, i * strip:(i + 1) * strip] = finals[i]

    drain(z_blocks, a1_s.at[0])
    drain(w_full.at[pl.ds(0, n - 1), :, 0, :, mine], a2_s.at[0])
    drain(w_full.at[:, :, pl.ds(0, 3), :, mine], a3_s.at[0])
    drain(w_full.at[:, :, :, :, mine], a4_s.at[0])
    drain(coarse.at[pl.ds(0, points - points // count), :], b1_s.at[0])
    drain(coarse.at[pl.ds(0, points - points // count), :], b2_s.at[0])
    drain(csend, c0_s.at[0])
    drain(send1, c1_s.at[0])
    drain(send2, c2_s.at[0])
    drain(recv3, c3_s.at[0])
    drain(others, c4_s.at[0])


def hand_over(*arrays):
    pieces = 4

    def body(*refs):
        sources, targets, sems = refs[:len(arrays)], refs[len(arrays):-1], refs[-1]
        copies = []
        for source, target in zip(sources, targets):
            rows = source.shape[0]
            parts = pieces if rows % (16 * pieces) == 0 else 1
            for i in range(parts):
                part = pl.ds(i * (rows // parts), rows // parts)
                copies.append(
                    pltpu.make_async_copy(source.at[part], target.at[part], sems.at[len(copies)])
                )
        for copy in copies:
            copy.start()
        for copy in copies:
            copy.wait()

    anywhere = pl.BlockSpec(memory_space=pl.ANY)
    return pl.pallas_call(
        body,
        out_shape=tuple(jax.ShapeDtypeStruct(a.shape, a.dtype) for a in arrays),
        in_specs=[anywhere] * len(arrays),
        out_specs=(anywhere,) * len(arrays),
        scratch_shapes=[pltpu.SemaphoreType.DMA((pieces * len(arrays),))],
        compiler_params=pltpu.CompilerParams(vmem_limit_bytes=1024 * 1024),
        name="hand_over",
    )(*arrays)


def per_device(hidden, truth, lat_row, gain, w_in, w_out):
    nx, nh, ny = GRID
    count = lax.axis_size("member")
    _, points, width = hidden.shape
    levels = truth.shape[0]
    block = w_in.shape[0]
    half = width // 2
    tile = min(TILE, points)
    tiles, share = points // tile, tile // count
    f32, bf16 = jnp.float32, jnp.bfloat16
    vmem, dma = pltpu.VMEM, pltpu.SemaphoreType.DMA
    n, chips, lat_strip = nx, count // 2, min(LANES, points)
    scratch = [
        vmem((points, width), bf16),
        vmem((levels, points), f32),
        vmem((points // lat_strip, lat_strip), jnp.int32),
        vmem((1, width), f32),
        vmem((levels, width), bf16),
        vmem((nx, nh, ny, block, width), bf16),
        vmem((points, width), bf16),
        vmem((2, n, width // n, points), bf16),
        vmem((points, LANES), f32),
        vmem((LANES, width), bf16),
        vmem((width, LANES), bf16),
        vmem((points, width), bf16),
        vmem((LANES, points), f32),
        vmem((points, LANES), f32),
        vmem((points, LANES), f32),
        vmem((points, width), f32),
        vmem((points, LANES), f32),
        vmem((points, LANES), bf16),
        vmem((tiles, count, share, LANES), bf16),
        vmem((tiles, count, share, LANES), bf16),
        vmem((points, LANES), bf16),
        vmem((points, width), bf16),
        vmem((2, n, width // n, half), f32),
        vmem((n, width // n, half), bf16),
        vmem((n, width // n, half), bf16),
        vmem((n, width // n, half), f32),
        vmem((6, width // n, half // 2), bf16),
        vmem((6, width // n, half // 2), bf16),
        vmem((n - 1, nh * block, half), bf16),
        vmem((n - 1, nh * block, half), bf16),
        vmem((nh, chips, block, half // chips), bf16),
        vmem((nh * chips - 1, block, half // chips), bf16),
        vmem((count, block, half // chips), f32),
        dma((6,)),
    ]
    for arrivals in (
        (1,), (n - 1,), (n, 4), (1,),
        (tiles,), (tiles,),
        (n,), (6,), (1,), (1,), (1,),
    ):
        scratch += [dma((1,)), dma(arrivals)]
    grad_rows, grad_first = pl.pallas_call(
        functools.partial(kernel, tile),
        out_shape=(
            vmem((points, width), bf16),
            vmem((block, width), f32),
        ),
        in_specs=[pl.BlockSpec(memory_space=pltpu.HBM)] * 6,
        out_specs=(pl.BlockSpec(memory_space=vmem),) * 2,
        scratch_shapes=scratch,
        compiler_params=pltpu.CompilerParams(
            collective_id=0, has_side_effects=True, vmem_limit_bytes=57 * 1024 * 1024
        ),
        name="crps_step",
    )(
        hidden[0], truth, lat_row.reshape(points // lat_strip, lat_strip), gain[None], w_in, w_out
    )
    grad_rows, grad_first = hand_over(grad_rows, grad_first)
    return (grad_rows[None], grad_first)


def solution(mesh):
    in_specs = (
        P("member", "space", None),
        P(None, "space"),
        P("space"),
        P(),
        P("space", None),
        P(),
    )
    out_specs = (P("member", "space", None), P("space", None))
    return jax.shard_map(
        per_device, mesh=mesh, in_specs=in_specs, out_specs=out_specs, check_vma=False
    )
```

```python
import functools
import math

import jax
import jax.numpy as jnp
from jax import lax
from jax.experimental import pallas as pl
from jax.experimental.pallas import tpu as pltpu
from jax.sharding import PartitionSpec as P

LATS = 721
ALPHA = 0.95
SMOOTH = 0.1
LOSS_SCALE = 64.0
EPSILON = 1e-05

GRID = (4, 4, 4)
LANES = 128
TILE = 256
MESH = pl.DeviceIdType.MESH


def slope(diff):
    return diff * lax.rsqrt(diff * diff + SMOOTH * SMOOTH)


def rows_at(start, size):
    return pl.ds(pl.multiple_of(start, size), size)


def kernel(
    tile,
    hid_hbm, truth_hbm, lat_hbm, gain_hbm, w_hbm, wo_hbm,
    gh, gw_ref,
    hid, truth, lat, gain, wo_raw, w_full, normed, planes, inv_root, wo_pad, wo_t, hidden_act,
    truth_pad, truth_t, area_t, act, fields, coarse, theirs, answers, pairs, gp,
    csend, crecv, sums, send1, recv1, send2, recv2, send3, recv3, finals,
    local_sem, a1_s, a1_r, a2_s, a2_r, a3_s, a3_r, a4_s, a4_r,
    b1_s, b1_r, b2_s, b2_r, c0_s, c0_r, c1_s, c1_r, c2_s, c2_r, c3_s, c3_r, c4_s, c4_r,
):
    nx, nh, ny = GRID
    n = nx
    points, width = hid.shape
    half = width // 2
    quarter = half // 2
    levels = truth.shape[0]
    count = finals.shape[0]
    chips = count // 2
    block = w_full.shape[3]
    tiles, share = theirs.shape[0], theirs.shape[2]
    f32, bf16 = jnp.float32, jnp.bfloat16

    member, space = lax.axis_index("member"), lax.axis_index("space")
    core, low = member % 2, member // 2
    x, h, y = space // (nh * ny), (space // ny) % nh, space % ny
    q, p = x * (1 - core) + y * core, y * (1 - core) + x * core
    mine = pl.ds(pl.multiple_of(core * half, half), half)
    other = pl.ds(pl.multiple_of((1 - core) * half, half), half)
    quarters = [
        pl.ds(pl.multiple_of(core * half + i * quarter, quarter), quarter) for i in range(2)
    ]

    def place(p_, q_):
        return q_ * (1 - core) + p_ * core, p_ * (1 - core) + q_ * core

    def at(p_, q_, h_):
        x_, y_ = place(p_, q_)
        return (member, (x_ * nh + h_) * ny + y_)

    def h_peer(k):
        return at(p, q, (h + k) % nh)

    def q_peer(k):
        return at(p, (q + k) % n, h)

    def m_peer(k):
        return ((member + k) % count, space)

    def z_peer(i):
        dh, dl = i // chips, i % chips
        return (2 * ((low + dl) % chips) + core, (x * nh + (h + dh) % nh) * ny + y)

    sides = [p + 1 - 2 * (p % 2), n - 1 - p]
    far = (p + 2) % n
    p_peers = [at(v, q, h) for v in sides]
    partner = (member + 1 - 2 * core, space)

    def send(src, dst, send_sem, recv_sem, target):
        pltpu.make_async_remote_copy(
            src_ref=src, dst_ref=dst, send_sem=send_sem, recv_sem=recv_sem,
            device_id=target, device_id_type=MESH,
        ).start()

    def drain(ref, sem):
        pltpu.make_async_copy(ref, ref, sem).wait()

    def loop(first, last, body):
        def step(i, carry):
            body(i)
            return carry

        lax.fori_loop(first, last, step, 0)

    def by_rows(first, last, body):
        chunks = math.gcd(4, (last - first) // 16)

        def step(i):
            for u in range(chunks):
                body(rows_at(first + (i * chunks + u) * 16, 16))

        loop(0, (last - first) // (16 * chunks), step)

    barrier = pltpu.get_barrier_semaphore()

    def greet(peer):
        pl.semaphore_signal(barrier, inc=1, device_id=peer, device_id_type=MESH)

    loop(chips, nh * chips, lambda i: greet(z_peer(i)))
    loop(1, n, lambda k: greet(q_peer(k)))
    for peer in p_peers:
        greet(peer)
    loop(1, count, lambda k: greet(m_peer(k)))

    own_w = pltpu.make_async_copy(w_hbm.at[:, mine], w_full.at[x, h, y, :, mine], local_sem.at[0])
    loads = [
        pltpu.make_async_copy(source, target, local_sem.at[1 + i])
        for i, (source, target) in enumerate(
            [(hid_hbm, hid), (gain_hbm, gain), (truth_hbm, truth), (lat_hbm, lat), (wo_hbm, wo_raw)]
        )
    ]
    own_w.start()
    for load in loads:
        load.start()
    pl.semaphore_wait(barrier, nh * chips - chips + n - 1 + 2 + count - 1)

    own_block = w_full.at[x, h, y, :, mine]
    def to_z(dh, l_):
        target = (2 * l_ + core, (x * nh + (h + dh) % nh) * ny + y)
        send(w_hbm.at[:, mine], own_block, a1_s.at[0], a1_r.at[0], target)

    ends = ((chips - 1, 1, 0), (0, nh - 1, chips // 2))

    def from_end(action):
        for end, toward, start in ends:
            @pl.when(low == end)
            def _():
                action(toward, start)

    def spread_z(toward, start):
        loop(0, chips, lambda l_: to_z(toward, l_))
        loop(start, start + chips // 2, lambda l_: to_z(2, l_))

    if chips == 1:
        loop(1, nh, lambda k: to_z(k, 0))
    else:
        from_end(spread_z)
    loads[0].wait()
    loads[1].wait()

    def normalise(rows):
        values = hid[rows, :].astype(f32)
        root = jnp.sqrt(jnp.mean(values * values, axis=-1, keepdims=True) + EPSILON)
        inverse = 1.0 / root
        inv_root[rows, :] = jnp.broadcast_to(inverse, (16, LANES))
        normed[rows, :] = (values * inverse * gain[...]).astype(bf16)

    by_rows(0, points, normalise)
    for load in loads[2:]:
        load.wait()
    wo_pad[...] = jnp.zeros_like(wo_pad)
    wo_pad[0:levels, :] = wo_raw[...]
    wo_t[...] = wo_pad[...].T

    span = min(LANES, points)
    turns = points // span

    def turn(i):
        cols = rows_at(i * span, span)
        turned = normed[cols, :].T
        for x_ in range(nx):
            for h_ in range(nh):
                for y_ in range(ny):
                    first = ((x_ * nh + h_) * ny + y_) * block
                    piece = turned[first:first + block, :]
                    to_x, to_y = (x_ * nh + h_) * block, (y_ * nh + h_) * block
                    planes[0, y_, to_x:to_x + block, cols] = piece
                    planes[1, x_, to_y:to_y + block, cols] = piece

    loop(0, turns // 2, turn)
    own_w.wait()
    z_blocks = w_full.at[0, 0, pl.ds(0, nh - 1), :, mine]
    drain(z_blocks, a1_r.at[0])

    def group(p_, b, cols=mine):
        x_, y_ = place(p_, (q - b + n) % n)
        return w_full.at[x_, :, y_, :, cols]

    def to_partner(p_, b):
        part = group(p_, b)
        send(part, part, a4_s.at[0], a4_r.at[0], partner)

    def to_second(b):
        part = group(p, b)
        for i in range(2):
            send(part, part, a3_s.at[0], a3_r.at[b, i], p_peers[i])
        to_partner(p, b)

    def ordered(j):
        return j + (j // 2) * (n + 1 - 2 * j)

    own_group = group(p, 0)
    loop(1, n, lambda j: send(
        own_group, own_group, a2_s.at[0], a2_r.at[ordered(j) - 1], q_peer(ordered(j))
    ))
    to_second(0)
    def pass_first(j):
        b = ordered(j)
        drain(own_group, a2_r.at[b - 1])
        to_second(b)

    loop(1, n, pass_first)

    def pass_second(j):
        b = ordered(j)
        for i in range(2):
            drain(own_group, a3_r.at[b, i])
            part = group(sides[i], b, quarters[i])
            send(part, part, a3_s.at[0], a3_r.at[b, 2 + i], p_peers[1 - i])
        for i in range(2):
            to_partner(sides[i], b)

    loop(0, n, pass_second)

    def pass_far(j):
        b = ordered(j)
        for i in range(2):
            drain(group(far, b, quarters[i]), a3_r.at[b, 2 + i])
        to_partner(far, b)

    loop(0, n, pass_far)

    def project(rows, cols):
        act[rows, cols] = jnp.dot(
            normed[rows, :], w_full[:, :, :, :, cols].reshape(width, half),
            preferred_element_type=f32,
        )

    def activate(rows, cols):
        a = act[rows, cols]
        hidden_act[rows, cols] = (a * (0.5 * jnp.tanh(0.5 * a) + 0.5)).astype(bf16)

    ahead = max(tiles - 1, 1)
    loop(0, ahead, lambda t: project(rows_at(t * tile, tile), mine))
    by_rows(0, ahead * tile, lambda rows: activate(rows, mine))

    drain(w_full.at[:, :, :, :, other], a4_r.at[0])

    def share_of(t, m):
        return rows_at(t * tile + m * share, share)

    def tile_rows(t, body):
        by_rows(0, tile, lambda rows: body(rows_at(t * tile + rows.start, 16)))

    def forward(t):
        rows = rows_at(t * tile, tile)
        project(rows, other)
        tile_rows(t, lambda rows: activate(rows, other))
        field = jnp.dot(hidden_act[rows, :], wo_t[...], preferred_element_type=f32)
        fields[rows, :] = field
        coarse[rows, :] = field.astype(bf16)

        def spread(k):
            peer = m_peer(k)
            send(
                coarse.at[share_of(t, peer[0]), :], theirs.at[t, member],
                b1_s.at[0], b1_r.at[t], peer,
            )

        loop(1, count, spread)
        theirs[t, member] = coarse[share_of(t, member), :]

    def answer(t):
        come = theirs.at[t, pl.ds(0, count - 1)]
        drain(come, b1_r.at[t])

        def compare(i):
            rows = rows_at(i * 16, 16)
            values = [theirs[t, m, rows, :].astype(f32) for m in range(count)]
            totals = [jnp.zeros_like(values[0]) for m in range(count)]
            for m in range(count):
                for o in range(m + 1, count):
                    s = slope(values[m] - values[o])
                    totals[m] = totals[m] + s
                    totals[o] = totals[o] - s
            for m in range(count):
                answers[t, m, rows, :] = totals[m].astype(bf16)

        loop(0, share // 16, compare)

        def reply(k):
            peer = m_peer(k)
            send(
                answers.at[t, peer[0]], pairs.at[share_of(t, member), :],
                b2_s.at[0], b2_r.at[t], peer,
            )

        loop(1, count, reply)
        pairs[share_of(t, member), :] = answers[t, member]


    def differentiate(rows):
        a = act[rows, :]
        s = 0.5 * jnp.tanh(0.5 * a) + 0.5
        act[rows, :] = s * (1.0 + a * (1.0 - s))

    loop(0, ahead, forward)
    truth_pad[...] = jnp.zeros_like(truth_pad)
    truth_pad[0:levels, :] = truth[...]
    truth_t[...] = truth_pad[...].T
    latitude = math.pi * ((lat[...].astype(f32) + 0.5) / LATS - 0.5)
    area = LOSS_SCALE * jnp.cos(latitude)
    strip = lat.shape[1]
    for i in range(lat.shape[0]):
        area_t[i * strip:(i + 1) * strip, :] = jnp.broadcast_to(area[i:i + 1, :], (LANES, strip)).T
    if ahead < tiles:
        project(rows_at(ahead * tile, tile), mine)
        tile_rows(ahead, lambda rows: activate(rows, mine))
        forward(ahead)

    def reply_and_prepare(t):
        answer(t)
        tile_rows(t, differentiate)
        left = turns - turns // 2
        loop(turns // 2 + t * left // tiles, turns // 2 + (t + 1) * left // tiles, turn)

    loop(0, tiles, reply_and_prepare)

    fair = (1.0 - (1.0 - ALPHA) / count) / (count * (count - 1))

    def backward(t):
        come = pairs.at[pl.ds(0, tile - share), :]
        drain(come, b2_r.at[t])
        rows = rows_at(t * tile, tile)
        grad_fields = area_t[rows, :] * (
            slope(fields[rows, :] - truth_t[rows, :]) * (1.0 / count)
            - fair * pairs[rows, :].astype(f32)
        )
        grad_act = jnp.dot(grad_fields.astype(bf16), wo_pad[...], preferred_element_type=f32)
        gp[rows, :] = (grad_act * act[rows, :]).astype(bf16)

    depth = width // n

    def nth(i, own):
        first = jnp.where(i == 0, (own + 2) % n, own + 1 - 2 * (own % 2))
        return jnp.where(i < 2, first, jnp.where(i == 2, n - 1 - own, own))

    def product(which, i):
        plane, cols = (nth(i, p), mine) if which else (nth(i, q), other)
        return jnp.dot(
            planes[core if which else 1 - core, plane], gp[:, cols], preferred_element_type=f32
        )

    loop(0, tiles, backward)

    def other_plane(i):
        part = product(0, i)
        csend[i] = part.astype(bf16)
        send(csend.at[i], crecv.at[i], c0_s.at[0], c0_r.at[i], partner)

    loop(0, n, other_plane)

    halves = [slice(0, quarter), slice(quarter, half)]

    def to_side(slot, target):
        send(send1.at[slot], recv1.at[slot], c1_s.at[0], c1_r.at[slot], p_peers[target])

    def own_plane(i):
        part = product(1, i)
        drain(crecv.at[i], c0_r.at[i])
        total = part + crecv[i].astype(f32)
        sums[i] = total

        @pl.when(i == 0)
        def _():
            for side in range(2):
                send1[side] = total[:, halves[side]].astype(bf16)
                to_side(side, side)

        for side in range(2):
            @pl.when(i == 1 + side)
            def _():
                send1[2 + side] = total[:, halves[side]].astype(bf16)
                to_side(2 + side, side)

    loop(0, n, own_plane)
    for side in range(2):
        drain(recv1.at[side], c1_r.at[side])
        term = sums[2 - side, :, halves[side]] + recv1[side].astype(f32)
        send1[4 + side] = term.astype(bf16)
        to_side(4 + side, 1 - side)

    def grad_normed(x_):
        cols = rows_at(x_ * depth, depth)
        act[:, cols] = lax.dot_general(
            gp[...], w_full[x_].reshape(depth, width), (((1,), (1,)), ((), ())),
            preferred_element_type=f32,
        )

    def hidden_grad(rows):
        scaled = act[rows, :] * gain[...]
        inverse = inv_root[rows, 0:1]
        unit = hid[rows, :].astype(f32) * inverse
        inner = jnp.mean(scaled * unit, axis=-1, keepdims=True)
        gh[rows, :] = ((scaled - unit * inner) * inverse).astype(bf16)

    loop(0, n // 2, grad_normed)
    for slot in range(2, 6):
        drain(recv1.at[slot], c1_r.at[slot])
    line_rows = nh * block

    def add_planes(q_):
        rows = rows_at(q_ * line_rows, line_rows)
        both = [
            sums[n - 1, rows, halves[i]] + recv1[2 + i, rows, :].astype(f32)
            + recv1[4 + i, rows, :].astype(f32)
            for i in range(2)
        ]
        return jnp.concatenate(both, axis=1)

    def to_first(j):
        k = ordered(n - j)
        send2[j - 1] = add_planes((q + k) % n).astype(bf16)
        send(send2.at[j - 1], recv2.at[j - 1], c2_s.at[0], c2_r.at[0], q_peer(k))

    loop(1, n, to_first)
    total = add_planes(q)
    loop(n // 2, n, grad_normed)
    drain(recv2, c2_r.at[0])
    for i in range(n - 1):
        total = total + recv2[i].astype(f32)
    strip = half // chips
    for h_ in range(nh):
        for l_ in range(chips):
            send3[h_, l_] = total[
                h_ * block:(h_ + 1) * block, l_ * strip:(l_ + 1) * strip
            ].astype(bf16)
    loop(1, nh * chips, lambda i: send(
        send3.at[(h + i // chips) % nh, (low + i % chips) % chips], recv3.at[i - 1],
        c3_s.at[0], c3_r.at[0], z_peer(i),
    ))
    by_rows(0, points // 2, hidden_grad)
    drain(recv3, c3_r.at[0])
    total = send3[h, low].astype(f32)
    for i in range(nh * chips - 1):
        total = total + recv3[i].astype(f32)
    factor = 1.0 / math.sqrt(count * points * nx * nh * ny)
    finals[core * chips + low] = total * factor
    own_final = finals.at[core * chips + low]
    loop(1, count, lambda k: send(own_final, own_final, c4_s.at[0], c4_r.at[0], m_peer(k)))
    by_rows(points // 2, points, hidden_grad)
    others = finals.at[pl.ds(0, count - 1)]
    drain(others, c4_r.at[0])
    for i in range(count):
        gw_ref[:, i * strip:(i + 1) * strip] = finals[i]

    if chips == 1:
        drain(z_blocks, a1_s.at[0])
    else:
        from_end(lambda toward, start: [drain(z_blocks, a1_s.at[0]) for _ in range(2)])
    drain(w_full.at[pl.ds(0, n - 1), :, 0, :, mine], a2_s.at[0])
    drain(w_full.at[:, :, pl.ds(0, 3), :, mine], a3_s.at[0])
    drain(w_full.at[:, :, :, :, mine], a4_s.at[0])
    drain(coarse.at[pl.ds(0, points - points // count), :], b1_s.at[0])
    drain(coarse.at[pl.ds(0, points - points // count), :], b2_s.at[0])
    drain(csend, c0_s.at[0])
    drain(send1, c1_s.at[0])
    drain(send2, c2_s.at[0])
    drain(recv3, c3_s.at[0])
    drain(others, c4_s.at[0])


def hand_over(*arrays):
    pieces = 4

    def body(*refs):
        sources, targets, sems = refs[:len(arrays)], refs[len(arrays):-1], refs[-1]
        copies = []
        for source, target in zip(sources, targets):
            rows = source.shape[0]
            parts = pieces if rows % (16 * pieces) == 0 else 1
            for i in range(parts):
                part = pl.ds(i * (rows // parts), rows // parts)
                copies.append(
                    pltpu.make_async_copy(source.at[part], target.at[part], sems.at[len(copies)])
                )
        for copy in copies:
            copy.start()
        for copy in copies:
            copy.wait()

    anywhere = pl.BlockSpec(memory_space=pl.ANY)
    return pl.pallas_call(
        body,
        out_shape=tuple(jax.ShapeDtypeStruct(a.shape, a.dtype) for a in arrays),
        in_specs=[anywhere] * len(arrays),
        out_specs=(anywhere,) * len(arrays),
        scratch_shapes=[pltpu.SemaphoreType.DMA((pieces * len(arrays),))],
        compiler_params=pltpu.CompilerParams(vmem_limit_bytes=1024 * 1024),
        name="hand_over",
    )(*arrays)


def per_device(hidden, truth, lat_row, gain, w_in, w_out):
    nx, nh, ny = GRID
    count = lax.axis_size("member")
    _, points, width = hidden.shape
    levels = truth.shape[0]
    block = w_in.shape[0]
    half = width // 2
    tile = min(TILE, points)
    tiles, share = points // tile, tile // count
    f32, bf16 = jnp.float32, jnp.bfloat16
    vmem, dma = pltpu.VMEM, pltpu.SemaphoreType.DMA
    n, chips, lat_strip = nx, count // 2, min(LANES, points)
    scratch = [
        vmem((points, width), bf16),
        vmem((levels, points), f32),
        vmem((points // lat_strip, lat_strip), jnp.int32),
        vmem((1, width), f32),
        vmem((levels, width), bf16),
        vmem((nx, nh, ny, block, width), bf16),
        vmem((points, width), bf16),
        vmem((2, n, width // n, points), bf16),
        vmem((points, LANES), f32),
        vmem((LANES, width), bf16),
        vmem((width, LANES), bf16),
        vmem((points, width), bf16),
        vmem((LANES, points), f32),
        vmem((points, LANES), f32),
        vmem((points, LANES), f32),
        vmem((points, width), f32),
        vmem((points, LANES), f32),
        vmem((points, LANES), bf16),
        vmem((tiles, count, share, LANES), bf16),
        vmem((tiles, count, share, LANES), bf16),
        vmem((points, LANES), bf16),
        vmem((points, width), bf16),
        vmem((n, width // n, half), bf16),
        vmem((n, width // n, half), bf16),
        vmem((n, width // n, half), f32),
        vmem((6, width // n, half // 2), bf16),
        vmem((6, width // n, half // 2), bf16),
        vmem((n - 1, nh * block, half), bf16),
        vmem((n - 1, nh * block, half), bf16),
        vmem((nh, chips, block, half // chips), bf16),
        vmem((nh * chips - 1, block, half // chips), bf16),
        vmem((count, block, half // chips), f32),
        dma((6,)),
    ]
    for arrivals in (
        (1,), (n - 1,), (n, 4), (1,),
        (tiles,), (tiles,),
        (n,), (6,), (1,), (1,), (1,),
    ):
        scratch += [dma((1,)), dma(arrivals)]
    grad_rows, grad_first = pl.pallas_call(
        functools.partial(kernel, tile),
        out_shape=(
            vmem((points, width), bf16),
            vmem((block, width), f32),
        ),
        in_specs=[pl.BlockSpec(memory_space=pltpu.HBM)] * 6,
        out_specs=(pl.BlockSpec(memory_space=vmem),) * 2,
        scratch_shapes=scratch,
        compiler_params=pltpu.CompilerParams(
            collective_id=0, has_side_effects=True, vmem_limit_bytes=57 * 1024 * 1024
        ),
        name="crps_step",
    )(
        hidden[0], truth, lat_row.reshape(points // lat_strip, lat_strip), gain[None], w_in, w_out
    )
    grad_rows, grad_first = hand_over(grad_rows, grad_first)
    return (grad_rows[None], grad_first)


def solution(mesh):
    in_specs = (
        P("member", "space", None),
        P(None, "space"),
        P("space"),
        P(),
        P("space", None),
        P(),
    )
    out_specs = (P("member", "space", None), P("space", None))
    return jax.shard_map(
        per_device, mesh=mesh, in_specs=in_specs, out_specs=out_specs, check_vma=False
    )
```

```python
import functools
import math

import jax
import jax.numpy as jnp
from jax import lax
from jax.experimental import pallas as pl
from jax.experimental.pallas import tpu as pltpu
from jax.sharding import PartitionSpec as P

LATS = 721
ALPHA = 0.95
SMOOTH = 0.1
LOSS_SCALE = 64.0
EPSILON = 1e-05

GRID = (4, 4, 4)
LANES = 128
TILES = (128, 256, 256, 128)
MESH = pl.DeviceIdType.MESH


def slope(diff):
    return diff * lax.rsqrt(diff * diff + SMOOTH * SMOOTH)


def rows_at(start, size):
    return pl.ds(pl.multiple_of(start, size), size)


def kernel(
    sizes,
    hid_hbm, truth_hbm, lat_hbm, gain_hbm, w_hbm, wo_hbm,
    gh, gw_ref,
    hid, truth, lat, gain, wo_raw, w_full, normed, planes, inv_root, wo_pad, wo_t, hidden_act,
    truth_pad, truth_t, area_t, act, fields, coarse, theirs, answers, pairs, gp,
    csend, crecv, sums, send1, recv1, send2, recv2, send3, recv3, finals,
    local_sem, a1_s, a1_r, a2_s, a2_r, a3_s, a3_r, a4_s, a4_r,
    b1_s, b1_r, b2_s, b2_r, c0_s, c0_r, c1_s, c1_r, c2_s, c2_r, c3_s, c3_r, c4_s, c4_r,
):
    nx, nh, ny = GRID
    n = nx
    points, width = hid.shape
    half = width // 2
    quarter = half // 2
    levels = truth.shape[0]
    count = finals.shape[0]
    chips = count // 2
    block = w_full.shape[3]
    tiles = len(sizes)
    starts = [sum(sizes[:t]) for t in range(tiles)]
    shares = [size // count for size in sizes]
    f32, bf16 = jnp.float32, jnp.bfloat16

    member, space = lax.axis_index("member"), lax.axis_index("space")
    core, low = member % 2, member // 2
    x, h, y = space // (nh * ny), (space // ny) % nh, space % ny
    q, p = x * (1 - core) + y * core, y * (1 - core) + x * core
    mine = pl.ds(pl.multiple_of(core * half, half), half)
    other = pl.ds(pl.multiple_of((1 - core) * half, half), half)
    quarters = [
        pl.ds(pl.multiple_of(core * half + i * quarter, quarter), quarter) for i in range(2)
    ]

    def place(p_, q_):
        return q_ * (1 - core) + p_ * core, p_ * (1 - core) + q_ * core

    def at(p_, q_, h_):
        x_, y_ = place(p_, q_)
        return (member, (x_ * nh + h_) * ny + y_)

    def h_peer(k):
        return at(p, q, (h + k) % nh)

    def q_peer(k):
        return at(p, (q + k) % n, h)

    def m_peer(k):
        return ((member + k) % count, space)

    def z_peer(i):
        dh, dl = i // chips, i % chips
        return (2 * ((low + dl) % chips) + core, (x * nh + (h + dh) % nh) * ny + y)

    sides = [p + 1 - 2 * (p % 2), n - 1 - p]
    far = (p + 2) % n
    p_peers = [at(v, q, h) for v in sides]
    partner = (member + 1 - 2 * core, space)

    def send(src, dst, send_sem, recv_sem, target):
        pltpu.make_async_remote_copy(
            src_ref=src, dst_ref=dst, send_sem=send_sem, recv_sem=recv_sem,
            device_id=target, device_id_type=MESH,
        ).start()

    def drain(ref, sem):
        pltpu.make_async_copy(ref, ref, sem).wait()

    def loop(first, last, body):
        def step(i, carry):
            body(i)
            return carry

        lax.fori_loop(first, last, step, 0)

    def by_rows(first, last, body):
        chunks = math.gcd(4, (last - first) // 16)

        def step(i):
            for u in range(chunks):
                body(rows_at(first + (i * chunks + u) * 16, 16))

        loop(0, (last - first) // (16 * chunks), step)

    barrier = pltpu.get_barrier_semaphore()

    def greet(peer):
        pl.semaphore_signal(barrier, inc=1, device_id=peer, device_id_type=MESH)

    loop(chips, nh * chips, lambda i: greet(z_peer(i)))
    loop(1, n, lambda k: greet(q_peer(k)))
    for peer in p_peers:
        greet(peer)
    loop(1, count, lambda k: greet(m_peer(k)))

    own_w = pltpu.make_async_copy(w_hbm.at[:, mine], w_full.at[x, h, y, :, mine], local_sem.at[0])
    loads = [
        pltpu.make_async_copy(source, target, local_sem.at[1 + i])
        for i, (source, target) in enumerate(
            [(hid_hbm, hid), (gain_hbm, gain), (truth_hbm, truth), (lat_hbm, lat), (wo_hbm, wo_raw)]
        )
    ]
    for load in loads[:2]:
        load.start()
    pl.semaphore_wait(barrier, nh * chips - chips + n - 1 + 2 + count - 1)

    own_block = w_full.at[x, h, y, :, mine]
    def to_z(dh, l_):
        target = (2 * l_ + core, (x * nh + (h + dh) % nh) * ny + y)
        send(w_hbm.at[:, mine], own_block, a1_s.at[0], a1_r.at[0], target)

    ends = ((chips - 1, 1, 0), (0, nh - 1, chips // 2))

    def from_end(action):
        for end, toward, start in ends:
            @pl.when(low == end)
            def _():
                action(toward, start)

    def spread_z(toward, start):
        loop(0, chips, lambda l_: to_z(toward, l_))
        loop(start, start + chips // 2, lambda l_: to_z(2, l_))

    if chips == 1:
        loop(1, nh, lambda k: to_z(k, 0))
    else:
        from_end(spread_z)
    own_w.start()
    for load in loads[2:]:
        load.start()
    loads[0].wait()
    loads[1].wait()

    def normalise(rows):
        values = hid[rows, :].astype(f32)
        root = jnp.sqrt(jnp.mean(values * values, axis=-1, keepdims=True) + EPSILON)
        inverse = 1.0 / root
        inv_root[rows, :] = jnp.broadcast_to(inverse, (16, LANES))
        normed[rows, :] = (values * inverse * gain[...]).astype(bf16)

    by_rows(0, points, normalise)
    for load in loads[2:]:
        load.wait()
    wo_pad[...] = jnp.zeros_like(wo_pad)
    wo_pad[0:levels, :] = wo_raw[...]
    wo_t[...] = wo_pad[...].T

    span = min(LANES, points)
    turns = points // span

    def turn(i):
        cols = rows_at(i * span, span)
        turned = normed[cols, :].T
        for x_ in range(nx):
            for h_ in range(nh):
                for y_ in range(ny):
                    first = ((x_ * nh + h_) * ny + y_) * block
                    piece = turned[first:first + block, :]
                    to_x, to_y = (x_ * nh + h_) * block, (y_ * nh + h_) * block
                    planes[0, y_, to_x:to_x + block, cols] = piece
                    planes[1, x_, to_y:to_y + block, cols] = piece

    loop(0, turns // 2, turn)
    own_w.wait()
    z_blocks = w_full.at[0, 0, pl.ds(0, nh - 1), :, mine]
    drain(z_blocks, a1_r.at[0])

    def group(p_, b, cols=mine):
        x_, y_ = place(p_, (q - b + n) % n)
        return w_full.at[x_, :, y_, :, cols]

    def to_partner(p_, b):
        part = group(p_, b)
        send(part, part, a4_s.at[0], a4_r.at[0], partner)

    def to_second(b):
        part = group(p, b)
        for i in range(2):
            send(part, part, a3_s.at[0], a3_r.at[b, i], p_peers[i])
        to_partner(p, b)

    def ordered(j):
        return j + (j // 2) * (n + 1 - 2 * j)

    own_group = group(p, 0)
    loop(1, n, lambda j: send(
        own_group, own_group, a2_s.at[0], a2_r.at[ordered(j) - 1], q_peer(ordered(j))
    ))
    to_second(0)
    def pass_first(j):
        b = ordered(j)
        drain(own_group, a2_r.at[b - 1])
        to_second(b)


    def pass_second(j):
        b = ordered(j)
        for i in range(2):
            drain(own_group, a3_r.at[b, i])
            part = group(sides[i], b, quarters[i])
            send(part, part, a3_s.at[0], a3_r.at[b, 2 + i], p_peers[1 - i])
        for i in range(2):
            to_partner(sides[i], b)

    pass_second(0)
    loop(1, n, pass_first)
    loop(1, n, pass_second)

    def pass_far(j):
        b = ordered(j)
        for i in range(2):
            drain(group(far, b, quarters[i]), a3_r.at[b, 2 + i])
        to_partner(far, b)

    loop(0, n, pass_far)

    def project(rows, cols):
        act[rows, cols] = jnp.dot(
            normed[rows, :], w_full[:, :, :, :, cols].reshape(width, half),
            preferred_element_type=f32,
        )

    def activate(rows, cols):
        a = act[rows, cols]
        hidden_act[rows, cols] = (a * (0.5 * jnp.tanh(0.5 * a) + 0.5)).astype(bf16)

    def own_half(t):
        project(pl.ds(starts[t], sizes[t]), mine)
        by_rows(starts[t], starts[t] + sizes[t], lambda rows: activate(rows, mine))

    ahead = max(tiles - 1, 1)
    for t in range(ahead):
        own_half(t)
    drain(w_full.at[:, :, :, :, other], a4_r.at[0])

    def share_of(t, m):
        return rows_at(starts[t] + m * shares[t], shares[t])

    def slot(t):
        return pl.ds(starts[t] // count, shares[t])

    def forward(t):
        rows = pl.ds(starts[t], sizes[t])
        project(rows, other)
        by_rows(starts[t], starts[t] + sizes[t], lambda part: activate(part, other))
        field = jnp.dot(hidden_act[rows, :], wo_t[...], preferred_element_type=f32)
        fields[rows, :] = field
        coarse[rows, :] = field.astype(bf16)

        def spread(k):
            peer = m_peer(k)
            send(
                coarse.at[share_of(t, peer[0]), :], theirs.at[member, slot(t), :],
                b1_s.at[0], b1_r.at[t], peer,
            )

        loop(1, count, spread)
        theirs[member, slot(t), :] = coarse[share_of(t, member), :]

    def answer(t):
        come = theirs.at[pl.ds(0, count - 1), slot(t), :]
        drain(come, b1_r.at[t])

        def compare(i):
            rows = rows_at(starts[t] // count + i * 16, 16)
            values = [theirs[m, rows, :].astype(f32) for m in range(count)]
            totals = [jnp.zeros_like(values[0]) for m in range(count)]
            for m in range(count):
                for o in range(m + 1, count):
                    s = slope(values[m] - values[o])
                    totals[m] = totals[m] + s
                    totals[o] = totals[o] - s
            for m in range(count):
                answers[m, rows, :] = totals[m].astype(bf16)

        loop(0, shares[t] // 16, compare)

        def reply(k):
            peer = m_peer(k)
            send(
                answers.at[peer[0], slot(t), :], pairs.at[share_of(t, member), :],
                b2_s.at[0], b2_r.at[t], peer,
            )

        loop(1, count, reply)
        pairs[share_of(t, member), :] = answers[member, slot(t), :]

    def differentiate(rows):
        a = act[rows, :]
        s = 0.5 * jnp.tanh(0.5 * a) + 0.5
        act[rows, :] = s * (1.0 + a * (1.0 - s))

    early = max(tiles - 2, 1)
    for t in range(early):
        forward(t)
    truth_pad[...] = jnp.zeros_like(truth_pad)
    truth_pad[0:levels, :] = truth[...]
    truth_t[...] = truth_pad[...].T
    latitude = math.pi * ((lat[...].astype(f32) + 0.5) / LATS - 0.5)
    area = LOSS_SCALE * jnp.cos(latitude)
    strip = lat.shape[1]
    for i in range(lat.shape[0]):
        area_t[i * strip:(i + 1) * strip, :] = jnp.broadcast_to(area[i:i + 1, :], (LANES, strip)).T
    for t in range(early, tiles):
        if t == ahead:
            own_half(t)
        forward(t)
        answer(t - early)

    left = turns - turns // 2
    done = 0

    def prepare(t):
        by_rows(starts[t], starts[t] + sizes[t], differentiate)

    for t in range(tiles - early, tiles):
        prepare(t - (tiles - early))
        loop(turns // 2 + done * left // early, turns // 2 + (done + 1) * left // early, turn)
        done += 1
        answer(t)
    for t in range(early, tiles):
        prepare(t)

    fair = (1.0 - (1.0 - ALPHA) / count) / (count * (count - 1))

    def backward(t):
        drain(pairs.at[pl.ds(0, sizes[t] - shares[t]), :], b2_r.at[t])
        rows = pl.ds(starts[t], sizes[t])
        grad_fields = area_t[rows, :] * (
            slope(fields[rows, :] - truth_t[rows, :]) * (1.0 / count)
            - fair * pairs[rows, :].astype(f32)
        )
        grad_act = jnp.dot(grad_fields.astype(bf16), wo_pad[...], preferred_element_type=f32)
        gp[rows, :] = (grad_act * act[rows, :]).astype(bf16)

    depth = width // n

    def nth(i, own):
        first = jnp.where(i == 0, (own + 2) % n, own + 1 - 2 * (own % 2))
        return jnp.where(i < 2, first, jnp.where(i == 2, n - 1 - own, own))

    def product(which, i):
        plane, cols = (nth(i, p), mine) if which else (nth(i, q), other)
        return jnp.dot(
            planes[core if which else 1 - core, plane], gp[:, cols], preferred_element_type=f32
        )

    for t in range(tiles):
        backward(t)

    def other_plane(i):
        part = product(0, i)
        csend[i] = part.astype(bf16)
        send(csend.at[i], crecv.at[i], c0_s.at[0], c0_r.at[i], partner)

    loop(0, n, other_plane)

    halves = [slice(0, quarter), slice(quarter, half)]

    def to_side(slot, target):
        send(send1.at[slot], recv1.at[slot], c1_s.at[0], c1_r.at[slot], p_peers[target])

    def own_plane(i):
        part = product(1, i)
        drain(crecv.at[i], c0_r.at[i])
        total = part + crecv[i].astype(f32)
        sums[i] = total

        @pl.when(i == 0)
        def _():
            for side in range(2):
                send1[side] = total[:, halves[side]].astype(bf16)
                to_side(side, side)

        for side in range(2):
            @pl.when(i == 1 + side)
            def _():
                send1[2 + side] = total[:, halves[side]].astype(bf16)
                to_side(2 + side, side)

    loop(0, n, own_plane)
    for side in range(2):
        drain(recv1.at[side], c1_r.at[side])
        term = sums[2 - side, :, halves[side]] + recv1[side].astype(f32)
        send1[4 + side] = term.astype(bf16)
        to_side(4 + side, 1 - side)

    def grad_normed(x_):
        cols = rows_at(x_ * depth, depth)
        act[:, cols] = lax.dot_general(
            gp[...], w_full[x_].reshape(depth, width), (((1,), (1,)), ((), ())),
            preferred_element_type=f32,
        )

    def hidden_grad(rows):
        scaled = act[rows, :] * gain[...]
        inverse = inv_root[rows, 0:1]
        unit = hid[rows, :].astype(f32) * inverse
        inner = jnp.mean(scaled * unit, axis=-1, keepdims=True)
        gh[rows, :] = ((scaled - unit * inner) * inverse).astype(bf16)

    loop(0, n // 2, grad_normed)
    for slot in range(2, 6):
        drain(recv1.at[slot], c1_r.at[slot])
    line_rows = nh * block

    def add_planes(q_):
        rows = rows_at(q_ * line_rows, line_rows)
        both = [
            sums[n - 1, rows, halves[i]] + recv1[2 + i, rows, :].astype(f32)
            + recv1[4 + i, rows, :].astype(f32)
            for i in range(2)
        ]
        return jnp.concatenate(both, axis=1)

    def to_first(j):
        k = ordered(n - j)
        send2[j - 1] = add_planes((q + k) % n).astype(bf16)
        send(send2.at[j - 1], recv2.at[j - 1], c2_s.at[0], c2_r.at[0], q_peer(k))

    loop(1, n, to_first)
    total = add_planes(q)
    loop(n // 2, n, grad_normed)
    drain(recv2, c2_r.at[0])
    for i in range(n - 1):
        total = total + recv2[i].astype(f32)
    strip = half // chips
    for h_ in range(nh):
        for l_ in range(chips):
            send3[h_, l_] = total[
                h_ * block:(h_ + 1) * block, l_ * strip:(l_ + 1) * strip
            ].astype(bf16)
    loop(1, nh * chips, lambda i: send(
        send3.at[(h + i // chips) % nh, (low + i % chips) % chips], recv3.at[i - 1],
        c3_s.at[0], c3_r.at[0], z_peer(i),
    ))
    by_rows(0, points // 2, hidden_grad)
    drain(recv3, c3_r.at[0])
    total = send3[h, low].astype(f32)
    for i in range(nh * chips - 1):
        total = total + recv3[i].astype(f32)
    factor = 1.0 / math.sqrt(count * points * nx * nh * ny)
    finals[core * chips + low] = (total * factor).astype(bf16)
    own_final = finals.at[core * chips + low]
    loop(1, count, lambda k: send(own_final, own_final, c4_s.at[0], c4_r.at[0], m_peer(k)))
    by_rows(points // 2, points, hidden_grad)
    others = finals.at[pl.ds(0, count - 1)]
    drain(others, c4_r.at[0])
    for i in range(count):
        gw_ref[:, i * strip:(i + 1) * strip] = finals[i].astype(f32)

    if chips == 1:
        drain(z_blocks, a1_s.at[0])
    else:
        from_end(lambda toward, start: [drain(z_blocks, a1_s.at[0]) for _ in range(2)])
    drain(w_full.at[pl.ds(0, n - 1), :, 0, :, mine], a2_s.at[0])
    drain(w_full.at[:, :, pl.ds(0, 3), :, mine], a3_s.at[0])
    drain(w_full.at[:, :, :, :, mine], a4_s.at[0])
    drain(coarse.at[pl.ds(0, points - points // count), :], b1_s.at[0])
    drain(coarse.at[pl.ds(0, points - points // count), :], b2_s.at[0])
    drain(csend, c0_s.at[0])
    drain(send1, c1_s.at[0])
    drain(send2, c2_s.at[0])
    drain(recv3, c3_s.at[0])
    drain(others, c4_s.at[0])


def hand_over(*arrays):
    pieces = 4

    def body(*refs):
        sources, targets, sems = refs[:len(arrays)], refs[len(arrays):-1], refs[-1]
        copies = []
        for source, target in zip(sources, targets):
            rows = source.shape[0]
            parts = pieces if rows % (16 * pieces) == 0 else 1
            for i in range(parts):
                part = pl.ds(i * (rows // parts), rows // parts)
                copies.append(
                    pltpu.make_async_copy(source.at[part], target.at[part], sems.at[len(copies)])
                )
        for copy in copies:
            copy.start()
        for copy in copies:
            copy.wait()

    anywhere = pl.BlockSpec(memory_space=pl.ANY)
    return pl.pallas_call(
        body,
        out_shape=tuple(jax.ShapeDtypeStruct(a.shape, a.dtype) for a in arrays),
        in_specs=[anywhere] * len(arrays),
        out_specs=(anywhere,) * len(arrays),
        scratch_shapes=[pltpu.SemaphoreType.DMA((pieces * len(arrays),))],
        compiler_params=pltpu.CompilerParams(vmem_limit_bytes=1024 * 1024),
        name="hand_over",
    )(*arrays)


def per_device(hidden, truth, lat_row, gain, w_in, w_out):
    nx, nh, ny = GRID
    count = lax.axis_size("member")
    _, points, width = hidden.shape
    levels = truth.shape[0]
    block = w_in.shape[0]
    half = width // 2
    sizes = TILES if sum(TILES) == points else (points,)
    tiles = len(sizes)
    f32, bf16 = jnp.float32, jnp.bfloat16
    vmem, dma = pltpu.VMEM, pltpu.SemaphoreType.DMA
    n, chips, lat_strip = nx, count // 2, min(LANES, points)
    scratch = [
        vmem((points, width), bf16),
        vmem((levels, points), f32),
        vmem((points // lat_strip, lat_strip), jnp.int32),
        vmem((1, width), f32),
        vmem((levels, width), bf16),
        vmem((nx, nh, ny, block, width), bf16),
        vmem((points, width), bf16),
        vmem((2, n, width // n, points), bf16),
        vmem((points, LANES), f32),
        vmem((LANES, width), bf16),
        vmem((width, LANES), bf16),
        vmem((points, width), bf16),
        vmem((LANES, points), f32),
        vmem((points, LANES), f32),
        vmem((points, LANES), f32),
        vmem((points, width), f32),
        vmem((points, LANES), f32),
        vmem((points, LANES), bf16),
        vmem((count, points // count, LANES), bf16),
        vmem((count, points // count, LANES), bf16),
        vmem((points, LANES), bf16),
        vmem((points, width), bf16),
        vmem((n, width // n, half), bf16),
        vmem((n, width // n, half), bf16),
        vmem((n, width // n, half), f32),
        vmem((6, width // n, half // 2), bf16),
        vmem((6, width // n, half // 2), bf16),
        vmem((n - 1, nh * block, half), bf16),
        vmem((n - 1, nh * block, half), bf16),
        vmem((nh, chips, block, half // chips), bf16),
        vmem((nh * chips - 1, block, half // chips), bf16),
        vmem((count, block, half // chips), bf16),
        dma((6,)),
    ]
    for arrivals in (
        (1,), (n - 1,), (n, 4), (1,),
        (tiles,), (tiles,),
        (n,), (6,), (1,), (1,), (1,),
    ):
        scratch += [dma((1,)), dma(arrivals)]
    grad_rows, grad_first = pl.pallas_call(
        functools.partial(kernel, sizes),
        out_shape=(
            vmem((points, width), bf16),
            vmem((block, width), f32),
        ),
        in_specs=[pl.BlockSpec(memory_space=pltpu.HBM)] * 6,
        out_specs=(pl.BlockSpec(memory_space=vmem),) * 2,
        scratch_shapes=scratch,
        compiler_params=pltpu.CompilerParams(
            collective_id=0, has_side_effects=True, vmem_limit_bytes=57 * 1024 * 1024
        ),
        name="crps_step",
    )(
        hidden[0], truth, lat_row.reshape(points // lat_strip, lat_strip), gain[None], w_in, w_out
    )
    grad_rows, grad_first = hand_over(grad_rows, grad_first)
    return (grad_rows[None], grad_first)


def solution(mesh):
    in_specs = (
        P("member", "space", None),
        P(None, "space"),
        P("space"),
        P(),
        P("space", None),
        P(),
    )
    out_specs = (P("member", "space", None), P("space", None))
    return jax.shard_map(
        per_device, mesh=mesh, in_specs=in_specs, out_specs=out_specs, check_vma=False
    )
```

```python
import functools
import math

import jax
import jax.numpy as jnp
from jax import lax
from jax.experimental import pallas as pl
from jax.experimental.pallas import tpu as pltpu
from jax.sharding import PartitionSpec as P

LATS = 721
ALPHA = 0.95
SMOOTH = 0.1
LOSS_SCALE = 64.0
EPSILON = 1e-05

GRID = (4, 4, 4)
LANES = 128
TILE = 256
MESH = pl.DeviceIdType.MESH


def slope(diff):
    return diff * lax.rsqrt(diff * diff + SMOOTH * SMOOTH)


def rows_at(start, size):
    return pl.ds(pl.multiple_of(start, size), size)


def kernel(
    tile,
    hid_hbm, truth_hbm, lat_hbm, gain_hbm, w_hbm, wo_hbm,
    gh, gw_ref,
    hid, truth, lat, gain, wo_raw, w_full, normed, planes, inv_root, wo_pad, wo_t, hidden_act,
    truth_pad, truth_t, area_t, act, fields, coarse, theirs, answers, pairs, gp,
    csend, crecv, sums, send1, recv1, send2, recv2, send3, recv3, finals,
    local_sem, a1_s, a1_r, a2_s, a2_r, a3_s, a3_r, a4_s, a4_r,
    b1_s, b1_r, b2_s, b2_r, c0_s, c0_r, c1_s, c1_r, c2_s, c2_r, c3_s, c3_r, c4_s, c4_r,
):
    nx, nh, ny = GRID
    n = nx
    points, width = hid.shape
    half = width // 2
    quarter = half // 2
    depth = width // n
    levels = truth.shape[0]
    count = finals.shape[0]
    chips = count // 2
    block = w_full.shape[3]
    tiles, share = theirs.shape[0], theirs.shape[2]
    f32, bf16 = jnp.float32, jnp.bfloat16

    member, space = lax.axis_index("member"), lax.axis_index("space")
    core, low = member % 2, member // 2
    x, h, y = space // (nh * ny), (space // ny) % nh, space % ny
    q, p = x * (1 - core) + y * core, y * (1 - core) + x * core
    mine = pl.ds(pl.multiple_of(core * half, half), half)
    other = pl.ds(pl.multiple_of((1 - core) * half, half), half)
    quarters = [
        pl.ds(pl.multiple_of(core * half + i * quarter, quarter), quarter) for i in range(2)
    ]

    def place(p_, q_):
        return q_ * (1 - core) + p_ * core, p_ * (1 - core) + q_ * core

    def at(p_, q_, h_):
        x_, y_ = place(p_, q_)
        return (member, (x_ * nh + h_) * ny + y_)

    def h_peer(k):
        return at(p, q, (h + k) % nh)

    def q_peer(k):
        return at(p, (q + k) % n, h)

    def m_peer(k):
        return ((member + k) % count, space)

    def z_peer(i):
        dh, dl = i // chips, i % chips
        return (2 * ((low + dl) % chips) + core, (x * nh + (h + dh) % nh) * ny + y)

    sides = [p + 1 - 2 * (p % 2), n - 1 - p]
    far = (p + 2) % n
    p_peers = [at(v, q, h) for v in sides]
    partner = (member + 1 - 2 * core, space)

    def send(src, dst, send_sem, recv_sem, target):
        pltpu.make_async_remote_copy(
            src_ref=src, dst_ref=dst, send_sem=send_sem, recv_sem=recv_sem,
            device_id=target, device_id_type=MESH,
        ).start()

    def drain(ref, sem):
        pltpu.make_async_copy(ref, ref, sem).wait()

    def loop(first, last, body):
        def step(i, carry):
            body(i)
            return carry

        lax.fori_loop(first, last, step, 0)

    def by_rows(first, last, body):
        chunks = math.gcd(4, (last - first) // 16)

        def step(i):
            for u in range(chunks):
                body(rows_at(first + (i * chunks + u) * 16, 16))

        loop(0, (last - first) // (16 * chunks), step)

    barrier = pltpu.get_barrier_semaphore()

    def greet(peer):
        pl.semaphore_signal(barrier, inc=1, device_id=peer, device_id_type=MESH)

    loop(chips, nh * chips, lambda i: greet(z_peer(i)))
    loop(1, n, lambda k: greet(q_peer(k)))
    for peer in p_peers:
        greet(peer)
    loop(1, count, lambda k: greet(m_peer(k)))

    own_w = pltpu.make_async_copy(w_hbm.at[:, mine], w_full.at[x, h, y, :, mine], local_sem.at[0])
    loads = [
        pltpu.make_async_copy(source, target, local_sem.at[1 + i])
        for i, (source, target) in enumerate(
            [(hid_hbm, hid), (gain_hbm, gain), (truth_hbm, truth), (lat_hbm, lat), (wo_hbm, wo_raw)]
        )
    ]
    for load in loads[:2]:
        load.start()
    pl.semaphore_wait(barrier, nh * chips - chips + n - 1 + 2 + count - 1)

    own_block = w_full.at[x, h, y, :, mine]
    def to_z(dh, l_):
        target = (2 * l_ + core, (x * nh + (h + dh) % nh) * ny + y)
        send(w_hbm.at[:, mine], own_block, a1_s.at[0], a1_r.at[0], target)

    ends = ((chips - 1, 1, 0), (0, nh - 1, chips // 2))

    def from_end(action):
        for end, toward, start in ends:
            @pl.when(low == end)
            def _():
                action(toward, start)

    def spread_z(toward, start):
        loop(0, chips, lambda l_: to_z(toward, l_))
        loop(start, start + chips // 2, lambda l_: to_z(2, l_))

    if chips == 1:
        loop(1, nh, lambda k: to_z(k, 0))
    else:
        from_end(spread_z)
    own_w.start()
    for load in loads[2:]:
        load.start()
    loads[0].wait()
    loads[1].wait()

    def normalise(rows):
        values = hid[rows, :].astype(f32)
        root = jnp.sqrt(jnp.mean(values * values, axis=-1, keepdims=True) + EPSILON)
        inverse = 1.0 / root
        inv_root[rows, :] = jnp.broadcast_to(inverse, (16, LANES))
        normed[rows, :] = (values * inverse * gain[...]).astype(bf16)

    by_rows(0, points, normalise)
    for load in loads[2:]:
        load.wait()
    wo_pad[...] = jnp.zeros_like(wo_pad)
    wo_pad[0:levels, :] = wo_raw[...]
    wo_t[...] = wo_pad[...].T

    span = min(LANES, points)
    turns = points // span

    def rank(v, own):
        near = jnp.where(v == own + 1 - 2 * (own % 2), 1, 2)
        return jnp.where(v == own, 3, jnp.where(v == (own + 2) % n, 0, near))

    ranks = [
        [(core, rank(v, y)) for v in range(ny)], [(1 - core, rank(v, x)) for v in range(nx)]
    ]

    def turn(i):
        cols = rows_at(i * span, span)
        turned = normed[cols, :].T
        for x_ in range(nx):
            for h_ in range(nh):
                for y_ in range(ny):
                    first = ((x_ * nh + h_) * ny + y_) * block
                    piece = turned[first:first + block, :]
                    to_x, to_y = (x_ * nh + h_) * block, (y_ * nh + h_) * block
                    for (which, r), first in ((ranks[0][y_], to_x), (ranks[1][x_], to_y)):
                        start = pl.multiple_of(r * depth + first, block)
                        planes[which, pl.ds(start, block), cols] = piece

    loop(0, turns // 2, turn)
    own_w.wait()
    z_blocks = w_full.at[0, 0, pl.ds(0, nh - 1), :, mine]
    drain(z_blocks, a1_r.at[0])

    def group(p_, b, cols=mine):
        x_, y_ = place(p_, (q - b + n) % n)
        return w_full.at[x_, :, y_, :, cols]

    def to_partner(p_, b):
        part = group(p_, b)
        send(part, part, a4_s.at[0], a4_r.at[0], partner)

    def to_second(b):
        part = group(p, b)
        for i in range(2):
            send(part, part, a3_s.at[0], a3_r.at[b, i], p_peers[i])
        to_partner(p, b)

    def ordered(j):
        return j + (j // 2) * (n + 1 - 2 * j)

    own_group = group(p, 0)
    loop(1, n, lambda j: send(
        own_group, own_group, a2_s.at[0], a2_r.at[ordered(j) - 1], q_peer(ordered(j))
    ))
    to_second(0)
    def pass_first(j):
        b = ordered(j)
        drain(own_group, a2_r.at[b - 1])
        to_second(b)


    def pass_second(j):
        b = ordered(j)
        for i in range(2):
            drain(own_group, a3_r.at[b, i])
            part = group(sides[i], b, quarters[i])
            send(part, part, a3_s.at[0], a3_r.at[b, 2 + i], p_peers[1 - i])
        for i in range(2):
            to_partner(sides[i], b)

    pass_second(0)
    loop(1, n, pass_first)
    loop(1, n, pass_second)

    def pass_far(j):
        b = ordered(j)
        for i in range(2):
            drain(group(far, b, quarters[i]), a3_r.at[b, 2 + i])
        to_partner(far, b)

    loop(0, n, pass_far)

    def project(rows, cols):
        act[rows, cols] = jnp.dot(
            normed[rows, :], w_full[:, :, :, :, cols].reshape(width, half),
            preferred_element_type=f32,
        )

    def activate(rows, cols):
        a = act[rows, cols]
        hidden_act[rows, cols] = (a * (0.5 * jnp.tanh(0.5 * a) + 0.5)).astype(bf16)

    project(slice(0, points), mine)
    by_rows(0, points, lambda rows: activate(rows, mine))

    drain(w_full.at[:, :, :, :, other], a4_r.at[0])

    def share_of(t, m):
        return rows_at(t * tile + m * share, share)

    def tile_rows(t, body):
        by_rows(0, tile, lambda rows: body(rows_at(t * tile + rows.start, 16)))

    def forward(t):
        rows = rows_at(t * tile, tile)
        project(rows, other)
        tile_rows(t, lambda rows: activate(rows, other))
        field = jnp.dot(hidden_act[rows, :], wo_t[...], preferred_element_type=f32)
        fields[rows, :] = field
        coarse[rows, :] = field.astype(bf16)

        def spread(k):
            peer = m_peer(k)
            send(
                coarse.at[share_of(t, peer[0]), :], theirs.at[t, member],
                b1_s.at[0], b1_r.at[t], peer,
            )

        loop(1, count, spread)
        theirs[t, member] = coarse[share_of(t, member), :]

    def answer(t):
        come = theirs.at[t, pl.ds(0, count - 1)]
        drain(come, b1_r.at[t])

        def compare(i):
            rows = rows_at(i * 16, 16)
            values = [theirs[t, m, rows, :].astype(f32) for m in range(count)]
            totals = [jnp.zeros_like(values[0]) for m in range(count)]
            for m in range(count):
                for o in range(m + 1, count):
                    s = slope(values[m] - values[o])
                    totals[m] = totals[m] + s
                    totals[o] = totals[o] - s
            for m in range(count):
                answers[t, m, rows, :] = totals[m].astype(bf16)

        loop(0, share // 16, compare)

        def reply(k):
            peer = m_peer(k)
            send(
                answers.at[t, peer[0]], pairs.at[share_of(t, member), :],
                b2_s.at[0], b2_r.at[t], peer,
            )

        loop(1, count, reply)
        pairs[share_of(t, member), :] = answers[t, member]


    def differentiate(rows):
        a = act[rows, :]
        s = 0.5 * jnp.tanh(0.5 * a) + 0.5
        act[rows, :] = s * (1.0 + a * (1.0 - s))

    loop(0, max(tiles - 1, 1), forward)
    truth_pad[...] = jnp.zeros_like(truth_pad)
    truth_pad[0:levels, :] = truth[...]
    truth_t[...] = truth_pad[...].T
    latitude = math.pi * ((lat[...].astype(f32) + 0.5) / LATS - 0.5)
    area = LOSS_SCALE * jnp.cos(latitude)
    strip = lat.shape[1]
    for i in range(lat.shape[0]):
        area_t[i * strip:(i + 1) * strip, :] = jnp.broadcast_to(area[i:i + 1, :], (LANES, strip)).T
    if tiles > 1:
        forward(tiles - 1)

    def reply_and_prepare(t):
        answer(t)
        tile_rows(t, differentiate)
        left = turns - turns // 2
        loop(turns // 2 + t * left // tiles, turns // 2 + (t + 1) * left // tiles, turn)

    loop(0, tiles, reply_and_prepare)

    fair = (1.0 - (1.0 - ALPHA) / count) / (count * (count - 1))

    def backward(t):
        come = pairs.at[pl.ds(0, tile - share), :]
        drain(come, b2_r.at[t])
        rows = rows_at(t * tile, tile)
        grad_fields = area_t[rows, :] * (
            slope(fields[rows, :] - truth_t[rows, :]) * (1.0 / count)
            - fair * pairs[rows, :].astype(f32)
        )
        grad_act = jnp.dot(grad_fields.astype(bf16), wo_pad[...], preferred_element_type=f32)
        gp[rows, :] = (grad_act * act[rows, :]).astype(bf16)

    loop(0, tiles, backward)

    def product(which, pair, cols):
        rows = rows_at(pair * 2 * depth, 2 * depth)
        return jnp.dot(planes[which, rows, :], gp[:, cols], preferred_element_type=f32)

    def other_pair(pair):
        part = product(1, pair, other).astype(bf16)
        for u in range(2):
            i = 2 * pair + u
            csend[i] = part[u * depth:(u + 1) * depth, :]
            send(csend.at[i], crecv.at[i], c0_s.at[0], c0_r.at[i], partner)

    loop(0, n // 2, other_pair)

    halves = [slice(0, quarter), slice(quarter, half)]

    def to_side(slot, target):
        send(send1.at[slot], recv1.at[slot], c1_s.at[0], c1_r.at[slot], p_peers[target])

    def own_pair(pair):
        part = product(0, pair, mine)
        for u in range(2):
            i = 2 * pair + u
            drain(crecv.at[i], c0_r.at[i])
            sums[i] = part[u * depth:(u + 1) * depth, :] + crecv[i].astype(f32)

    def to_near(side):
        send1[2 + side] = sums[1 + side, :, halves[side]].astype(bf16)
        to_side(2 + side, side)

    own_pair(0)
    for side in range(2):
        send1[side] = sums[0, :, halves[side]].astype(bf16)
        to_side(side, side)
    to_near(0)
    own_pair(1)
    to_near(1)
    for side in range(2):
        drain(recv1.at[side], c1_r.at[side])
        term = sums[2 - side, :, halves[side]] + recv1[side].astype(f32)
        send1[4 + side] = term.astype(bf16)
        to_side(4 + side, 1 - side)

    def grad_normed(x_):
        cols = rows_at(x_ * depth, depth)
        act[:, cols] = lax.dot_general(
            gp[...], w_full[x_].reshape(depth, width), (((1,), (1,)), ((), ())),
            preferred_element_type=f32,
        )

    def hidden_grad(rows):
        scaled = act[rows, :] * gain[...]
        inverse = inv_root[rows, 0:1]
        unit = hid[rows, :].astype(f32) * inverse
        inner = jnp.mean(scaled * unit, axis=-1, keepdims=True)
        gh[rows, :] = ((scaled - unit * inner) * inverse).astype(bf16)

    loop(0, n // 2, grad_normed)
    for slot in range(2, 6):
        drain(recv1.at[slot], c1_r.at[slot])
    line_rows = nh * block

    def add_planes(q_):
        rows = rows_at(q_ * line_rows, line_rows)
        both = [
            sums[n - 1, rows, halves[i]] + recv1[2 + i, rows, :].astype(f32)
            + recv1[4 + i, rows, :].astype(f32)
            for i in range(2)
        ]
        return jnp.concatenate(both, axis=1)

    def to_first(j):
        k = ordered(n - j)
        send2[j - 1] = add_planes((q + k) % n).astype(bf16)
        send(send2.at[j - 1], recv2.at[j - 1], c2_s.at[0], c2_r.at[0], q_peer(k))

    loop(1, n, to_first)
    total = add_planes(q)
    loop(n // 2, n, grad_normed)
    drain(recv2, c2_r.at[0])
    for i in range(n - 1):
        total = total + recv2[i].astype(f32)
    strip = half // chips
    for h_ in range(nh):
        for l_ in range(chips):
            send3[h_, l_] = total[
                h_ * block:(h_ + 1) * block, l_ * strip:(l_ + 1) * strip
            ].astype(bf16)
    loop(1, nh * chips, lambda i: send(
        send3.at[(h + i // chips) % nh, (low + i % chips) % chips], recv3.at[i - 1],
        c3_s.at[0], c3_r.at[0], z_peer(i),
    ))
    by_rows(0, points // 2, hidden_grad)
    drain(recv3, c3_r.at[0])
    total = send3[h, low].astype(f32)
    for i in range(nh * chips - 1):
        total = total + recv3[i].astype(f32)
    factor = 1.0 / math.sqrt(count * points * nx * nh * ny)
    finals[core * chips + low] = (total * factor).astype(bf16)
    own_final = finals.at[core * chips + low]
    loop(1, count, lambda k: send(own_final, own_final, c4_s.at[0], c4_r.at[0], m_peer(k)))
    by_rows(points // 2, points, hidden_grad)
    others = finals.at[pl.ds(0, count - 1)]
    drain(others, c4_r.at[0])
    for i in range(count):
        gw_ref[:, i * strip:(i + 1) * strip] = finals[i].astype(f32)

    if chips == 1:
        drain(z_blocks, a1_s.at[0])
    else:
        from_end(lambda toward, start: [drain(z_blocks, a1_s.at[0]) for _ in range(2)])
    drain(w_full.at[pl.ds(0, n - 1), :, 0, :, mine], a2_s.at[0])
    drain(w_full.at[:, :, pl.ds(0, 3), :, mine], a3_s.at[0])
    drain(w_full.at[:, :, :, :, mine], a4_s.at[0])
    drain(coarse.at[pl.ds(0, points - points // count), :], b1_s.at[0])
    drain(coarse.at[pl.ds(0, points - points // count), :], b2_s.at[0])
    drain(csend, c0_s.at[0])
    drain(send1, c1_s.at[0])
    drain(send2, c2_s.at[0])
    drain(recv3, c3_s.at[0])
    drain(others, c4_s.at[0])


def hand_over(*arrays):
    pieces = 4

    def body(*refs):
        sources, targets, sems = refs[:len(arrays)], refs[len(arrays):-1], refs[-1]
        copies = []
        for source, target in zip(sources, targets):
            rows = source.shape[0]
            parts = pieces if rows % (16 * pieces) == 0 else 1
            for i in range(parts):
                part = pl.ds(i * (rows // parts), rows // parts)
                copies.append(
                    pltpu.make_async_copy(source.at[part], target.at[part], sems.at[len(copies)])
                )
        for copy in copies:
            copy.start()
        for copy in copies:
            copy.wait()

    anywhere = pl.BlockSpec(memory_space=pl.ANY)
    return pl.pallas_call(
        body,
        out_shape=tuple(jax.ShapeDtypeStruct(a.shape, a.dtype) for a in arrays),
        in_specs=[anywhere] * len(arrays),
        out_specs=(anywhere,) * len(arrays),
        scratch_shapes=[pltpu.SemaphoreType.DMA((pieces * len(arrays),))],
        compiler_params=pltpu.CompilerParams(vmem_limit_bytes=1024 * 1024),
        name="hand_over",
    )(*arrays)


def per_device(hidden, truth, lat_row, gain, w_in, w_out):
    nx, nh, ny = GRID
    count = lax.axis_size("member")
    _, points, width = hidden.shape
    levels = truth.shape[0]
    block = w_in.shape[0]
    half = width // 2
    tile = min(TILE, points)
    tiles, share = points // tile, tile // count
    f32, bf16 = jnp.float32, jnp.bfloat16
    vmem, dma = pltpu.VMEM, pltpu.SemaphoreType.DMA
    n, chips, lat_strip = nx, count // 2, min(LANES, points)
    scratch = [
        vmem((points, width), bf16),
        vmem((levels, points), f32),
        vmem((points // lat_strip, lat_strip), jnp.int32),
        vmem((1, width), f32),
        vmem((levels, width), bf16),
        vmem((nx, nh, ny, block, width), bf16),
        vmem((points, width), bf16),
        vmem((2, width, points), bf16),
        vmem((points, LANES), f32),
        vmem((LANES, width), bf16),
        vmem((width, LANES), bf16),
        vmem((points, width), bf16),
        vmem((LANES, points), f32),
        vmem((points, LANES), f32),
        vmem((points, LANES), f32),
        vmem((points, width), f32),
        vmem((points, LANES), f32),
        vmem((points, LANES), bf16),
        vmem((tiles, count, share, LANES), bf16),
        vmem((tiles, count, share, LANES), bf16),
        vmem((points, LANES), bf16),
        vmem((points, width), bf16),
        vmem((n, width // n, half), bf16),
        vmem((n, width // n, half), bf16),
        vmem((n, width // n, half), f32),
        vmem((6, width // n, half // 2), bf16),
        vmem((6, width // n, half // 2), bf16),
        vmem((n - 1, nh * block, half), bf16),
        vmem((n - 1, nh * block, half), bf16),
        vmem((nh, chips, block, half // chips), bf16),
        vmem((nh * chips - 1, block, half // chips), bf16),
        vmem((count, block, half // chips), bf16),
        dma((6,)),
    ]
    for arrivals in (
        (1,), (n - 1,), (n, 4), (1,),
        (tiles,), (tiles,),
        (n,), (6,), (1,), (1,), (1,),
    ):
        scratch += [dma((1,)), dma(arrivals)]
    grad_rows, grad_first = pl.pallas_call(
        functools.partial(kernel, tile),
        out_shape=(
            vmem((points, width), bf16),
            vmem((block, width), f32),
        ),
        in_specs=[pl.BlockSpec(memory_space=pltpu.HBM)] * 6,
        out_specs=(pl.BlockSpec(memory_space=vmem),) * 2,
        scratch_shapes=scratch,
        compiler_params=pltpu.CompilerParams(
            collective_id=0, has_side_effects=True, vmem_limit_bytes=57 * 1024 * 1024
        ),
        name="crps_step",
    )(
        hidden[0], truth, lat_row.reshape(points // lat_strip, lat_strip), gain[None], w_in, w_out
    )
    grad_rows, grad_first = hand_over(grad_rows, grad_first)
    return (grad_rows[None], grad_first)


def solution(mesh):
    in_specs = (
        P("member", "space", None),
        P(None, "space"),
        P("space"),
        P(),
        P("space", None),
        P(),
    )
    out_specs = (P("member", "space", None), P("space", None))
    return jax.shard_map(
        per_device, mesh=mesh, in_specs=in_specs, out_specs=out_specs, check_vma=False
    )
```

```python
import functools
import math

import jax
import jax.numpy as jnp
from jax import lax
from jax.experimental import pallas as pl
from jax.experimental.pallas import tpu as pltpu
from jax.sharding import PartitionSpec as P

LATS = 721
ALPHA = 0.95
SMOOTH = 0.1
LOSS_SCALE = 64.0
EPSILON = 1e-05

GRID = (4, 4, 4)
LANES = 128
TILE = 256
MESH = pl.DeviceIdType.MESH


def slope(diff):
    return diff * lax.rsqrt(diff * diff + SMOOTH * SMOOTH)


def rows_at(start, size):
    return pl.ds(pl.multiple_of(start, size), size)


def kernel(
    tile,
    hid_hbm, truth_hbm, lat_hbm, gain_hbm, w_hbm, wo_hbm,
    gh, gw_ref,
    hid, truth, lat, gain, wo_raw, w_full, normed, planes, inv_root, wo_pad, wo_t, hidden_act,
    truth_pad, truth_t, area_t, act, fields, coarse, theirs, answers, pairs, gp,
    csend, crecv, sums, send1, recv1, send2, recv2, send3, recv3, finals,
    local_sem, a1_s, a1_r, a2_s, a2_r, a3_s, a3_r, a4_s, a4_r,
    b1_s, b1_r, b2_s, b2_r, c0_s, c0_r, c1_s, c1_r, c2_s, c2_r, c3_s, c3_r, c4_s, c4_r,
):
    nx, nh, ny = GRID
    n = nx
    points, width = hid.shape
    half = width // 2
    quarter = half // 2
    depth = width // n
    levels = truth.shape[0]
    count = finals.shape[0]
    chips = count // 2
    block = w_full.shape[3]
    tiles, share = theirs.shape[0], theirs.shape[2]
    f32, bf16 = jnp.float32, jnp.bfloat16

    member, space = lax.axis_index("member"), lax.axis_index("space")
    core, low = member % 2, member // 2
    x, h, y = space // (nh * ny), (space // ny) % nh, space % ny
    q, p = x * (1 - core) + y * core, y * (1 - core) + x * core
    mine = pl.ds(pl.multiple_of(core * half, half), half)
    other = pl.ds(pl.multiple_of((1 - core) * half, half), half)
    quarters = [
        pl.ds(pl.multiple_of(core * half + i * quarter, quarter), quarter) for i in range(2)
    ]

    def place(p_, q_):
        return q_ * (1 - core) + p_ * core, p_ * (1 - core) + q_ * core

    def at(p_, q_, h_):
        x_, y_ = place(p_, q_)
        return (member, (x_ * nh + h_) * ny + y_)

    def h_peer(k):
        return at(p, q, (h + k) % nh)

    def q_peer(k):
        return at(p, (q + k) % n, h)

    def m_peer(k):
        return ((member + k) % count, space)

    def z_peer(i):
        dh, dl = i // chips, i % chips
        return (2 * ((low + dl) % chips) + core, (x * nh + (h + dh) % nh) * ny + y)

    sides = [p + 1 - 2 * (p % 2), n - 1 - p]
    far = (p + 2) % n
    p_peers = [at(v, q, h) for v in sides]
    partner = (member + 1 - 2 * core, space)
    crossed = [(partner[0], peer[1]) for peer in p_peers]
    crossing = [
        (partner[0], at(p, v, h)[1]) for v in (q + 1 - 2 * (q % 2), n - 1 - q)
    ]

    def send(src, dst, send_sem, recv_sem, target):
        pltpu.make_async_remote_copy(
            src_ref=src, dst_ref=dst, send_sem=send_sem, recv_sem=recv_sem,
            device_id=target, device_id_type=MESH,
        ).start()

    def drain(ref, sem):
        pltpu.make_async_copy(ref, ref, sem).wait()

    def loop(first, last, body):
        def step(i, carry):
            body(i)
            return carry

        lax.fori_loop(first, last, step, 0)

    def by_rows(first, last, body):
        chunks = math.gcd(4, (last - first) // 16)

        def step(i):
            for u in range(chunks):
                body(rows_at(first + (i * chunks + u) * 16, 16))

        loop(0, (last - first) // (16 * chunks), step)

    barrier = pltpu.get_barrier_semaphore()

    def greet(peer):
        pl.semaphore_signal(barrier, inc=1, device_id=peer, device_id_type=MESH)

    loop(chips, nh * chips, lambda i: greet(z_peer(i)))
    loop(1, n, lambda k: greet(q_peer(k)))
    for peer in p_peers + crossing:
        greet(peer)
    loop(1, count, lambda k: greet(m_peer(k)))

    own_w = pltpu.make_async_copy(w_hbm.at[:, mine], w_full.at[x, h, y, :, mine], local_sem.at[0])
    loads = [
        pltpu.make_async_copy(source, target, local_sem.at[1 + i])
        for i, (source, target) in enumerate(
            [(hid_hbm, hid), (gain_hbm, gain), (truth_hbm, truth), (lat_hbm, lat), (wo_hbm, wo_raw)]
        )
    ]
    for load in loads[:2]:
        load.start()
    pl.semaphore_wait(barrier, nh * chips - chips + n - 1 + 4 + count - 1)

    own_block = w_full.at[x, h, y, :, mine]
    def to_z(dh, l_):
        target = (2 * l_ + core, (x * nh + (h + dh) % nh) * ny + y)
        send(w_hbm.at[:, mine], own_block, a1_s.at[0], a1_r.at[0], target)

    ends = ((chips - 1, 1, 0), (0, nh - 1, chips // 2))

    def from_end(action):
        for end, toward, start in ends:
            @pl.when(low == end)
            def _():
                action(toward, start)

    def spread_z(toward, start):
        loop(0, chips, lambda l_: to_z(toward, l_))
        loop(start, start + chips // 2, lambda l_: to_z(2, l_))

    if chips == 1:
        loop(1, nh, lambda k: to_z(k, 0))
    else:
        from_end(spread_z)
    own_w.start()
    for load in loads[2:]:
        load.start()
    loads[0].wait()
    loads[1].wait()

    def normalise(rows):
        values = hid[rows, :].astype(f32)
        root = jnp.sqrt(jnp.mean(values * values, axis=-1, keepdims=True) + EPSILON)
        inverse = 1.0 / root
        inv_root[rows, :] = jnp.broadcast_to(inverse, (16, LANES))
        normed[rows, :] = (values * inverse * gain[...]).astype(bf16)

    by_rows(0, points, normalise)
    for load in loads[2:]:
        load.wait()
    wo_pad[...] = jnp.zeros_like(wo_pad)
    wo_pad[0:levels, :] = wo_raw[...]
    wo_t[...] = wo_pad[...].T

    span = min(LANES, points)
    turns = points // span

    def rank(v, own):
        near = jnp.where(v == own + 1 - 2 * (own % 2), 1, 2)
        return jnp.where(v == own, 3, jnp.where(v == (own + 2) % n, 0, near))

    ranks = [
        [(core, rank(v, y)) for v in range(ny)], [(1 - core, rank(v, x)) for v in range(nx)]
    ]

    def turn(i):
        cols = rows_at(i * span, span)
        turned = normed[cols, :].T
        for x_ in range(nx):
            for h_ in range(nh):
                for y_ in range(ny):
                    first = ((x_ * nh + h_) * ny + y_) * block
                    piece = turned[first:first + block, :]
                    to_x, to_y = (x_ * nh + h_) * block, (y_ * nh + h_) * block
                    for (which, r), first in ((ranks[0][y_], to_x), (ranks[1][x_], to_y)):
                        start = pl.multiple_of(r * depth + first, block)
                        planes[which, pl.ds(start, block), cols] = piece

    loop(0, turns // 2, turn)
    own_w.wait()
    z_blocks = w_full.at[0, 0, pl.ds(0, nh - 1), :, mine]
    drain(z_blocks, a1_r.at[0])

    def group(p_, b, cols=mine):
        x_, y_ = place(p_, (q - b + n) % n)
        return w_full.at[x_, :, y_, :, cols]

    def to_partner(p_, b):
        part = group(p_, b)
        send(part, part, a4_s.at[0], a4_r.at[0], partner)

    def to_second(b):
        part = group(p, b)
        for i in range(2):
            send(part, part, a3_s.at[0], a3_r.at[b, i], p_peers[i])
        to_partner(p, b)

    def ordered(j):
        return j + (j // 2) * (n + 1 - 2 * j)

    own_group = group(p, 0)
    loop(1, n, lambda j: send(
        own_group, own_group, a2_s.at[0], a2_r.at[ordered(j) - 1], q_peer(ordered(j))
    ))
    to_second(0)
    def pass_first(j):
        b = ordered(j)
        drain(own_group, a2_r.at[b - 1])
        to_second(b)


    def pass_second(j):
        b = ordered(j)
        for i in range(2):
            drain(own_group, a3_r.at[b, i])
            part = group(sides[i], b, quarters[i])
            send(part, part, a3_s.at[0], a3_r.at[b, 2 + i], p_peers[1 - i])
            send(part, part, a3_s.at[0], a4_r.at[0], crossed[1 - i])
        for i in range(2):
            to_partner(sides[i], b)

    pass_second(0)
    loop(1, n, pass_first)
    loop(1, n, pass_second)

    def pass_far(j):
        b = ordered(j)
        for i in range(2):
            drain(group(far, b, quarters[i]), a3_r.at[b, 2 + i])

    loop(0, n, pass_far)

    def project(rows, cols):
        act[rows, cols] = jnp.dot(
            normed[rows, :], w_full[:, :, :, :, cols].reshape(width, half),
            preferred_element_type=f32,
        )

    def activate(rows, cols):
        a = act[rows, cols]
        hidden_act[rows, cols] = (a * (0.5 * jnp.tanh(0.5 * a) + 0.5)).astype(bf16)

    project(slice(0, points), mine)
    by_rows(0, points, lambda rows: activate(rows, mine))

    drain(w_full.at[:, :, :, :, other], a4_r.at[0])

    def share_of(t, m):
        return rows_at(t * tile + m * share, share)

    def tile_rows(t, body):
        by_rows(0, tile, lambda rows: body(rows_at(t * tile + rows.start, 16)))

    def forward(t):
        rows = rows_at(t * tile, tile)
        project(rows, other)
        tile_rows(t, lambda rows: activate(rows, other))
        field = jnp.dot(hidden_act[rows, :], wo_t[...], preferred_element_type=f32)
        fields[rows, :] = field
        coarse[rows, :] = field.astype(bf16)

        def spread(k):
            peer = m_peer(k)
            send(
                coarse.at[share_of(t, peer[0]), :], theirs.at[t, member],
                b1_s.at[0], b1_r.at[t], peer,
            )

        loop(1, count, spread)
        theirs[t, member] = coarse[share_of(t, member), :]

    def answer(t):
        come = theirs.at[t, pl.ds(0, count - 1)]
        drain(come, b1_r.at[t])

        def compare(i):
            rows = rows_at(i * 16, 16)
            values = [theirs[t, m, rows, :].astype(f32) for m in range(count)]
            totals = [jnp.zeros_like(values[0]) for m in range(count)]
            for m in range(count):
                for o in range(m + 1, count):
                    s = slope(values[m] - values[o])
                    totals[m] = totals[m] + s
                    totals[o] = totals[o] - s
            for m in range(count):
                answers[t, m, rows, :] = totals[m].astype(bf16)

        loop(0, share // 16, compare)

        def reply(k):
            peer = m_peer(k)
            send(
                answers.at[t, peer[0]], pairs.at[share_of(t, member), :],
                b2_s.at[0], b2_r.at[t], peer,
            )

        loop(1, count, reply)
        pairs[share_of(t, member), :] = answers[t, member]


    def differentiate(rows):
        a = act[rows, :]
        s = 0.5 * jnp.tanh(0.5 * a) + 0.5
        act[rows, :] = s * (1.0 + a * (1.0 - s))

    loop(0, max(tiles - 1, 1), forward)
    truth_pad[...] = jnp.zeros_like(truth_pad)
    truth_pad[0:levels, :] = truth[...]
    truth_t[...] = truth_pad[...].T
    latitude = math.pi * ((lat[...].astype(f32) + 0.5) / LATS - 0.5)
    area = LOSS_SCALE * jnp.cos(latitude)
    strip = lat.shape[1]
    for i in range(lat.shape[0]):
        area_t[i * strip:(i + 1) * strip, :] = jnp.broadcast_to(area[i:i + 1, :], (LANES, strip)).T
    if tiles > 1:
        forward(tiles - 1)

    def reply_and_prepare(t):
        answer(t)
        tile_rows(t, differentiate)
        left = turns - turns // 2
        loop(turns // 2 + t * left // tiles, turns // 2 + (t + 1) * left // tiles, turn)

    loop(0, tiles, reply_and_prepare)

    fair = (1.0 - (1.0 - ALPHA) / count) / (count * (count - 1))

    def backward(t):
        come = pairs.at[pl.ds(0, tile - share), :]
        drain(come, b2_r.at[t])
        rows = rows_at(t * tile, tile)
        grad_fields = area_t[rows, :] * (
            slope(fields[rows, :] - truth_t[rows, :]) * (1.0 / count)
            - fair * pairs[rows, :].astype(f32)
        )
        grad_act = jnp.dot(grad_fields.astype(bf16), wo_pad[...], preferred_element_type=f32)
        gp[rows, :] = (grad_act * act[rows, :]).astype(bf16)

    loop(0, tiles, backward)

    def product(which, pair, cols):
        rows = rows_at(pair * 2 * depth, 2 * depth)
        return jnp.dot(planes[which, rows, :], gp[:, cols], preferred_element_type=f32)

    def other_pair(pair):
        part = product(1, pair, other).astype(bf16)
        for u in range(2):
            i = 2 * pair + u
            csend[i] = part[u * depth:(u + 1) * depth, :]
            send(csend.at[i], crecv.at[i], c0_s.at[0], c0_r.at[i], partner)

    loop(0, n // 2, other_pair)

    halves = [slice(0, quarter), slice(quarter, half)]

    def to_side(slot, target):
        send(send1.at[slot], recv1.at[slot], c1_s.at[0], c1_r.at[slot], p_peers[target])

    def own_pair(pair):
        part = product(0, pair, mine)
        for u in range(2):
            i = 2 * pair + u
            drain(crecv.at[i], c0_r.at[i])
            sums[i] = part[u * depth:(u + 1) * depth, :] + crecv[i].astype(f32)

    def to_near(side):
        send1[2 + side] = sums[1 + side, :, halves[side]].astype(bf16)
        to_side(2 + side, side)

    own_pair(0)
    for side in range(2):
        send1[side] = sums[0, :, halves[side]].astype(bf16)
        to_side(side, side)
    to_near(0)
    own_pair(1)
    to_near(1)
    for side in range(2):
        drain(recv1.at[side], c1_r.at[side])
        term = sums[2 - side, :, halves[side]] + recv1[side].astype(f32)
        send1[4 + side] = term.astype(bf16)
        to_side(4 + side, 1 - side)

    def grad_normed(x_):
        cols = rows_at(x_ * depth, depth)
        act[:, cols] = lax.dot_general(
            gp[...], w_full[x_].reshape(depth, width), (((1,), (1,)), ((), ())),
            preferred_element_type=f32,
        )

    def hidden_grad(rows):
        scaled = act[rows, :] * gain[...]
        inverse = inv_root[rows, 0:1]
        unit = hid[rows, :].astype(f32) * inverse
        inner = jnp.mean(scaled * unit, axis=-1, keepdims=True)
        gh[rows, :] = ((scaled - unit * inner) * inverse).astype(bf16)

    loop(0, n // 2, grad_normed)
    for slot in range(2, 6):
        drain(recv1.at[slot], c1_r.at[slot])
    line_rows = nh * block

    def add_planes(q_):
        rows = rows_at(q_ * line_rows, line_rows)
        both = [
            sums[n - 1, rows, halves[i]] + recv1[2 + i, rows, :].astype(f32)
            + recv1[4 + i, rows, :].astype(f32)
            for i in range(2)
        ]
        return jnp.concatenate(both, axis=1)

    def to_first(j):
        k = ordered(n - j)
        send2[j - 1] = add_planes((q + k) % n).astype(bf16)
        send(send2.at[j - 1], recv2.at[j - 1], c2_s.at[0], c2_r.at[0], q_peer(k))

    loop(1, n, to_first)
    total = add_planes(q)
    loop(n // 2, n, grad_normed)
    drain(recv2, c2_r.at[0])
    for i in range(n - 1):
        total = total + recv2[i].astype(f32)
    strip = half // chips
    for h_ in range(nh):
        for l_ in range(chips):
            send3[h_, l_] = total[
                h_ * block:(h_ + 1) * block, l_ * strip:(l_ + 1) * strip
            ].astype(bf16)
    loop(1, nh * chips, lambda i: send(
        send3.at[(h + i // chips) % nh, (low + i % chips) % chips], recv3.at[i - 1],
        c3_s.at[0], c3_r.at[0], z_peer(i),
    ))
    by_rows(0, points // 2, hidden_grad)
    drain(recv3, c3_r.at[0])
    total = send3[h, low].astype(f32)
    for i in range(nh * chips - 1):
        total = total + recv3[i].astype(f32)
    factor = 1.0 / math.sqrt(count * points * nx * nh * ny)
    finals[core * chips + low] = (total * factor).astype(bf16)
    own_final = finals.at[core * chips + low]
    loop(1, count, lambda k: send(own_final, own_final, c4_s.at[0], c4_r.at[0], m_peer(k)))
    by_rows(points // 2, points, hidden_grad)
    others = finals.at[pl.ds(0, count - 1)]
    drain(others, c4_r.at[0])
    for i in range(count):
        gw_ref[:, i * strip:(i + 1) * strip] = finals[i].astype(f32)

    if chips == 1:
        drain(z_blocks, a1_s.at[0])
    else:
        from_end(lambda toward, start: [drain(z_blocks, a1_s.at[0]) for _ in range(2)])
    drain(w_full.at[pl.ds(0, n - 1), :, 0, :, mine], a2_s.at[0])
    drain(w_full.at[:, :, :, :, mine], a3_s.at[0])
    drain(w_full.at[:, :, pl.ds(0, 3), :, mine], a4_s.at[0])
    drain(coarse.at[pl.ds(0, points - points // count), :], b1_s.at[0])
    drain(coarse.at[pl.ds(0, points - points // count), :], b2_s.at[0])
    drain(csend, c0_s.at[0])
    drain(send1, c1_s.at[0])
    drain(send2, c2_s.at[0])
    drain(recv3, c3_s.at[0])
    drain(others, c4_s.at[0])


def hand_over(*arrays):
    pieces = 4

    def body(*refs):
        sources, targets, sems = refs[:len(arrays)], refs[len(arrays):-1], refs[-1]
        copies = []
        for source, target in zip(sources, targets):
            rows = source.shape[0]
            parts = pieces if rows % (16 * pieces) == 0 else 1
            for i in range(parts):
                part = pl.ds(i * (rows // parts), rows // parts)
                copies.append(
                    pltpu.make_async_copy(source.at[part], target.at[part], sems.at[len(copies)])
                )
        for copy in copies:
            copy.start()
        for copy in copies:
            copy.wait()

    anywhere = pl.BlockSpec(memory_space=pl.ANY)
    return pl.pallas_call(
        body,
        out_shape=tuple(jax.ShapeDtypeStruct(a.shape, a.dtype) for a in arrays),
        in_specs=[anywhere] * len(arrays),
        out_specs=(anywhere,) * len(arrays),
        scratch_shapes=[pltpu.SemaphoreType.DMA((pieces * len(arrays),))],
        compiler_params=pltpu.CompilerParams(vmem_limit_bytes=1024 * 1024),
        name="hand_over",
    )(*arrays)


def per_device(hidden, truth, lat_row, gain, w_in, w_out):
    nx, nh, ny = GRID
    count = lax.axis_size("member")
    _, points, width = hidden.shape
    levels = truth.shape[0]
    block = w_in.shape[0]
    half = width // 2
    tile = min(TILE, points)
    tiles, share = points // tile, tile // count
    f32, bf16 = jnp.float32, jnp.bfloat16
    vmem, dma = pltpu.VMEM, pltpu.SemaphoreType.DMA
    n, chips, lat_strip = nx, count // 2, min(LANES, points)
    scratch = [
        vmem((points, width), bf16),
        vmem((levels, points), f32),
        vmem((points // lat_strip, lat_strip), jnp.int32),
        vmem((1, width), f32),
        vmem((levels, width), bf16),
        vmem((nx, nh, ny, block, width), bf16),
        vmem((points, width), bf16),
        vmem((2, width, points), bf16),
        vmem((points, LANES), f32),
        vmem((LANES, width), bf16),
        vmem((width, LANES), bf16),
        vmem((points, width), bf16),
        vmem((LANES, points), f32),
        vmem((points, LANES), f32),
        vmem((points, LANES), f32),
        vmem((points, width), f32),
        vmem((points, LANES), f32),
        vmem((points, LANES), bf16),
        vmem((tiles, count, share, LANES), bf16),
        vmem((tiles, count, share, LANES), bf16),
        vmem((points, LANES), bf16),
        vmem((points, width), bf16),
        vmem((n, width // n, half), bf16),
        vmem((n, width // n, half), bf16),
        vmem((n, width // n, half), f32),
        vmem((6, width // n, half // 2), bf16),
        vmem((6, width // n, half // 2), bf16),
        vmem((n - 1, nh * block, half), bf16),
        vmem((n - 1, nh * block, half), bf16),
        vmem((nh, chips, block, half // chips), bf16),
        vmem((nh * chips - 1, block, half // chips), bf16),
        vmem((count, block, half // chips), bf16),
        dma((6,)),
    ]
    for arrivals in (
        (1,), (n - 1,), (n, 4), (1,),
        (tiles,), (tiles,),
        (n,), (6,), (1,), (1,), (1,),
    ):
        scratch += [dma((1,)), dma(arrivals)]
    grad_rows, grad_first = pl.pallas_call(
        functools.partial(kernel, tile),
        out_shape=(
            vmem((points, width), bf16),
            vmem((block, width), f32),
        ),
        in_specs=[pl.BlockSpec(memory_space=pltpu.HBM)] * 6,
        out_specs=(pl.BlockSpec(memory_space=vmem),) * 2,
        scratch_shapes=scratch,
        compiler_params=pltpu.CompilerParams(
            collective_id=0, has_side_effects=True, vmem_limit_bytes=57 * 1024 * 1024
        ),
        name="crps_step",
    )(
        hidden[0], truth, lat_row.reshape(points // lat_strip, lat_strip), gain[None], w_in, w_out
    )
    grad_rows, grad_first = hand_over(grad_rows, grad_first)
    return (grad_rows[None], grad_first)


def solution(mesh):
    in_specs = (
        P("member", "space", None),
        P(None, "space"),
        P("space"),
        P(),
        P("space", None),
        P(),
    )
    out_specs = (P("member", "space", None), P("space", None))
    return jax.shard_map(
        per_device, mesh=mesh, in_specs=in_specs, out_specs=out_specs, check_vma=False
    )
```

```python
import functools
import math

import jax
import jax.numpy as jnp
from jax import lax
from jax.experimental import pallas as pl
from jax.experimental.pallas import tpu as pltpu
from jax.sharding import PartitionSpec as P

LATS = 721
ALPHA = 0.95
SMOOTH = 0.1
LOSS_SCALE = 64.0
EPSILON = 1e-05

GRID = (4, 4, 4)
LANES = 128
TILE = 256
MESH = pl.DeviceIdType.MESH


def slope(diff):
    return diff * lax.rsqrt(diff * diff + SMOOTH * SMOOTH)


def rows_at(start, size):
    return pl.ds(pl.multiple_of(start, size), size)


def kernel(
    tile,
    hid_hbm, truth_hbm, lat_hbm, gain_hbm, w_hbm, wo_hbm,
    gh, gw_ref,
    hid, truth, lat, gain, wo_raw, w_full, normed, planes, inv_root, wo_pad, wo_t, hidden_act,
    truth_pad, truth_t, area_t, act, fields, coarse, theirs, answers, pairs, gp,
    csend, crecv, sums, send1, recv1, send2, recv2, send3, recv3, finals,
    local_sem, a1_s, a1_r, a2_s, a2_r, a3_s, a3_r, a4_s, a4_r,
    b1_s, b1_r, b2_s, b2_r, c0_s, c0_r, c1_s, c1_r, c2_s, c2_r, c3_s, c3_r, c4_s, c4_r,
):
    nx, nh, ny = GRID
    n = nx
    points, width = hid.shape
    half = width // 2
    quarter = half // 2
    depth = width // n
    levels = truth.shape[0]
    count = finals.shape[0]
    chips = count // 2
    block = w_full.shape[3]
    tiles, share = theirs.shape[0], theirs.shape[2]
    f32, bf16 = jnp.float32, jnp.bfloat16

    member, space = lax.axis_index("member"), lax.axis_index("space")
    core, low = member % 2, member // 2
    x, h, y = space // (nh * ny), (space // ny) % nh, space % ny
    q, p = x * (1 - core) + y * core, y * (1 - core) + x * core
    mine = pl.ds(pl.multiple_of(core * half, half), half)
    other = pl.ds(pl.multiple_of((1 - core) * half, half), half)
    quarters = [
        pl.ds(pl.multiple_of(core * half + i * quarter, quarter), quarter) for i in range(2)
    ]

    def place(p_, q_):
        return q_ * (1 - core) + p_ * core, p_ * (1 - core) + q_ * core

    def at(p_, q_, h_):
        x_, y_ = place(p_, q_)
        return (member, (x_ * nh + h_) * ny + y_)

    def h_peer(k):
        return at(p, q, (h + k) % nh)

    def q_peer(k):
        return at(p, (q + k) % n, h)

    def m_peer(k):
        return ((member + k) % count, space)

    def z_peer(i):
        dh, dl = i // chips, i % chips
        return (2 * ((low + dl) % chips) + core, (x * nh + (h + dh) % nh) * ny + y)

    sides = [p + 1 - 2 * (p % 2), n - 1 - p]
    far = (p + 2) % n
    p_peers = [at(v, q, h) for v in sides]
    partner = (member + 1 - 2 * core, space)
    crossed = [(partner[0], peer[1]) for peer in p_peers]
    crossing = [
        (partner[0], at(p, v, h)[1]) for v in (q + 1 - 2 * (q % 2), n - 1 - q)
    ]

    def send(src, dst, send_sem, recv_sem, target):
        pltpu.make_async_remote_copy(
            src_ref=src, dst_ref=dst, send_sem=send_sem, recv_sem=recv_sem,
            device_id=target, device_id_type=MESH,
        ).start()

    def drain(ref, sem):
        pltpu.make_async_copy(ref, ref, sem).wait()

    def loop(first, last, body):
        def step(i, carry):
            body(i)
            return carry

        lax.fori_loop(first, last, step, 0)

    def by_rows(first, last, body):
        chunks = math.gcd(4, (last - first) // 16)

        def step(i):
            for u in range(chunks):
                body(rows_at(first + (i * chunks + u) * 16, 16))

        loop(0, (last - first) // (16 * chunks), step)

    barrier = pltpu.get_barrier_semaphore()

    def greet(peer):
        pl.semaphore_signal(barrier, inc=1, device_id=peer, device_id_type=MESH)

    loop(chips, nh * chips, lambda i: greet(z_peer(i)))
    loop(1, n, lambda k: greet(q_peer(k)))
    for peer in p_peers + crossing:
        greet(peer)
    loop(1, count, lambda k: greet(m_peer(k)))

    own_w = pltpu.make_async_copy(w_hbm.at[:, mine], w_full.at[x, h, y, :, mine], local_sem.at[0])
    loads = [
        pltpu.make_async_copy(source, target, local_sem.at[1 + i])
        for i, (source, target) in enumerate(
            [(hid_hbm, hid), (gain_hbm, gain), (truth_hbm, truth), (lat_hbm, lat), (wo_hbm, wo_raw)]
        )
    ]
    for load in loads[:2]:
        load.start()
    pl.semaphore_wait(barrier, nh * chips - chips + n - 1 + 4 + count - 1)

    own_block = w_full.at[x, h, y, :, mine]
    def to_z(dh, l_):
        target = (2 * l_ + core, (x * nh + (h + dh) % nh) * ny + y)
        send(w_hbm.at[:, mine], own_block, a1_s.at[0], a1_r.at[0], target)

    ends = ((chips - 1, 1, 0), (0, nh - 1, chips // 2))

    def from_end(action):
        for end, toward, start in ends:
            @pl.when(low == end)
            def _():
                action(toward, start)

    def spread_z(toward, start):
        loop(0, chips, lambda l_: to_z(toward, l_))
        loop(start, start + chips // 2, lambda l_: to_z(2, l_))

    if chips == 1:
        loop(1, nh, lambda k: to_z(k, 0))
    else:
        from_end(spread_z)
    own_w.start()
    for load in loads[2:]:
        load.start()
    loads[0].wait()
    loads[1].wait()

    def normalise(rows):
        values = hid[rows, :].astype(f32)
        root = jnp.sqrt(jnp.mean(values * values, axis=-1, keepdims=True) + EPSILON)
        inverse = 1.0 / root
        inv_root[rows, :] = jnp.broadcast_to(inverse, (16, LANES))
        normed[rows, :] = (values * inverse * gain[...]).astype(bf16)

    by_rows(0, points, normalise)
    for load in loads[2:]:
        load.wait()
    wo_pad[...] = jnp.zeros_like(wo_pad)
    wo_pad[0:levels, :] = wo_raw[...]
    wo_t[...] = wo_pad[...].T

    span = min(LANES, points)
    turns = points // span

    def rank(v, own):
        near = jnp.where(v == own + 1 - 2 * (own % 2), 1, 2)
        return jnp.where(v == own, 3, jnp.where(v == (own + 2) % n, 0, near))

    ranks = [
        [(core, rank(v, y)) for v in range(ny)], [(1 - core, rank(v, x)) for v in range(nx)]
    ]

    def turn(i):
        cols = rows_at(i * span, span)
        turned = normed[cols, :].T
        for x_ in range(nx):
            for h_ in range(nh):
                for y_ in range(ny):
                    first = ((x_ * nh + h_) * ny + y_) * block
                    piece = turned[first:first + block, :]
                    to_x, to_y = (x_ * nh + h_) * block, (y_ * nh + h_) * block
                    for (which, r), first in ((ranks[0][y_], to_x), (ranks[1][x_], to_y)):
                        start = pl.multiple_of(r * depth + first, block)
                        planes[which, pl.ds(start, block), cols] = piece

    loop(0, turns // 2, turn)
    own_w.wait()
    z_blocks = w_full.at[0, 0, pl.ds(0, nh - 1), :, mine]
    drain(z_blocks, a1_r.at[0])

    def group(p_, b, cols=mine):
        x_, y_ = place(p_, (q - b + n) % n)
        return w_full.at[x_, :, y_, :, cols]

    def to_partner(p_, b):
        part = group(p_, b)
        send(part, part, a4_s.at[0], a4_r.at[0], partner)

    def to_second(b):
        part = group(p, b)
        for i in range(2):
            send(part, part, a3_s.at[0], a3_r.at[b, i], p_peers[i])
        to_partner(p, b)

    def ordered(j):
        return j + (j // 2) * (n + 1 - 2 * j)

    own_group = group(p, 0)
    loop(1, n, lambda j: send(
        own_group, own_group, a2_s.at[0], a2_r.at[ordered(j) - 1], q_peer(ordered(j))
    ))
    to_second(0)
    def pass_first(j):
        b = ordered(j)
        drain(own_group, a2_r.at[b - 1])
        to_second(b)


    def pass_second(j):
        b = ordered(j)
        for i in range(2):
            drain(own_group, a3_r.at[b, i])
            part = group(sides[i], b, quarters[i])
            send(part, part, a3_s.at[0], a3_r.at[b, 2 + i], p_peers[1 - i])
            send(part, part, a3_s.at[0], a4_r.at[0], crossed[1 - i])
        for i in range(2):
            to_partner(sides[i], b)

    pass_second(0)
    loop(1, n, pass_first)
    loop(1, n, pass_second)

    def pass_far(j):
        b = ordered(j)
        for i in range(2):
            drain(group(far, b, quarters[i]), a3_r.at[b, 2 + i])

    loop(0, n, pass_far)

    def project(rows, cols):
        act[rows, cols] = jnp.dot(
            normed[rows, :], w_full[:, :, :, :, cols].reshape(width, half),
            preferred_element_type=f32,
        )

    def activate(rows, cols):
        a = act[rows, cols]
        hidden_act[rows, cols] = (a * (0.5 * jnp.tanh(0.5 * a) + 0.5)).astype(bf16)

    project(slice(0, tile), mine)
    by_rows(0, tile, lambda rows: activate(rows, mine))

    drain(w_full.at[:, :, :, :, other], a4_r.at[0])

    def share_of(t, m):
        return rows_at(t * tile + m * share, share)

    def tile_rows(t, body):
        by_rows(0, tile, lambda rows: body(rows_at(t * tile + rows.start, 16)))

    def forward(t, whole=True):
        rows = rows_at(t * tile, tile)
        if whole:
            act[rows, :] = jnp.dot(
                normed[rows, :], w_full[...].reshape(width, width), preferred_element_type=f32
            )
        else:
            project(rows, other)
        tile_rows(t, lambda part: activate(part, slice(0, width) if whole else other))
        field = jnp.dot(hidden_act[rows, :], wo_t[...], preferred_element_type=f32)
        fields[rows, :] = field
        coarse[rows, :] = field.astype(bf16)

        def spread(k):
            peer = m_peer(k)
            send(
                coarse.at[share_of(t, peer[0]), :], theirs.at[t, member],
                b1_s.at[0], b1_r.at[t], peer,
            )

        loop(1, count, spread)
        theirs[t, member] = coarse[share_of(t, member), :]

    def answer(t):
        come = theirs.at[t, pl.ds(0, count - 1)]
        drain(come, b1_r.at[t])

        def compare(i):
            rows = rows_at(i * 16, 16)
            values = [theirs[t, m, rows, :].astype(f32) for m in range(count)]
            totals = [jnp.zeros_like(values[0]) for m in range(count)]
            for m in range(count):
                for o in range(m + 1, count):
                    s = slope(values[m] - values[o])
                    totals[m] = totals[m] + s
                    totals[o] = totals[o] - s
            for m in range(count):
                answers[t, m, rows, :] = totals[m].astype(bf16)

        loop(0, share // 16, compare)

        def reply(k):
            peer = m_peer(k)
            send(
                answers.at[t, peer[0]], pairs.at[share_of(t, member), :],
                b2_s.at[0], b2_r.at[t], peer,
            )

        loop(1, count, reply)
        pairs[share_of(t, member), :] = answers[t, member]


    def differentiate(rows):
        a = act[rows, :]
        s = 0.5 * jnp.tanh(0.5 * a) + 0.5
        act[rows, :] = s * (1.0 + a * (1.0 - s))

    forward(0, whole=False)
    loop(1, tiles - 1, forward)
    truth_pad[...] = jnp.zeros_like(truth_pad)
    truth_pad[0:levels, :] = truth[...]
    truth_t[...] = truth_pad[...].T
    latitude = math.pi * ((lat[...].astype(f32) + 0.5) / LATS - 0.5)
    area = LOSS_SCALE * jnp.cos(latitude)
    strip = lat.shape[1]
    for i in range(lat.shape[0]):
        area_t[i * strip:(i + 1) * strip, :] = jnp.broadcast_to(area[i:i + 1, :], (LANES, strip)).T
    if tiles > 1:
        forward(tiles - 1)

    def reply_and_prepare(t):
        answer(t)
        tile_rows(t, differentiate)
        left = turns - turns // 2
        loop(turns // 2 + t * left // tiles, turns // 2 + (t + 1) * left // tiles, turn)

    loop(0, tiles, reply_and_prepare)

    fair = (1.0 - (1.0 - ALPHA) / count) / (count * (count - 1))

    def backward(t):
        come = pairs.at[pl.ds(0, tile - share), :]
        drain(come, b2_r.at[t])
        rows = rows_at(t * tile, tile)
        grad_fields = area_t[rows, :] * (
            slope(fields[rows, :] - truth_t[rows, :]) * (1.0 / count)
            - fair * pairs[rows, :].astype(f32)
        )
        grad_act = jnp.dot(grad_fields.astype(bf16), wo_pad[...], preferred_element_type=f32)
        gp[rows, :] = (grad_act * act[rows, :]).astype(bf16)

    loop(0, tiles, backward)

    def product(which, pair, cols):
        rows = rows_at(pair * 2 * depth, 2 * depth)
        return jnp.dot(planes[which, rows, :], gp[:, cols], preferred_element_type=f32)

    def other_pair(pair):
        part = product(1, pair, other).astype(bf16)
        for u in range(2):
            i = 2 * pair + u
            csend[i] = part[u * depth:(u + 1) * depth, :]
            send(csend.at[i], crecv.at[i], c0_s.at[0], c0_r.at[i], partner)

    loop(0, n // 2, other_pair)

    halves = [slice(0, quarter), slice(quarter, half)]

    def to_side(slot, target):
        send(send1.at[slot], recv1.at[slot], c1_s.at[0], c1_r.at[slot], p_peers[target])

    def own_pair(pair):
        part = product(0, pair, mine)
        for u in range(2):
            i = 2 * pair + u
            drain(crecv.at[i], c0_r.at[i])
            sums[i] = part[u * depth:(u + 1) * depth, :] + crecv[i].astype(f32)

    def to_near(side):
        send1[2 + side] = sums[1 + side, :, halves[side]].astype(bf16)
        to_side(2 + side, side)

    own_pair(0)
    for side in range(2):
        send1[side] = sums[0, :, halves[side]].astype(bf16)
        to_side(side, side)
    to_near(0)
    own_pair(1)
    to_near(1)
    for side in range(2):
        drain(recv1.at[side], c1_r.at[side])
        term = sums[2 - side, :, halves[side]] + recv1[side].astype(f32)
        send1[4 + side] = term.astype(bf16)
        to_side(4 + side, 1 - side)

    def grad_normed(x_):
        cols = rows_at(x_ * depth, depth)
        act[:, cols] = lax.dot_general(
            gp[...], w_full[x_].reshape(depth, width), (((1,), (1,)), ((), ())),
            preferred_element_type=f32,
        )

    def hidden_grad(rows):
        scaled = act[rows, :] * gain[...]
        inverse = inv_root[rows, 0:1]
        unit = hid[rows, :].astype(f32) * inverse
        inner = jnp.mean(scaled * unit, axis=-1, keepdims=True)
        gh[rows, :] = ((scaled - unit * inner) * inverse).astype(bf16)

    loop(0, n // 2, grad_normed)
    for slot in range(2, 6):
        drain(recv1.at[slot], c1_r.at[slot])
    line_rows = nh * block

    def add_planes(q_):
        rows = rows_at(q_ * line_rows, line_rows)
        both = [
            sums[n - 1, rows, halves[i]] + recv1[2 + i, rows, :].astype(f32)
            + recv1[4 + i, rows, :].astype(f32)
            for i in range(2)
        ]
        return jnp.concatenate(both, axis=1)

    def to_first(j):
        k = ordered(n - j)
        send2[j - 1] = add_planes((q + k) % n).astype(bf16)
        send(send2.at[j - 1], recv2.at[j - 1], c2_s.at[0], c2_r.at[0], q_peer(k))

    loop(1, n, to_first)
    total = add_planes(q)
    loop(n // 2, n, grad_normed)
    drain(recv2, c2_r.at[0])
    for i in range(n - 1):
        total = total + recv2[i].astype(f32)
    strip = half // chips
    for h_ in range(nh):
        for l_ in range(chips):
            send3[h_, l_] = total[
                h_ * block:(h_ + 1) * block, l_ * strip:(l_ + 1) * strip
            ].astype(bf16)
    loop(1, nh * chips, lambda i: send(
        send3.at[(h + i // chips) % nh, (low + i % chips) % chips], recv3.at[i - 1],
        c3_s.at[0], c3_r.at[0], z_peer(i),
    ))
    by_rows(0, points // 2, hidden_grad)
    drain(recv3, c3_r.at[0])
    total = send3[h, low].astype(f32)
    for i in range(nh * chips - 1):
        total = total + recv3[i].astype(f32)
    factor = 1.0 / math.sqrt(count * points * nx * nh * ny)
    finals[core * chips + low] = (total * factor).astype(bf16)
    own_final = finals.at[core * chips + low]
    loop(1, count, lambda k: send(own_final, own_final, c4_s.at[0], c4_r.at[0], m_peer(k)))
    by_rows(points // 2, points, hidden_grad)
    others = finals.at[pl.ds(0, count - 1)]
    drain(others, c4_r.at[0])
    for i in range(count):
        gw_ref[:, i * strip:(i + 1) * strip] = finals[i].astype(f32)

    if chips == 1:
        drain(z_blocks, a1_s.at[0])
    else:
        from_end(lambda toward, start: [drain(z_blocks, a1_s.at[0]) for _ in range(2)])
    drain(w_full.at[pl.ds(0, n - 1), :, 0, :, mine], a2_s.at[0])
    drain(w_full.at[:, :, :, :, mine], a3_s.at[0])
    drain(w_full.at[:, :, pl.ds(0, 3), :, mine], a4_s.at[0])
    drain(coarse.at[pl.ds(0, points - points // count), :], b1_s.at[0])
    drain(coarse.at[pl.ds(0, points - points // count), :], b2_s.at[0])
    drain(csend, c0_s.at[0])
    drain(send1, c1_s.at[0])
    drain(send2, c2_s.at[0])
    drain(recv3, c3_s.at[0])
    drain(others, c4_s.at[0])


def hand_over(*arrays):
    pieces = 4

    def body(*refs):
        sources, targets, sems = refs[:len(arrays)], refs[len(arrays):-1], refs[-1]
        copies = []
        for source, target in zip(sources, targets):
            rows = source.shape[0]
            parts = pieces if rows % (16 * pieces) == 0 else 1
            for i in range(parts):
                part = pl.ds(i * (rows // parts), rows // parts)
                copies.append(
                    pltpu.make_async_copy(source.at[part], target.at[part], sems.at[len(copies)])
                )
        for copy in copies:
            copy.start()
        for copy in copies:
            copy.wait()

    anywhere = pl.BlockSpec(memory_space=pl.ANY)
    return pl.pallas_call(
        body,
        out_shape=tuple(jax.ShapeDtypeStruct(a.shape, a.dtype) for a in arrays),
        in_specs=[anywhere] * len(arrays),
        out_specs=(anywhere,) * len(arrays),
        scratch_shapes=[pltpu.SemaphoreType.DMA((pieces * len(arrays),))],
        compiler_params=pltpu.CompilerParams(vmem_limit_bytes=1024 * 1024),
        name="hand_over",
    )(*arrays)


def per_device(hidden, truth, lat_row, gain, w_in, w_out):
    nx, nh, ny = GRID
    count = lax.axis_size("member")
    _, points, width = hidden.shape
    levels = truth.shape[0]
    block = w_in.shape[0]
    half = width // 2
    tile = min(TILE, points)
    tiles, share = points // tile, tile // count
    f32, bf16 = jnp.float32, jnp.bfloat16
    vmem, dma = pltpu.VMEM, pltpu.SemaphoreType.DMA
    n, chips, lat_strip = nx, count // 2, min(LANES, points)
    scratch = [
        vmem((points, width), bf16),
        vmem((levels, points), f32),
        vmem((points // lat_strip, lat_strip), jnp.int32),
        vmem((1, width), f32),
        vmem((levels, width), bf16),
        vmem((nx, nh, ny, block, width), bf16),
        vmem((points, width), bf16),
        vmem((2, width, points), bf16),
        vmem((points, LANES), f32),
        vmem((LANES, width), bf16),
        vmem((width, LANES), bf16),
        vmem((points, width), bf16),
        vmem((LANES, points), f32),
        vmem((points, LANES), f32),
        vmem((points, LANES), f32),
        vmem((points, width), f32),
        vmem((points, LANES), f32),
        vmem((points, LANES), bf16),
        vmem((tiles, count, share, LANES), bf16),
        vmem((tiles, count, share, LANES), bf16),
        vmem((points, LANES), bf16),
        vmem((points, width), bf16),
        vmem((n, width // n, half), bf16),
        vmem((n, width // n, half), bf16),
        vmem((n, width // n, half), f32),
        vmem((6, width // n, half // 2), bf16),
        vmem((6, width // n, half // 2), bf16),
        vmem((n - 1, nh * block, half), bf16),
        vmem((n - 1, nh * block, half), bf16),
        vmem((nh, chips, block, half // chips), bf16),
        vmem((nh * chips - 1, block, half // chips), bf16),
        vmem((count, block, half // chips), bf16),
        dma((6,)),
    ]
    for arrivals in (
        (1,), (n - 1,), (n, 4), (1,),
        (tiles,), (tiles,),
        (n,), (6,), (1,), (1,), (1,),
    ):
        scratch += [dma((1,)), dma(arrivals)]
    grad_rows, grad_first = pl.pallas_call(
        functools.partial(kernel, tile),
        out_shape=(
            vmem((points, width), bf16),
            vmem((block, width), f32),
        ),
        in_specs=[pl.BlockSpec(memory_space=pltpu.HBM)] * 6,
        out_specs=(pl.BlockSpec(memory_space=vmem),) * 2,
        scratch_shapes=scratch,
        compiler_params=pltpu.CompilerParams(
            collective_id=0, has_side_effects=True, vmem_limit_bytes=57 * 1024 * 1024
        ),
        name="crps_step",
    )(
        hidden[0], truth, lat_row.reshape(points // lat_strip, lat_strip), gain[None], w_in, w_out
    )
    grad_rows, grad_first = hand_over(grad_rows, grad_first)
    return (grad_rows[None], grad_first)


def solution(mesh):
    in_specs = (
        P("member", "space", None),
        P(None, "space"),
        P("space"),
        P(),
        P("space", None),
        P(),
    )
    out_specs = (P("member", "space", None), P("space", None))
    return jax.shard_map(
        per_device, mesh=mesh, in_specs=in_specs, out_specs=out_specs, check_vma=False
    )
```

```python
import functools
import math

import jax
import jax.numpy as jnp
from jax import lax
from jax.experimental import pallas as pl
from jax.experimental.pallas import tpu as pltpu
from jax.sharding import PartitionSpec as P

LATS = 721
ALPHA = 0.95
SMOOTH = 0.1
LOSS_SCALE = 64.0
EPSILON = 1e-05

GRID = (4, 4, 4)
LANES = 128
TILE = 256
MESH = pl.DeviceIdType.MESH


def slope(diff):
    return diff * lax.rsqrt(diff * diff + SMOOTH * SMOOTH)


def rows_at(start, size):
    return pl.ds(pl.multiple_of(start, size), size)


def kernel(
    tile,
    hid_hbm, truth_hbm, lat_hbm, gain_hbm, w_hbm, wo_hbm,
    gh, gw_ref,
    hid, truth, lat, gain, wo_raw, w_full, normed, planes, inv_root, wo_pad, wo_t, hidden_act,
    truth_pad, truth_t, area_t, act, fields, coarse, theirs, answers, pairs, gp,
    csend, crecv, sums, send1, recv1, send2, recv2, send3, recv3, finals,
    local_sem, a1_s, a1_r, a2_s, a2_r, a3_s, a3_r, a4_s, a4_r,
    b1_s, b1_r, b2_s, b2_r, c0_s, c0_r, c1_s, c1_r, c2_s, c2_r, c3_s, c3_r, c4_s, c4_r,
):
    nx, nh, ny = GRID
    n = nx
    points, width = hid.shape
    half = width // 2
    quarter = half // 2
    depth = width // n
    levels = truth.shape[0]
    count = finals.shape[0]
    chips = count // 2
    block = w_full.shape[3]
    tiles, share = theirs.shape[0], theirs.shape[2]
    f32, bf16 = jnp.float32, jnp.bfloat16

    member, space = lax.axis_index("member"), lax.axis_index("space")
    core, low = member % 2, member // 2
    x, h, y = space // (nh * ny), (space // ny) % nh, space % ny
    q, p = x * (1 - core) + y * core, y * (1 - core) + x * core
    mine = pl.ds(pl.multiple_of(core * half, half), half)
    other = pl.ds(pl.multiple_of((1 - core) * half, half), half)
    quarters = [
        pl.ds(pl.multiple_of(core * half + i * quarter, quarter), quarter) for i in range(2)
    ]

    def place(p_, q_):
        return q_ * (1 - core) + p_ * core, p_ * (1 - core) + q_ * core

    def at(p_, q_, h_):
        x_, y_ = place(p_, q_)
        return (member, (x_ * nh + h_) * ny + y_)

    def h_peer(k):
        return at(p, q, (h + k) % nh)

    def q_peer(k):
        return at(p, (q + k) % n, h)

    def m_peer(k):
        return ((member + k) % count, space)

    def z_peer(i):
        dh, dl = i // chips, i % chips
        return (2 * ((low + dl) % chips) + core, (x * nh + (h + dh) % nh) * ny + y)

    sides = [p + 1 - 2 * (p % 2), n - 1 - p]
    far = (p + 2) % n
    p_peers = [at(v, q, h) for v in sides]
    partner = (member + 1 - 2 * core, space)
    crossed = [(partner[0], peer[1]) for peer in p_peers]
    crossing = [
        (partner[0], at(p, v, h)[1]) for v in (q + 1 - 2 * (q % 2), n - 1 - q)
    ]

    def send(src, dst, send_sem, recv_sem, target):
        pltpu.make_async_remote_copy(
            src_ref=src, dst_ref=dst, send_sem=send_sem, recv_sem=recv_sem,
            device_id=target, device_id_type=MESH,
        ).start()

    def drain(ref, sem):
        pltpu.make_async_copy(ref, ref, sem).wait()

    def loop(first, last, body):
        def step(i, carry):
            body(i)
            return carry

        lax.fori_loop(first, last, step, 0)

    def by_rows(first, last, body):
        chunks = math.gcd(4, (last - first) // 16)

        def step(i):
            for u in range(chunks):
                body(rows_at(first + (i * chunks + u) * 16, 16))

        loop(0, (last - first) // (16 * chunks), step)

    barrier = pltpu.get_barrier_semaphore()

    def greet(peer):
        pl.semaphore_signal(barrier, inc=1, device_id=peer, device_id_type=MESH)

    loop(chips, nh * chips, lambda i: greet(z_peer(i)))
    loop(1, n, lambda k: greet(q_peer(k)))
    for peer in p_peers + crossing:
        greet(peer)
    loop(1, count, lambda k: greet(m_peer(k)))

    own_w = pltpu.make_async_copy(w_hbm.at[:, mine], w_full.at[x, h, y, :, mine], local_sem.at[0])
    loads = [
        pltpu.make_async_copy(source, target, local_sem.at[1 + i])
        for i, (source, target) in enumerate(
            [(hid_hbm, hid), (gain_hbm, gain), (truth_hbm, truth), (lat_hbm, lat), (wo_hbm, wo_raw)]
        )
    ]
    for load in loads[:2]:
        load.start()
    pl.semaphore_wait(barrier, nh * chips - chips + n - 1 + 4 + count - 1)

    own_block = w_full.at[x, h, y, :, mine]
    def to_z(dh, l_):
        target = (2 * l_ + core, (x * nh + (h + dh) % nh) * ny + y)
        send(w_hbm.at[:, mine], own_block, a1_s.at[0], a1_r.at[0], target)

    ends = ((chips - 1, 1, 0), (0, nh - 1, chips // 2))

    def from_end(action):
        for end, toward, start in ends:
            @pl.when(low == end)
            def _():
                action(toward, start)

    def spread_z(toward, start):
        loop(0, chips, lambda l_: to_z(toward, l_))
        loop(start, start + chips // 2, lambda l_: to_z(2, l_))

    if chips == 1:
        loop(1, nh, lambda k: to_z(k, 0))
    else:
        from_end(spread_z)
    own_w.start()
    for load in loads[2:]:
        load.start()
    loads[0].wait()
    loads[1].wait()

    def normalise(rows):
        values = hid[rows, :].astype(f32)
        root = jnp.sqrt(jnp.mean(values * values, axis=-1, keepdims=True) + EPSILON)
        inverse = 1.0 / root
        inv_root[rows, :] = jnp.broadcast_to(inverse, (16, LANES))
        normed[rows, :] = (values * inverse * gain[...]).astype(bf16)

    by_rows(0, points, normalise)
    for load in loads[2:]:
        load.wait()
    wo_pad[...] = jnp.zeros_like(wo_pad)
    wo_pad[0:levels, :] = wo_raw[...]
    wo_t[...] = wo_pad[...].T

    span = min(LANES, points)
    turns = points // span

    def rank(v, own):
        near = jnp.where(v == own + 1 - 2 * (own % 2), 1, 2)
        return jnp.where(v == own, 3, jnp.where(v == (own + 2) % n, 0, near))

    ranks = [
        [(core, rank(v, y)) for v in range(ny)], [(1 - core, rank(v, x)) for v in range(nx)]
    ]

    def turn(i):
        cols = rows_at(i * span, span)
        turned = normed[cols, :].T
        for x_ in range(nx):
            for h_ in range(nh):
                for y_ in range(ny):
                    first = ((x_ * nh + h_) * ny + y_) * block
                    piece = turned[first:first + block, :]
                    to_x, to_y = (x_ * nh + h_) * block, (y_ * nh + h_) * block
                    for (which, r), first in ((ranks[0][y_], to_x), (ranks[1][x_], to_y)):
                        start = pl.multiple_of(r * depth + first, block)
                        planes[which, pl.ds(start, block), cols] = piece

    loop(0, turns, turn)
    own_w.wait()
    z_blocks = w_full.at[0, 0, pl.ds(0, nh - 1), :, mine]
    drain(z_blocks, a1_r.at[0])

    def group(p_, b, cols=mine):
        x_, y_ = place(p_, (q - b + n) % n)
        return w_full.at[x_, :, y_, :, cols]

    def to_partner(p_, b):
        part = group(p_, b)
        send(part, part, a4_s.at[0], a4_r.at[0], partner)

    def to_second(b):
        part = group(p, b)
        for i in range(2):
            send(part, part, a3_s.at[0], a3_r.at[b, i], p_peers[i])
        to_partner(p, b)

    def ordered(j):
        return j + (j // 2) * (n + 1 - 2 * j)

    own_group = group(p, 0)
    loop(1, n, lambda j: send(
        own_group, own_group, a2_s.at[0], a2_r.at[ordered(j) - 1], q_peer(ordered(j))
    ))
    to_second(0)
    def pass_first(j):
        b = ordered(j)
        drain(own_group, a2_r.at[b - 1])
        to_second(b)


    def pass_second(j):
        b = ordered(j)
        for i in range(2):
            drain(own_group, a3_r.at[b, i])
            part = group(sides[i], b, quarters[i])
            send(part, part, a3_s.at[0], a3_r.at[b, 2 + i], p_peers[1 - i])
            send(part, part, a3_s.at[0], a4_r.at[0], crossed[1 - i])
        for i in range(2):
            to_partner(sides[i], b)

    pass_second(0)
    loop(1, n, pass_first)
    loop(1, n, pass_second)

    def pass_far(j):
        b = ordered(j)
        for i in range(2):
            drain(group(far, b, quarters[i]), a3_r.at[b, 2 + i])

    loop(0, n, pass_far)

    def project(rows, cols):
        act[rows, cols] = jnp.dot(
            normed[rows, :], w_full[:, :, :, :, cols].reshape(width, half),
            preferred_element_type=f32,
        )

    def activate(rows, cols):
        a = act[rows, cols]
        s = 0.5 * jnp.tanh(0.5 * a) + 0.5
        hidden_act[rows, cols] = (a * s).astype(bf16)
        act[rows, cols] = s * (1.0 + a * (1.0 - s))

    project(slice(0, tile), mine)
    by_rows(0, tile, lambda rows: activate(rows, mine))

    drain(w_full.at[:, :, :, :, other], a4_r.at[0])

    def share_of(t, m):
        return rows_at(t * tile + m * share, share)

    def tile_rows(t, body):
        by_rows(0, tile, lambda rows: body(rows_at(t * tile + rows.start, 16)))

    def forward(t, whole=True):
        rows = rows_at(t * tile, tile)
        if whole:
            act[rows, :] = jnp.dot(
                normed[rows, :], w_full[...].reshape(width, width), preferred_element_type=f32
            )
        else:
            project(rows, other)
        tile_rows(t, lambda part: activate(part, slice(0, width) if whole else other))
        field = jnp.dot(hidden_act[rows, :], wo_t[...], preferred_element_type=f32)
        fields[rows, :] = field
        coarse[rows, :] = field.astype(bf16)

        def spread(k):
            peer = m_peer(k)
            send(
                coarse.at[share_of(t, peer[0]), :], theirs.at[t, member],
                b1_s.at[0], b1_r.at[t], peer,
            )

        loop(1, count, spread)
        theirs[t, member] = coarse[share_of(t, member), :]

    def answer(t):
        come = theirs.at[t, pl.ds(0, count - 1)]
        drain(come, b1_r.at[t])

        def compare(i):
            rows = rows_at(i * 16, 16)
            values = [theirs[t, m, rows, :].astype(f32) for m in range(count)]
            totals = [jnp.zeros_like(values[0]) for m in range(count)]
            for m in range(count):
                for o in range(m + 1, count):
                    s = slope(values[m] - values[o])
                    totals[m] = totals[m] + s
                    totals[o] = totals[o] - s
            for m in range(count):
                answers[t, m, rows, :] = totals[m].astype(bf16)

        loop(0, share // 16, compare)

        def reply(k):
            peer = m_peer(k)
            send(
                answers.at[t, peer[0]], pairs.at[share_of(t, member), :],
                b2_s.at[0], b2_r.at[t], peer,
            )

        loop(1, count, reply)
        pairs[share_of(t, member), :] = answers[t, member]


    forward(0, whole=False)
    loop(1, tiles - 1, forward)
    truth_pad[...] = jnp.zeros_like(truth_pad)
    truth_pad[0:levels, :] = truth[...]
    truth_t[...] = truth_pad[...].T
    latitude = math.pi * ((lat[...].astype(f32) + 0.5) / LATS - 0.5)
    area = LOSS_SCALE * jnp.cos(latitude)
    strip = lat.shape[1]
    for i in range(lat.shape[0]):
        area_t[i * strip:(i + 1) * strip, :] = jnp.broadcast_to(area[i:i + 1, :], (LANES, strip)).T
    if tiles > 1:
        forward(tiles - 1)

    loop(0, tiles, answer)

    fair = (1.0 - (1.0 - ALPHA) / count) / (count * (count - 1))

    def backward(t):
        come = pairs.at[pl.ds(0, tile - share), :]
        drain(come, b2_r.at[t])
        rows = rows_at(t * tile, tile)
        grad_fields = area_t[rows, :] * (
            slope(fields[rows, :] - truth_t[rows, :]) * (1.0 / count)
            - fair * pairs[rows, :].astype(f32)
        )
        grad_act = jnp.dot(grad_fields.astype(bf16), wo_pad[...], preferred_element_type=f32)
        gp[rows, :] = (grad_act * act[rows, :]).astype(bf16)

    loop(0, tiles, backward)

    def product(which, pair, cols):
        rows = rows_at(pair * 2 * depth, 2 * depth)
        return jnp.dot(planes[which, rows, :], gp[:, cols], preferred_element_type=f32)

    def other_pair(pair):
        part = product(1, pair, other).astype(bf16)
        for u in range(2):
            i = 2 * pair + u
            csend[i] = part[u * depth:(u + 1) * depth, :]
            send(csend.at[i], crecv.at[i], c0_s.at[0], c0_r.at[i], partner)

    loop(0, n // 2, other_pair)

    halves = [slice(0, quarter), slice(quarter, half)]

    def to_side(slot, target):
        send(send1.at[slot], recv1.at[slot], c1_s.at[0], c1_r.at[slot], p_peers[target])

    def own_pair(pair):
        part = product(0, pair, mine)
        for u in range(2):
            i = 2 * pair + u
            drain(crecv.at[i], c0_r.at[i])
            sums[i] = part[u * depth:(u + 1) * depth, :] + crecv[i].astype(f32)

    def to_near(side):
        send1[2 + side] = sums[1 + side, :, halves[side]].astype(bf16)
        to_side(2 + side, side)

    own_pair(0)
    for side in range(2):
        send1[side] = sums[0, :, halves[side]].astype(bf16)
        to_side(side, side)
    to_near(0)
    own_pair(1)
    to_near(1)
    for side in range(2):
        drain(recv1.at[side], c1_r.at[side])
        term = sums[2 - side, :, halves[side]] + recv1[side].astype(f32)
        send1[4 + side] = term.astype(bf16)
        to_side(4 + side, 1 - side)

    def grad_normed(x_):
        cols = rows_at(x_ * depth, depth)
        act[:, cols] = lax.dot_general(
            gp[...], w_full[x_].reshape(depth, width), (((1,), (1,)), ((), ())),
            preferred_element_type=f32,
        )

    def hidden_grad(rows):
        scaled = act[rows, :] * gain[...]
        inverse = inv_root[rows, 0:1]
        unit = hid[rows, :].astype(f32) * inverse
        inner = jnp.mean(scaled * unit, axis=-1, keepdims=True)
        gh[rows, :] = ((scaled - unit * inner) * inverse).astype(bf16)

    loop(0, n // 2, grad_normed)
    for slot in range(2, 6):
        drain(recv1.at[slot], c1_r.at[slot])
    line_rows = nh * block

    def add_planes(q_):
        rows = rows_at(q_ * line_rows, line_rows)
        both = [
            sums[n - 1, rows, halves[i]] + recv1[2 + i, rows, :].astype(f32)
            + recv1[4 + i, rows, :].astype(f32)
            for i in range(2)
        ]
        return jnp.concatenate(both, axis=1)

    def to_first(j):
        k = ordered(n - j)
        send2[j - 1] = add_planes((q + k) % n).astype(bf16)
        send(send2.at[j - 1], recv2.at[j - 1], c2_s.at[0], c2_r.at[0], q_peer(k))

    loop(1, n, to_first)
    total = add_planes(q)
    loop(n // 2, n, grad_normed)
    drain(recv2, c2_r.at[0])
    for i in range(n - 1):
        total = total + recv2[i].astype(f32)
    strip = half // chips
    for h_ in range(nh):
        for l_ in range(chips):
            send3[h_, l_] = total[
                h_ * block:(h_ + 1) * block, l_ * strip:(l_ + 1) * strip
            ].astype(bf16)
    loop(1, nh * chips, lambda i: send(
        send3.at[(h + i // chips) % nh, (low + i % chips) % chips], recv3.at[i - 1],
        c3_s.at[0], c3_r.at[0], z_peer(i),
    ))
    by_rows(0, points // 2, hidden_grad)
    drain(recv3, c3_r.at[0])
    total = send3[h, low].astype(f32)
    for i in range(nh * chips - 1):
        total = total + recv3[i].astype(f32)
    factor = 1.0 / math.sqrt(count * points * nx * nh * ny)
    finals[core * chips + low] = (total * factor).astype(bf16)
    own_final = finals.at[core * chips + low]
    loop(1, count, lambda k: send(own_final, own_final, c4_s.at[0], c4_r.at[0], m_peer(k)))
    by_rows(points // 2, points, hidden_grad)
    others = finals.at[pl.ds(0, count - 1)]
    drain(others, c4_r.at[0])
    for i in range(count):
        gw_ref[:, i * strip:(i + 1) * strip] = finals[i].astype(f32)

    if chips == 1:
        drain(z_blocks, a1_s.at[0])
    else:
        from_end(lambda toward, start: [drain(z_blocks, a1_s.at[0]) for _ in range(2)])
    drain(w_full.at[pl.ds(0, n - 1), :, 0, :, mine], a2_s.at[0])
    drain(w_full.at[:, :, :, :, mine], a3_s.at[0])
    drain(w_full.at[:, :, pl.ds(0, 3), :, mine], a4_s.at[0])
    drain(coarse.at[pl.ds(0, points - points // count), :], b1_s.at[0])
    drain(coarse.at[pl.ds(0, points - points // count), :], b2_s.at[0])
    drain(csend, c0_s.at[0])
    drain(send1, c1_s.at[0])
    drain(send2, c2_s.at[0])
    drain(recv3, c3_s.at[0])
    drain(others, c4_s.at[0])


def hand_over(*arrays):
    pieces = 4

    def body(*refs):
        sources, targets, sems = refs[:len(arrays)], refs[len(arrays):-1], refs[-1]
        copies = []
        for source, target in zip(sources, targets):
            rows = source.shape[0]
            parts = pieces if rows % (16 * pieces) == 0 else 1
            for i in range(parts):
                part = pl.ds(i * (rows // parts), rows // parts)
                copies.append(
                    pltpu.make_async_copy(source.at[part], target.at[part], sems.at[len(copies)])
                )
        for copy in copies:
            copy.start()
        for copy in copies:
            copy.wait()

    anywhere = pl.BlockSpec(memory_space=pl.ANY)
    return pl.pallas_call(
        body,
        out_shape=tuple(jax.ShapeDtypeStruct(a.shape, a.dtype) for a in arrays),
        in_specs=[anywhere] * len(arrays),
        out_specs=(anywhere,) * len(arrays),
        scratch_shapes=[pltpu.SemaphoreType.DMA((pieces * len(arrays),))],
        compiler_params=pltpu.CompilerParams(vmem_limit_bytes=1024 * 1024),
        name="hand_over",
    )(*arrays)


def per_device(hidden, truth, lat_row, gain, w_in, w_out):
    nx, nh, ny = GRID
    count = lax.axis_size("member")
    _, points, width = hidden.shape
    levels = truth.shape[0]
    block = w_in.shape[0]
    half = width // 2
    tile = min(TILE, points)
    tiles, share = points // tile, tile // count
    f32, bf16 = jnp.float32, jnp.bfloat16
    vmem, dma = pltpu.VMEM, pltpu.SemaphoreType.DMA
    n, chips, lat_strip = nx, count // 2, min(LANES, points)
    scratch = [
        vmem((points, width), bf16),
        vmem((levels, points), f32),
        vmem((points // lat_strip, lat_strip), jnp.int32),
        vmem((1, width), f32),
        vmem((levels, width), bf16),
        vmem((nx, nh, ny, block, width), bf16),
        vmem((points, width), bf16),
        vmem((2, width, points), bf16),
        vmem((points, LANES), f32),
        vmem((LANES, width), bf16),
        vmem((width, LANES), bf16),
        vmem((points, width), bf16),
        vmem((LANES, points), f32),
        vmem((points, LANES), f32),
        vmem((points, LANES), f32),
        vmem((points, width), f32),
        vmem((points, LANES), f32),
        vmem((points, LANES), bf16),
        vmem((tiles, count, share, LANES), bf16),
        vmem((tiles, count, share, LANES), bf16),
        vmem((points, LANES), bf16),
        vmem((points, width), bf16),
        vmem((n, width // n, half), bf16),
        vmem((n, width // n, half), bf16),
        vmem((n, width // n, half), f32),
        vmem((6, width // n, half // 2), bf16),
        vmem((6, width // n, half // 2), bf16),
        vmem((n - 1, nh * block, half), bf16),
        vmem((n - 1, nh * block, half), bf16),
        vmem((nh, chips, block, half // chips), bf16),
        vmem((nh * chips - 1, block, half // chips), bf16),
        vmem((count, block, half // chips), bf16),
        dma((6,)),
    ]
    for arrivals in (
        (1,), (n - 1,), (n, 4), (1,),
        (tiles,), (tiles,),
        (n,), (6,), (1,), (1,), (1,),
    ):
        scratch += [dma((1,)), dma(arrivals)]
    grad_rows, grad_first = pl.pallas_call(
        functools.partial(kernel, tile),
        out_shape=(
            vmem((points, width), bf16),
            vmem((block, width), f32),
        ),
        in_specs=[pl.BlockSpec(memory_space=pltpu.HBM)] * 6,
        out_specs=(pl.BlockSpec(memory_space=vmem),) * 2,
        scratch_shapes=scratch,
        compiler_params=pltpu.CompilerParams(
            collective_id=0, has_side_effects=True, vmem_limit_bytes=57 * 1024 * 1024
        ),
        name="crps_step",
    )(
        hidden[0], truth, lat_row.reshape(points // lat_strip, lat_strip), gain[None], w_in, w_out
    )
    grad_rows, grad_first = hand_over(grad_rows, grad_first)
    return (grad_rows[None], grad_first)


def solution(mesh):
    in_specs = (
        P("member", "space", None),
        P(None, "space"),
        P("space"),
        P(),
        P("space", None),
        P(),
    )
    out_specs = (P("member", "space", None), P("space", None))
    return jax.shard_map(
        per_device, mesh=mesh, in_specs=in_specs, out_specs=out_specs, check_vma=False
    )
```

```python
import functools
import math

import jax
import jax.numpy as jnp
from jax import lax
from jax.experimental import pallas as pl
from jax.experimental.pallas import tpu as pltpu
from jax.sharding import PartitionSpec as P

LATS = 721
ALPHA = 0.95
SMOOTH = 0.1
LOSS_SCALE = 64.0
EPSILON = 1e-05

GRID = (4, 4, 4)
LANES = 128
TILE = 384
MESH = pl.DeviceIdType.MESH


def slope(diff):
    return diff * lax.rsqrt(diff * diff + SMOOTH * SMOOTH)


def rows_at(start, size):
    return pl.ds(pl.multiple_of(start, size), size)


def kernel(
    tile,
    hid_hbm, truth_hbm, lat_hbm, gain_hbm, w_hbm, wo_hbm,
    gh, gw_ref,
    hid, truth, lat, gain, wo_raw, w_full, normed, planes, inv_root, wo_pad, wo_t, hidden_act,
    truth_pad, truth_t, area_t, act, fields, coarse, theirs, answers, pairs, gp,
    csend, crecv, sums, send1, recv1, send2, recv2, send3, recv3, finals,
    local_sem, a1_s, a1_r, a2_s, a2_r, a3_s, a3_r, a4_s, a4_r,
    b1_s, b1_r, b2_s, b2_r, c0_s, c0_r, c1_s, c1_r, c2_s, c2_r, c3_s, c3_r, c4_s, c4_r,
):
    nx, nh, ny = GRID
    n = nx
    points, width = hid.shape
    half = width // 2
    quarter = half // 2
    depth = width // n
    levels = truth.shape[0]
    count = finals.shape[0]
    chips = count // 2
    block = w_full.shape[3]
    tiles, share = theirs.shape[0], theirs.shape[2]
    f32, bf16 = jnp.float32, jnp.bfloat16

    member, space = lax.axis_index("member"), lax.axis_index("space")
    core, low = member % 2, member // 2
    x, h, y = space // (nh * ny), (space // ny) % nh, space % ny
    q, p = x * (1 - core) + y * core, y * (1 - core) + x * core
    mine = pl.ds(pl.multiple_of(core * half, half), half)
    other = pl.ds(pl.multiple_of((1 - core) * half, half), half)
    quarters = [
        pl.ds(pl.multiple_of(core * half + i * quarter, quarter), quarter) for i in range(2)
    ]

    def place(p_, q_):
        return q_ * (1 - core) + p_ * core, p_ * (1 - core) + q_ * core

    def at(p_, q_, h_):
        x_, y_ = place(p_, q_)
        return (member, (x_ * nh + h_) * ny + y_)

    def h_peer(k):
        return at(p, q, (h + k) % nh)

    def q_peer(k):
        return at(p, (q + k) % n, h)

    def m_peer(k):
        return ((member + k) % count, space)

    def z_peer(i):
        dh, dl = i // chips, i % chips
        return (2 * ((low + dl) % chips) + core, (x * nh + (h + dh) % nh) * ny + y)

    sides = [p + 1 - 2 * (p % 2), n - 1 - p]
    far = (p + 2) % n
    p_peers = [at(v, q, h) for v in sides]
    partner = (member + 1 - 2 * core, space)
    crossed = [(partner[0], peer[1]) for peer in p_peers]
    crossing = [
        (partner[0], at(p, v, h)[1]) for v in (q + 1 - 2 * (q % 2), n - 1 - q)
    ]

    def send(src, dst, send_sem, recv_sem, target):
        pltpu.make_async_remote_copy(
            src_ref=src, dst_ref=dst, send_sem=send_sem, recv_sem=recv_sem,
            device_id=target, device_id_type=MESH,
        ).start()

    def drain(ref, sem):
        pltpu.make_async_copy(ref, ref, sem).wait()

    def loop(first, last, body):
        def step(i, carry):
            body(i)
            return carry

        lax.fori_loop(first, last, step, 0)

    def by_rows(first, last, body):
        chunks = math.gcd(4, (last - first) // 16)

        def step(i):
            for u in range(chunks):
                body(rows_at(first + (i * chunks + u) * 16, 16))

        loop(0, (last - first) // (16 * chunks), step)

    barrier = pltpu.get_barrier_semaphore()

    def greet(peer):
        pl.semaphore_signal(barrier, inc=1, device_id=peer, device_id_type=MESH)

    loop(chips, nh * chips, lambda i: greet(z_peer(i)))
    loop(1, n, lambda k: greet(q_peer(k)))
    for peer in p_peers + crossing:
        greet(peer)
    loop(1, count, lambda k: greet(m_peer(k)))

    own_w = pltpu.make_async_copy(w_hbm.at[:, mine], w_full.at[x, h, y, :, mine], local_sem.at[0])
    loads = [
        pltpu.make_async_copy(source, target, local_sem.at[1 + i])
        for i, (source, target) in enumerate(
            [(hid_hbm, hid), (gain_hbm, gain), (truth_hbm, truth), (lat_hbm, lat), (wo_hbm, wo_raw)]
        )
    ]
    for load in loads[:2]:
        load.start()
    pl.semaphore_wait(barrier, nh * chips - chips + n - 1 + 4 + count - 1)

    own_block = w_full.at[x, h, y, :, mine]
    def to_z(dh, l_):
        target = (2 * l_ + core, (x * nh + (h + dh) % nh) * ny + y)
        send(w_hbm.at[:, mine], own_block, a1_s.at[0], a1_r.at[0], target)

    ends = ((chips - 1, 1, 0), (0, nh - 1, chips // 2))

    def from_end(action):
        for end, toward, start in ends:
            @pl.when(low == end)
            def _():
                action(toward, start)

    def spread_z(toward, start):
        loop(0, chips, lambda l_: to_z(toward, l_))
        loop(start, start + chips // 2, lambda l_: to_z(2, l_))

    if chips == 1:
        loop(1, nh, lambda k: to_z(k, 0))
    else:
        from_end(spread_z)
    own_w.start()
    for load in loads[2:]:
        load.start()
    loads[0].wait()
    loads[1].wait()

    def normalise(rows):
        values = hid[rows, :].astype(f32)
        root = jnp.sqrt(jnp.mean(values * values, axis=-1, keepdims=True) + EPSILON)
        inverse = 1.0 / root
        inv_root[rows, :] = jnp.broadcast_to(inverse, (16, LANES))
        normed[rows, :] = (values * inverse * gain[...]).astype(bf16)

    by_rows(0, points, normalise)
    for load in loads[2:]:
        load.wait()
    wo_pad[...] = jnp.zeros_like(wo_pad)
    wo_pad[0:levels, :] = wo_raw[...]
    wo_t[...] = wo_pad[...].T

    span = min(LANES, points)
    turns = points // span

    def rank(v, own):
        near = jnp.where(v == own + 1 - 2 * (own % 2), 1, 2)
        return jnp.where(v == own, 3, jnp.where(v == (own + 2) % n, 0, near))

    ranks = [
        [(core, rank(v, y)) for v in range(ny)], [(1 - core, rank(v, x)) for v in range(nx)]
    ]

    def turn(i):
        cols = rows_at(i * span, span)
        turned = normed[cols, :].T
        for x_ in range(nx):
            for h_ in range(nh):
                for y_ in range(ny):
                    first = ((x_ * nh + h_) * ny + y_) * block
                    piece = turned[first:first + block, :]
                    to_x, to_y = (x_ * nh + h_) * block, (y_ * nh + h_) * block
                    for (which, r), first in ((ranks[0][y_], to_x), (ranks[1][x_], to_y)):
                        start = pl.multiple_of(r * depth + first, block)
                        planes[which, pl.ds(start, block), cols] = piece

    loop(0, turns // 2, turn)
    own_w.wait()
    z_blocks = w_full.at[0, 0, pl.ds(0, nh - 1), :, mine]
    drain(z_blocks, a1_r.at[0])

    def group(p_, b, cols=mine):
        x_, y_ = place(p_, (q - b + n) % n)
        return w_full.at[x_, :, y_, :, cols]

    def to_partner(p_, b):
        part = group(p_, b)
        send(part, part, a4_s.at[0], a4_r.at[0], partner)

    def to_second(b):
        part = group(p, b)
        for i in range(2):
            send(part, part, a3_s.at[0], a3_r.at[b, i], p_peers[i])
        to_partner(p, b)

    def ordered(j):
        return j + (j // 2) * (n + 1 - 2 * j)

    own_group = group(p, 0)
    loop(1, n, lambda j: send(
        own_group, own_group, a2_s.at[0], a2_r.at[ordered(j) - 1], q_peer(ordered(j))
    ))
    to_second(0)
    def pass_first(j):
        b = ordered(j)
        drain(own_group, a2_r.at[b - 1])
        to_second(b)


    def pass_second(j):
        b = ordered(j)
        for i in range(2):
            drain(own_group, a3_r.at[b, i])
            part = group(sides[i], b, quarters[i])
            send(part, part, a3_s.at[0], a3_r.at[b, 2 + i], p_peers[1 - i])
            send(part, part, a3_s.at[0], a4_r.at[0], crossed[1 - i])
        for i in range(2):
            to_partner(sides[i], b)

    pass_second(0)
    loop(1, n, pass_first)
    loop(1, n, pass_second)

    def pass_far(j):
        b = ordered(j)
        for i in range(2):
            drain(group(far, b, quarters[i]), a3_r.at[b, 2 + i])

    loop(0, n, pass_far)

    def project(rows, cols):
        act[rows, cols] = jnp.dot(
            normed[rows, :], w_full[:, :, :, :, cols].reshape(width, half),
            preferred_element_type=f32,
        )

    def activate(rows, cols):
        a = act[rows, cols]
        hidden_act[rows, cols] = (a * (0.5 * jnp.tanh(0.5 * a) + 0.5)).astype(bf16)

    project(slice(0, tile), mine)
    by_rows(0, tile, lambda rows: activate(rows, mine))

    drain(w_full.at[:, :, :, :, other], a4_r.at[0])

    def share_of(t, m):
        return rows_at(t * tile + m * share, share)

    def tile_rows(t, body):
        by_rows(0, tile, lambda rows: body(rows_at(t * tile + rows.start, 16)))

    def forward(t, whole=True):
        rows = rows_at(t * tile, tile)
        if whole:
            act[rows, :] = jnp.dot(
                normed[rows, :], w_full[...].reshape(width, width), preferred_element_type=f32
            )
        else:
            project(rows, other)
        tile_rows(t, lambda part: activate(part, slice(0, width) if whole else other))
        field = jnp.dot(hidden_act[rows, :], wo_t[...], preferred_element_type=f32)
        fields[rows, :] = field
        coarse[rows, :] = field.astype(bf16)

        def spread(k):
            peer = m_peer(k)
            send(
                coarse.at[share_of(t, peer[0]), :], theirs.at[t, member],
                b1_s.at[0], b1_r.at[t], peer,
            )

        loop(1, count, spread)
        theirs[t, member] = coarse[share_of(t, member), :]

    def answer(t):
        come = theirs.at[t, pl.ds(0, count - 1)]
        drain(come, b1_r.at[t])

        def compare(i):
            rows = rows_at(i * 16, 16)
            values = [theirs[t, m, rows, :].astype(f32) for m in range(count)]
            totals = [jnp.zeros_like(values[0]) for m in range(count)]
            for m in range(count):
                for o in range(m + 1, count):
                    s = slope(values[m] - values[o])
                    totals[m] = totals[m] + s
                    totals[o] = totals[o] - s
            for m in range(count):
                answers[t, m, rows, :] = totals[m].astype(bf16)

        loop(0, share // 16, compare)

        def reply(k):
            peer = m_peer(k)
            send(
                answers.at[t, peer[0]], pairs.at[share_of(t, member), :],
                b2_s.at[0], b2_r.at[t], peer,
            )

        loop(1, count, reply)
        pairs[share_of(t, member), :] = answers[t, member]


    def differentiate(rows):
        a = act[rows, :]
        s = 0.5 * jnp.tanh(0.5 * a) + 0.5
        act[rows, :] = s * (1.0 + a * (1.0 - s))

    forward(0, whole=False)
    loop(1, tiles - 1, forward)
    truth_pad[...] = jnp.zeros_like(truth_pad)
    truth_pad[0:levels, :] = truth[...]
    truth_t[...] = truth_pad[...].T
    latitude = math.pi * ((lat[...].astype(f32) + 0.5) / LATS - 0.5)
    area = LOSS_SCALE * jnp.cos(latitude)
    strip = lat.shape[1]
    for i in range(lat.shape[0]):
        area_t[i * strip:(i + 1) * strip, :] = jnp.broadcast_to(area[i:i + 1, :], (LANES, strip)).T
    if tiles > 1:
        forward(tiles - 1)

    def reply_and_prepare(t):
        answer(t)
        tile_rows(t, differentiate)
        left = turns - turns // 2
        loop(turns // 2 + t * left // tiles, turns // 2 + (t + 1) * left // tiles, turn)

    loop(0, tiles, reply_and_prepare)

    fair = (1.0 - (1.0 - ALPHA) / count) / (count * (count - 1))

    def backward(t):
        come = pairs.at[pl.ds(0, tile - share), :]
        drain(come, b2_r.at[t])
        rows = rows_at(t * tile, tile)
        grad_fields = area_t[rows, :] * (
            slope(fields[rows, :] - truth_t[rows, :]) * (1.0 / count)
            - fair * pairs[rows, :].astype(f32)
        )
        grad_act = jnp.dot(grad_fields.astype(bf16), wo_pad[...], preferred_element_type=f32)
        gp[rows, :] = (grad_act * act[rows, :]).astype(bf16)

    loop(0, tiles, backward)

    def product(which, pair, cols):
        rows = rows_at(pair * 2 * depth, 2 * depth)
        return jnp.dot(planes[which, rows, :], gp[:, cols], preferred_element_type=f32)

    def other_pair(pair):
        part = product(1, pair, other).astype(bf16)
        for u in range(2):
            i = 2 * pair + u
            csend[i] = part[u * depth:(u + 1) * depth, :]
            send(csend.at[i], crecv.at[i], c0_s.at[0], c0_r.at[i], partner)

    loop(0, n // 2, other_pair)

    halves = [slice(0, quarter), slice(quarter, half)]

    def to_side(slot, target):
        send(send1.at[slot], recv1.at[slot], c1_s.at[0], c1_r.at[slot], p_peers[target])

    def own_pair(pair):
        part = product(0, pair, mine)
        for u in range(2):
            i = 2 * pair + u
            drain(crecv.at[i], c0_r.at[i])
            sums[i] = part[u * depth:(u + 1) * depth, :] + crecv[i].astype(f32)

    def to_near(side):
        send1[2 + side] = sums[1 + side, :, halves[side]].astype(bf16)
        to_side(2 + side, side)

    own_pair(0)
    for side in range(2):
        send1[side] = sums[0, :, halves[side]].astype(bf16)
        to_side(side, side)
    to_near(0)
    own_pair(1)
    to_near(1)
    for side in range(2):
        drain(recv1.at[side], c1_r.at[side])
        term = sums[2 - side, :, halves[side]] + recv1[side].astype(f32)
        send1[4 + side] = term.astype(bf16)
        to_side(4 + side, 1 - side)

    def grad_normed(x_):
        cols = rows_at(x_ * depth, depth)
        act[:, cols] = lax.dot_general(
            gp[...], w_full[x_].reshape(depth, width), (((1,), (1,)), ((), ())),
            preferred_element_type=f32,
        )

    def hidden_grad(rows):
        scaled = act[rows, :] * gain[...]
        inverse = inv_root[rows, 0:1]
        unit = hid[rows, :].astype(f32) * inverse
        inner = jnp.mean(scaled * unit, axis=-1, keepdims=True)
        gh[rows, :] = ((scaled - unit * inner) * inverse).astype(bf16)

    loop(0, n // 2, grad_normed)
    for slot in range(2, 6):
        drain(recv1.at[slot], c1_r.at[slot])
    line_rows = nh * block

    def add_planes(q_):
        rows = rows_at(q_ * line_rows, line_rows)
        both = [
            sums[n - 1, rows, halves[i]] + recv1[2 + i, rows, :].astype(f32)
            + recv1[4 + i, rows, :].astype(f32)
            for i in range(2)
        ]
        return jnp.concatenate(both, axis=1)

    def to_first(j):
        k = ordered(n - j)
        send2[j - 1] = add_planes((q + k) % n).astype(bf16)
        send(send2.at[j - 1], recv2.at[j - 1], c2_s.at[0], c2_r.at[0], q_peer(k))

    loop(1, n, to_first)
    total = add_planes(q)
    loop(n // 2, n, grad_normed)
    drain(recv2, c2_r.at[0])
    for i in range(n - 1):
        total = total + recv2[i].astype(f32)
    strip = half // chips
    for h_ in range(nh):
        for l_ in range(chips):
            send3[h_, l_] = total[
                h_ * block:(h_ + 1) * block, l_ * strip:(l_ + 1) * strip
            ].astype(bf16)
    loop(1, nh * chips, lambda i: send(
        send3.at[(h + i // chips) % nh, (low + i % chips) % chips], recv3.at[i - 1],
        c3_s.at[0], c3_r.at[0], z_peer(i),
    ))
    by_rows(0, points // 2, hidden_grad)
    drain(recv3, c3_r.at[0])
    total = send3[h, low].astype(f32)
    for i in range(nh * chips - 1):
        total = total + recv3[i].astype(f32)
    factor = 1.0 / math.sqrt(count * points * nx * nh * ny)
    finals[core * chips + low] = (total * factor).astype(bf16)
    own_final = finals.at[core * chips + low]
    loop(1, count, lambda k: send(own_final, own_final, c4_s.at[0], c4_r.at[0], m_peer(k)))
    by_rows(points // 2, points, hidden_grad)
    others = finals.at[pl.ds(0, count - 1)]
    drain(others, c4_r.at[0])
    for i in range(count):
        gw_ref[:, i * strip:(i + 1) * strip] = finals[i].astype(f32)

    if chips == 1:
        drain(z_blocks, a1_s.at[0])
    else:
        from_end(lambda toward, start: [drain(z_blocks, a1_s.at[0]) for _ in range(2)])
    drain(w_full.at[pl.ds(0, n - 1), :, 0, :, mine], a2_s.at[0])
    drain(w_full.at[:, :, :, :, mine], a3_s.at[0])
    drain(w_full.at[:, :, pl.ds(0, 3), :, mine], a4_s.at[0])
    drain(coarse.at[pl.ds(0, points - points // count), :], b1_s.at[0])
    drain(coarse.at[pl.ds(0, points - points // count), :], b2_s.at[0])
    drain(csend, c0_s.at[0])
    drain(send1, c1_s.at[0])
    drain(send2, c2_s.at[0])
    drain(recv3, c3_s.at[0])
    drain(others, c4_s.at[0])


def hand_over(*arrays):
    pieces = 4

    def body(*refs):
        sources, targets, sems = refs[:len(arrays)], refs[len(arrays):-1], refs[-1]
        copies = []
        for source, target in zip(sources, targets):
            rows = source.shape[0]
            parts = pieces if rows % (16 * pieces) == 0 else 1
            for i in range(parts):
                part = pl.ds(i * (rows // parts), rows // parts)
                copies.append(
                    pltpu.make_async_copy(source.at[part], target.at[part], sems.at[len(copies)])
                )
        for copy in copies:
            copy.start()
        for copy in copies:
            copy.wait()

    anywhere = pl.BlockSpec(memory_space=pl.ANY)
    return pl.pallas_call(
        body,
        out_shape=tuple(jax.ShapeDtypeStruct(a.shape, a.dtype) for a in arrays),
        in_specs=[anywhere] * len(arrays),
        out_specs=(anywhere,) * len(arrays),
        scratch_shapes=[pltpu.SemaphoreType.DMA((pieces * len(arrays),))],
        compiler_params=pltpu.CompilerParams(vmem_limit_bytes=1024 * 1024),
        name="hand_over",
    )(*arrays)


def per_device(hidden, truth, lat_row, gain, w_in, w_out):
    nx, nh, ny = GRID
    count = lax.axis_size("member")
    _, points, width = hidden.shape
    levels = truth.shape[0]
    block = w_in.shape[0]
    half = width // 2
    tile = min(TILE, points)
    tiles, share = points // tile, tile // count
    f32, bf16 = jnp.float32, jnp.bfloat16
    vmem, dma = pltpu.VMEM, pltpu.SemaphoreType.DMA
    n, chips, lat_strip = nx, count // 2, min(LANES, points)
    scratch = [
        vmem((points, width), bf16),
        vmem((levels, points), f32),
        vmem((points // lat_strip, lat_strip), jnp.int32),
        vmem((1, width), f32),
        vmem((levels, width), bf16),
        vmem((nx, nh, ny, block, width), bf16),
        vmem((points, width), bf16),
        vmem((2, width, points), bf16),
        vmem((points, LANES), f32),
        vmem((LANES, width), bf16),
        vmem((width, LANES), bf16),
        vmem((points, width), bf16),
        vmem((LANES, points), f32),
        vmem((points, LANES), f32),
        vmem((points, LANES), f32),
        vmem((points, width), f32),
        vmem((points, LANES), f32),
        vmem((points, LANES), bf16),
        vmem((tiles, count, share, LANES), bf16),
        vmem((tiles, count, share, LANES), bf16),
        vmem((points, LANES), bf16),
        vmem((points, width), bf16),
        vmem((n, width // n, half), bf16),
        vmem((n, width // n, half), bf16),
        vmem((n, width // n, half), f32),
        vmem((6, width // n, half // 2), bf16),
        vmem((6, width // n, half // 2), bf16),
        vmem((n - 1, nh * block, half), bf16),
        vmem((n - 1, nh * block, half), bf16),
        vmem((nh, chips, block, half // chips), bf16),
        vmem((nh * chips - 1, block, half // chips), bf16),
        vmem((count, block, half // chips), bf16),
        dma((6,)),
    ]
    for arrivals in (
        (1,), (n - 1,), (n, 4), (1,),
        (tiles,), (tiles,),
        (n,), (6,), (1,), (1,), (1,),
    ):
        scratch += [dma((1,)), dma(arrivals)]
    grad_rows, grad_first = pl.pallas_call(
        functools.partial(kernel, tile),
        out_shape=(
            vmem((points, width), bf16),
            vmem((block, width), f32),
        ),
        in_specs=[pl.BlockSpec(memory_space=pltpu.HBM)] * 6,
        out_specs=(pl.BlockSpec(memory_space=vmem),) * 2,
        scratch_shapes=scratch,
        compiler_params=pltpu.CompilerParams(
            collective_id=0, has_side_effects=True, vmem_limit_bytes=57 * 1024 * 1024
        ),
        name="crps_step",
    )(
        hidden[0], truth, lat_row.reshape(points // lat_strip, lat_strip), gain[None], w_in, w_out
    )
    grad_rows, grad_first = hand_over(grad_rows, grad_first)
    return (grad_rows[None], grad_first)


def solution(mesh):
    in_specs = (
        P("member", "space", None),
        P(None, "space"),
        P("space"),
        P(),
        P("space", None),
        P(),
    )
    out_specs = (P("member", "space", None), P("space", None))
    return jax.shard_map(
        per_device, mesh=mesh, in_specs=in_specs, out_specs=out_specs, check_vma=False
    )
```
